32 devices in a mesh: row: 4 (over y, core), col: 8 (over z, x).
Axes of the slice: x: 2, y: 2, z: 4, core: 2. Of those that a mesh axis runs over, the one named last changes fastest.
Arguments:
- state: float32 [3, 512, 2048], P(None, 'row', 'col'), may hold values from -0.675 to 1.5, as said below
- row_count: int32 [4, 8], P('row', 'col'), may hold values from 0 to 64, as said below
- col_count: int32 [4, 8], P('row', 'col'), may hold values from 0 to 64, as said below
- patch_pos: int32 [4, 8, 2], P('row', 'col'), may hold values from 0 to 192, as said below
- patch_ext: int32 [4, 8, 2], P('row', 'col'), may hold values from 16 to 64, as said below
Outputs:
- richardson_error: float32 [256, 1024], P('row', 'col')
- moved_state: float32 [3, 512, 2048], P(None, 'row', 'col')
- refined_patch: float32 [3, 512, 1024], P(None, 'row', 'col')
The draws below stay inside these ranges and needn't reach their ends.
Inputs may be any that keep to these rules, and one draw needn't show every extreme that they name: `state`: depth lies in [0.5, 1.5]; the momenta are depth times a velocity of magnitude at most 0.45. `row_count`: some tile takes over exactly 64 rows and some none. `col_count`: some tile takes over exactly 64 columns and some none. `patch_pos`: component 0 is at most 64 and component 1 at most 192; both ends are reached. `patch_ext`: some tile is flagged over its whole patch.
All inputs are finite; a program needn't handle non-finite values.
Results may differ from the reference program's by a relative error of at most 0.0003.
Values sent between devices are 32-bit elements; how exact they have to be, the bound alone decides.
No kernel may reach another device: no remote copies, remote signals or barrier semaphores. Data moves between devices by JAX's collectives and lax.ppermute only.
A program may use at most 128 MiB of HBM per device.

```python
import jax
import jax.numpy as jnp
from jax import lax

TILE_R = 128
TILE_C = 256
SLAB = 64
PATCH = 64
GR = 4
GC = 8
NX = 512
NY = 2048


def draw_state(key, part):
    keys = jax.random.split(jax.random.fold_in(key, 7), 3)
    depth_draw = jax.random.uniform(keys[0], (NX, NY), jnp.float32)
    first_vel = jax.random.uniform(keys[1], (NX, NY), jnp.float32, -1.0, 1.0)
    second_vel = jax.random.uniform(keys[2], (NX, NY), jnp.float32, -1.0, 1.0)
    depth = 0.5 + depth_draw
    first_vel = 0.45 * first_vel
    second_vel = 0.45 * second_vel
    return jnp.stack([depth, depth * first_vel, depth * second_vel]).astype(jnp.float32)


def draw_counts(key, salt):
    counts = jax.random.randint(jax.random.fold_in(key, salt), (GR, GC), 0, SLAB + 1)
    return counts.at[0, 0].set(SLAB).at[GR - 1, GC - 1].set(0).astype(jnp.int32)


def draw_row_count(key, part):
    return draw_counts(key, 11)


def draw_col_count(key, part):
    return draw_counts(key, 12)


def draw_patch_pos(key, part):
    first_key, second_key = jax.random.split(jax.random.fold_in(key, 13))
    limit = jnp.array([TILE_R - PATCH, TILE_C - PATCH], jnp.int32)
    base = jax.random.randint(first_key, (GR, GC, 2), 0, limit + 1)
    pick = jax.random.randint(second_key, (GR, GC, 2), 0, 4)
    placed = jnp.where(pick == 0, 0, jnp.where(pick == 1, limit, base))
    return placed.at[0, 0].set(limit).at[GR - 1, GC - 1].set(0).astype(jnp.int32)


def draw_patch_ext(key, part):
    extent = jax.random.randint(jax.random.fold_in(key, 14), (GR, GC, 2), PATCH // 4, PATCH + 1)
    return extent.at[0, 0].set(PATCH).at[GR - 1, GC - 1].set(PATCH // 4).astype(jnp.int32)


def setup_inputs(seed: int = 0) -> dict:
    key_of = jax.random.split(jax.random.key(seed), 6)
    state = draw_state(jax.random.fold_in(key_of[5], 71), 0)
    row_count = draw_row_count(jax.random.fold_in(key_of[5], 71), 0)
    col_count = draw_col_count(jax.random.fold_in(key_of[5], 71), 0)
    patch_pos = draw_patch_pos(jax.random.fold_in(key_of[5], 71), 0)
    patch_ext = draw_patch_ext(jax.random.fold_in(key_of[5], 71), 0)
    return dict(state=state, row_count=row_count, col_count=col_count, patch_pos=patch_pos, patch_ext=patch_ext)


GRAV = 1.0
RATIO = 0.1
ERR_SCALE = 10.0

def face_flux(left_vals, right_vals, normal):
    tangent = 3 - normal

    def physical(fields):
        depth = fields[0]
        velocity = fields[normal] / depth
        flux = [None, None, None]
        flux[0] = fields[normal]
        flux[normal] = fields[normal] * velocity + 0.5 * GRAV * depth * depth
        flux[tangent] = fields[tangent] * velocity
        return (flux, jnp.abs(velocity) + jnp.sqrt(GRAV * depth))
    flux_left, speed_left = physical(left_vals)
    flux_right, speed_right = physical(right_vals)
    speed = jnp.maximum(speed_left, speed_right)
    return [0.5 * (flux_left[comp] + flux_right[comp]) - 0.5 * speed * (right_vals[comp] - left_vals[comp]) for comp in range(3)]

def rusanov_step(cells):
    fields = [cells[comp] for comp in range(3)]
    flux_row = face_flux([f[:-1, 1:-1] for f in fields], [f[1:, 1:-1] for f in fields], 1)
    flux_col = face_flux([f[1:-1, :-1] for f in fields], [f[1:-1, 1:] for f in fields], 2)
    result = [fields[comp][1:-1, 1:-1] - RATIO * (flux_row[comp][1:] - flux_row[comp][:-1]) - RATIO * (flux_col[comp][:, 1:] - flux_col[comp][:, :-1]) for comp in range(3)]
    return jnp.stack(result)

def coarsen(cells):
    shaped = cells.reshape(cells.shape[0], cells.shape[1] // 2, 2, cells.shape[2] // 2, 2)
    return 0.25 * (shaped[:, :, 0, :, 0] + shaped[:, :, 1, :, 0] + shaped[:, :, 0, :, 1] + shaped[:, :, 1, :, 1])

def richardson(fine_two, coarse_one):
    return ERR_SCALE * lax.optimization_barrier(jnp.sum(jnp.abs(coarsen(fine_two) - coarse_one), axis=0))

def minmod(lower_diff, upper_diff):
    chosen = jnp.where(jnp.abs(lower_diff) < jnp.abs(upper_diff), lower_diff, upper_diff)
    return jnp.where(lower_diff * upper_diff > 0, chosen, 0.0)

def muscl_step(cells):
    fields = [cells[comp] for comp in range(3)]
    inner_rows = cells.shape[1] - 4
    inner_cols = cells.shape[2] - 4
    row_band = [f[:, 2:-2] for f in fields]
    deltas = [b[1:] - b[:-1] for b in row_band]
    slopes = [minmod(d[:-1], d[1:]) for d in deltas]
    left_vals = [row_band[c][1:inner_rows + 2] + 0.5 * slopes[c][:inner_rows + 1] for c in range(3)]
    right_vals = [row_band[c][2:inner_rows + 3] - 0.5 * slopes[c][1:inner_rows + 2] for c in range(3)]
    flux_row = face_flux(left_vals, right_vals, 1)
    col_band = [f[2:-2, :] for f in fields]
    deltas = [b[:, 1:] - b[:, :-1] for b in col_band]
    slopes = [minmod(d[:, :-1], d[:, 1:]) for d in deltas]
    left_vals = [col_band[c][:, 1:inner_cols + 2] + 0.5 * slopes[c][:, :inner_cols + 1] for c in range(3)]
    right_vals = [col_band[c][:, 2:inner_cols + 3] - 0.5 * slopes[c][:, 1:inner_cols + 2] for c in range(3)]
    flux_col = face_flux(left_vals, right_vals, 2)
    result = [fields[comp][2:-2, 2:-2] - RATIO * (flux_row[comp][1:] - flux_row[comp][:-1]) - RATIO * (flux_col[comp][:, 1:] - flux_col[comp][:, :-1]) for comp in range(3)]
    return jnp.stack(result)

def place_top(own_cells, slab_in, count_in):
    buffer = jnp.concatenate([slab_in, jnp.zeros_like(slab_in)], axis=1)
    aligned = lax.dynamic_slice_in_dim(buffer, (SLAB - count_in).astype(jnp.int32), SLAB, 1)
    row_ids = lax.broadcasted_iota(jnp.int32, (1, SLAB, 1), 1)
    return jnp.where(row_ids < count_in, aligned, own_cells)

def place_rows(own_cells, slab_in, count_in):
    top_rows = place_top(own_cells[:, :SLAB, :], slab_in, count_in)
    return jnp.concatenate([top_rows, own_cells[:, SLAB:, :]], axis=1)

def place_cols(own_cells, slab_in, count_in):
    buffer = jnp.concatenate([slab_in, jnp.zeros_like(slab_in)], axis=2)
    aligned = lax.dynamic_slice_in_dim(buffer, (SLAB - count_in).astype(jnp.int32), SLAB, 2)
    col_ids = lax.broadcasted_iota(jnp.int32, (1, 1, SLAB), 2)
    left_part = jnp.where(col_ids < count_in, aligned, own_cells[:, :, :SLAB])
    return jnp.concatenate([left_part, own_cells[:, :, SLAB:]], axis=2)

def refine_patch(padded, row_start, col_start, extent):
    zero_index = jnp.zeros((), jnp.int32)
    region = lax.dynamic_slice(padded, (zero_index, row_start.astype(jnp.int32), col_start.astype(jnp.int32)), (3, PATCH + 4, PATCH + 4))
    refined_cells = jnp.broadcast_to(region[:, :, None, :, None], (3, PATCH + 4, 2, PATCH + 4, 2)).reshape(3, 2 * PATCH + 8, 2 * PATCH + 8)
    halfway = muscl_step(refined_cells)
    finished = muscl_step(halfway)
    row_ids = lax.broadcasted_iota(jnp.int32, (1, 2 * PATCH, 1), 1)
    col_ids = lax.broadcasted_iota(jnp.int32, (1, 1, 2 * PATCH), 2)
    inside = (row_ids < 2 * extent[0]) & (col_ids < 2 * extent[1])
    return jnp.where(inside, finished, 0.0)

def reference(state, row_count, col_count, patch_pos, patch_ext):
    wrapped = jnp.pad(state, ((0, 0), (2, 2), (2, 2)), mode='wrap')

    def error_rows(tile_index):
        row_block = lax.dynamic_slice_in_dim(wrapped, (tile_index * TILE_R).astype(jnp.int32), TILE_R + 4, 1)
        fine_two = rusanov_step(rusanov_step(row_block))
        coarse_one = rusanov_step(coarsen(row_block))
        return richardson(fine_two, coarse_one)
    error_field = lax.map(error_rows, jnp.arange(GR, dtype=jnp.int32)).reshape(NX // 2, NY // 2)
    tile_stack = state.reshape(3, GR, TILE_R, GC, TILE_C).transpose(1, 3, 0, 2, 4)
    upper_slab = jnp.roll(tile_stack, 1, axis=0)[:, :, :, TILE_R - SLAB:, :]
    row_moved = jax.vmap(jax.vmap(place_rows))(tile_stack, upper_slab, row_count)
    left_slab = jnp.roll(row_moved, 1, axis=1)[:, :, :, :, TILE_C - SLAB:]
    moved_tiles = jax.vmap(jax.vmap(place_cols))(row_moved, left_slab, col_count)
    moved_state = moved_tiles.transpose(2, 0, 3, 1, 4).reshape(3, NX, NY)
    wrapped_moved = jnp.pad(moved_state, ((0, 0), (2, 2), (2, 2)), mode='wrap')
    flat_pos = patch_pos.reshape(GR * GC, 2)
    flat_ext = patch_ext.reshape(GR * GC, 2)

    def one_patch(inputs):
        tile_index, patch_start, extent = inputs
        row_start = tile_index // GC * TILE_R + patch_start[0]
        col_start = tile_index % GC * TILE_C + patch_start[1]
        return refine_patch(wrapped_moved, row_start, col_start, extent)
    patches = lax.map(one_patch, (jnp.arange(GR * GC, dtype=jnp.int32), flat_pos, flat_ext))
    refined = patches.reshape(GR, GC, 3, 2 * PATCH, 2 * PATCH).transpose(2, 0, 3, 1, 4).reshape(3, GR * 2 * PATCH, GC * 2 * PATCH)
    return (error_field, moved_state, refined)
```

```python
import jax
import jax.numpy as jnp
from jax import lax
from jax.experimental import pallas as pl
from jax.experimental.pallas import tpu as pltpu
from jax.sharding import PartitionSpec as P

SLAB = 64
PATCH = 64
LANES = 128

RATIO = 0.1
ERR_SCALE = 10.0

RIGHT_ROWS, RIGHT_COLS, LEFT_ROWS, LEFT_COLS, OWN_ROWS, OWN_COLS = 6, 7, 8, 9, 10, 11

VMEM = pl.BlockSpec(memory_space=pltpu.VMEM)
SMEM = pl.BlockSpec(memory_space=pltpu.SMEM)
PARAMS = pltpu.CompilerParams(vmem_limit_bytes=32 * 1024 * 1024)


def f32(*shape):
    return jax.ShapeDtypeStruct(shape, jnp.float32)


def lane_ids(rows, width=LANES):
    return lax.broadcasted_iota(jnp.int32, (rows, width), 1)


def row_ids(rows, width=LANES):
    return lax.broadcasted_iota(jnp.int32, (rows, width), 0)


def roll(value, by, axis):
    return pltpu.roll(value, by % value.shape[axis], axis)


def cell_terms(depth, first, second):
    inverse_root = lax.rsqrt(depth)
    wave = depth * inverse_root
    inverse = inverse_root * inverse_root
    first_vel = first * inverse
    second_vel = second * inverse
    pressure = 0.5 * depth * depth
    cross = first * second_vel
    row_terms = (first, first * first_vel + pressure, cross, jnp.abs(first_vel) + wave)
    col_terms = (second, cross, second * second_vel + pressure, jnp.abs(second_vel) + wave)
    return row_terms, col_terms


def doubled_flux(left, right, left_terms, right_terms):
    speed = jnp.maximum(left_terms[3], right_terms[3])
    return [(left_terms[c] + right_terms[c]) - speed * (right[c] - left[c]) for c in range(3)]


def spread_step(fields, row_by, col_by):
    row_terms, col_terms = cell_terms(*fields)
    total = None
    for terms, by, axis in ((row_terms, row_by, 0), (col_terms, col_by, 1)):
        lower = [roll(f, by, axis) for f in fields]
        momentum = lower[1 + axis]
        lower_terms = [momentum if c == 0 else roll(terms[c], by, axis) for c in range(4)]
        flux = doubled_flux(lower, fields, lower_terms, terms)
        change = [roll(f, -by, axis) - f for f in flux]
        total = change if total is None else [t + c for t, c in zip(total, change)]
    return [f - (0.5 * RATIO) * t for f, t in zip(fields, total)]


def block_sum(field):
    pair = field + roll(field, -1, 0)
    return pair + roll(pair, -1, 1)


def error_rows(fields, halved):
    fine_two = spread_step(spread_step(fields, 1, 1), 1, 1)
    coarse_one = spread_step([0.25 * block_sum(f) for f in fields], 2, 2)
    total = None
    for fine, coarse in zip(fine_two, coarse_one):
        part = jnp.abs(0.25 * block_sum(fine) - coarse)
        total = part if total is None else total + part
    total = ERR_SCALE * total
    halved[0] = total[4:20, 0:LANES]
    halved[1] = total[4:20, LANES : 2 * LANES]
    lanes = lane_ids(8)
    even = (2 * lanes) % LANES
    low = jnp.take_along_axis(halved[0, pl.ds(0, 8, stride=2), :], even, axis=1)
    high = jnp.take_along_axis(halved[1, pl.ds(0, 8, stride=2), :], even, axis=1)
    return jnp.where(lanes < LANES // 2, low, high)


def pack_cols(row_count, col_count, last_ref, first_ref, left_ref, right_ref):
    rows = last_ref.shape[1]
    half = rows // 2
    rc = row_count[0, 0].astype(jnp.float32)
    cc = col_count[0, 0].astype(jnp.float32)
    lanes = lane_ids(half)
    for comp in range(3):
        upper = last_ref[comp, 0:half, :]
        lower = roll(last_ref[comp, half:rows, :], LANES // 2, 1)
        left_ref[comp, 0:half, :] = jnp.where(lanes >= LANES // 2, upper, lower)
        left_ref[comp, half : half + 8, :] = jnp.where(lane_ids(8) == LEFT_ROWS, rc, cc)
    lanes = lane_ids(rows)
    packed = jnp.where(lanes == RIGHT_ROWS, rc, cc)
    for comp in (2, 1, 0):
        packed = jnp.where(lanes < 2 * comp + 2, roll(first_ref[comp], 2 * comp, 1), packed)
    right_ref[...] = packed.T[0:8]


def pack_rows(row_count, col_count, left_ref, right_ref, state_ref, rim_ref, down_ref, up_ref):
    rows, cols = state_ref.shape[1], state_ref.shape[2]
    half = rows // 2
    rc = row_count[0, 0].astype(jnp.float32)
    cc = col_count[0, 0].astype(jnp.float32)
    right = jnp.concatenate([right_ref[...], jnp.zeros((LANES - 8, LANES), jnp.float32)], axis=0).T
    lanes = lane_ids(rows)
    from_left = (lanes == LEFT_ROWS) | (lanes == LEFT_COLS)
    counts = jnp.where(from_left, left_ref[0, half : half + 1, :], jnp.where(lanes == OWN_ROWS, rc, cc))
    for comp in range(3):
        packed = left_ref[comp, 0:half, :]
        left = jnp.concatenate([packed, roll(packed, LANES // 2, 1)], axis=0)
        inner = right if comp == 0 else roll(right, -2 * comp, 1)
        inner = jnp.where(lanes < LEFT_ROWS, inner, counts)
        rim = jnp.where(lanes >= LANES // 2, left, inner)
        rim_ref[comp] = rim
        down_ref[comp, :, 0:cols] = state_ref[comp, rows - SLAB : rows, :]
        down_ref[comp, :, cols : cols + LANES] = rim[rows - SLAB : rows]
        up_ref[comp, :, 0:cols] = state_ref[comp, 0:8, :]
        up_ref[comp, :, cols : cols + LANES] = rim[0:8]


def inner_error(state_ref, rim_ref, error_ref, halved):
    blocks = state_ref.shape[1] // 16

    def one(block, carry):
        start = pl.multiple_of(16 * block - 8, 8)
        fields = [
            jnp.concatenate(
                [state_ref[c, pl.ds(start, 32), :][4:28], rim_ref[c, pl.ds(start, 32), :][4:28]], axis=1
            )
            for c in range(3)
        ]
        error_ref[pl.ds(pl.multiple_of(8 * block, 8), 8), :] = error_rows(fields, halved)
        return carry

    lax.fori_loop(1, blocks - 1, one, 0)


def minmod(lower_diff, upper_diff):
    return jnp.maximum(jnp.minimum(lower_diff, upper_diff), 0.0) + jnp.minimum(
        jnp.maximum(lower_diff, upper_diff), 0.0
    )


def paired_change(near, far, axis):
    down = lambda v: roll(v, 1, axis)
    up = lambda v: roll(v, -1, axis)
    inner = [f - n for n, f in zip(near, far)]
    outer = [n - down(f) for n, f in zip(near, far)]
    near_half = [0.5 * minmod(o, i) for o, i in zip(outer, inner)]
    far_half = [0.5 * minmod(i, up(o)) for o, i in zip(outer, inner)]
    near_hi = [n + s for n, s in zip(near, near_half)]
    near_lo = [n - s for n, s in zip(near, near_half)]
    far_hi = [down(f + s) for f, s in zip(far, far_half)]
    far_lo = [f - s for f, s in zip(far, far_half)]
    terms = lambda cells: cell_terms(*cells)[axis]
    inner_flux = doubled_flux(near_hi, far_lo, terms(near_hi), terms(far_lo))
    outer_flux = doubled_flux(far_hi, near_lo, terms(far_hi), terms(near_lo))
    near_change = [i - o for i, o in zip(inner_flux, outer_flux)]
    far_change = [up(o) - i for i, o in zip(inner_flux, outer_flux)]
    return near_change, far_change


def doubled_first_step(cells):
    all_terms = cell_terms(*cells)
    changes = []
    for axis in (0, 1):
        terms = all_terms[axis]
        lower = [roll(f, 1, axis) for f in cells]
        lower_terms = [lower[1 + axis] if c == 0 else roll(terms[c], 1, axis) for c in range(4)]
        flux = doubled_flux(lower, cells, lower_terms, terms)
        own = [2.0 * terms[c] for c in range(3)]
        changes.append(
            (
                [o - f for o, f in zip(own, flux)],
                [roll(f, -1, axis) - o for o, f in zip(own, flux)],
            )
        )
    rows, cols = changes
    return [
        [
            [cells[c] - (0.5 * RATIO) * (rows[a][c] + cols[b][c]) for c in range(3)]
            for b in range(2)
        ]
        for a in range(2)
    ]


def patch_rows(cells):
    half = doubled_first_step(cells)
    by_row = [paired_change(half[0][b], half[1][b], 0) for b in range(2)]
    by_col = [paired_change(half[a][0], half[a][1], 1) for a in range(2)]
    lanes = lane_ids(16)
    result = []
    for a in range(2):
        fine = [
            [half[a][b][c] - (0.5 * RATIO) * (by_row[b][a][c] + by_col[a][b][c]) for c in range(3)]
            for b in range(2)
        ]
        parts = []
        for c in range(3):
            pick = lanes // 2 + 2
            even = jnp.take_along_axis(fine[0][c][4:20], pick, axis=1)
            odd = jnp.take_along_axis(fine[1][c][4:20], pick, axis=1)
            parts.append(jnp.where(lanes % 2 == 0, even, odd))
        result.append(parts)
    return result


def finish(
    row_count, col_count, patch_pos, patch_ext, state_ref, rim_ref, above_ref, below_ref, inner_ref,
    error_ref, moved_ref, patch_ref, edge, wide, window, halved,
):
    rows, cols = state_ref.shape[1], state_ref.shape[2]
    slab = slice(rows - SLAB, rows)
    top = slice(0, SLAB)
    right = slice(cols, cols + LANES)
    last = slice(cols - LANES, cols)

    rim_counts = rim_ref[0, 0:8, :]
    above_counts = above_ref[0, 0:8, right]
    below_counts = below_ref[0, 0:8, right]
    get = lambda counts, lane: counts[0, lane].astype(jnp.int32)
    rc, cc = row_count[0, 0], col_count[0, 0]
    rc_left, rc_right, cc_right = [get(rim_counts, k) for k in (LEFT_ROWS, RIGHT_ROWS, RIGHT_COLS)]
    cc_above, cc_above_right = [get(above_counts, k) for k in (OWN_COLS, RIGHT_COLS)]
    rc_below, cc_below, rc_below_left, rc_below_right, cc_below_right = [
        get(below_counts, k) for k in (OWN_ROWS, OWN_COLS, LEFT_ROWS, RIGHT_ROWS, RIGHT_COLS)
    ]

    for comp in range(3):
        edge[0, comp, 0:8, :] = above_ref[comp, SLAB - 8 : SLAB, :]
        edge[0, comp, 8:32, 0:cols] = state_ref[comp, 0:24, :]
        edge[0, comp, 8:32, right] = rim_ref[comp, 0:24, :]
        edge[1, comp, 0:24, 0:cols] = state_ref[comp, rows - 24 : rows, :]
        edge[1, comp, 0:24, right] = rim_ref[comp, rows - 24 : rows, :]
        edge[1, comp, 24:32, :] = below_ref[comp, :, :]

    half_rows = error_ref.shape[0]
    error_ref[8 : half_rows - 8, :] = inner_ref[8 : half_rows - 8, :]

    def edge_error(side, carry):
        fields = [edge[side, c][4:28] for c in range(3)]
        start = pl.multiple_of(side * (half_rows - 8), 8)
        error_ref[pl.ds(start, 8), :] = error_rows(fields, halved)
        return carry

    lax.fori_loop(0, 2, edge_error, 0)

    def moved_rows(own, own_rim, slab_rows, slab_rim, counts):
        here, left, right_count = counts
        size = own.shape[0]
        aligned = roll_by(slab_rows, here)[0:size]
        lanes, ids = lane_ids(size), row_ids(size)
        body = jnp.where(row_ids(size, cols) < here, aligned, own)
        on_left = lanes >= LANES // 2
        side = jnp.where(on_left, roll_by(slab_rim, left)[0:size], roll_by(slab_rim, right_count)[0:size])
        taken = ids < jnp.where(on_left, left, right_count)
        return body, jnp.where(taken, side, own_rim)

    def roll_by(value, by):
        return pltpu.roll(value, by & (SLAB - 1), 0)

    def moved_cols(body, rim, here, right_count):
        lanes = lane_ids(rim.shape[0])
        first = jnp.where(lanes < here, pltpu.roll(rim, here, 1), body[:, 0:LANES])
        outer = jnp.where(lanes < right_count, pltpu.roll(body[:, cols - LANES : cols], right_count, 1), rim)
        return first, body[:, LANES:cols], jnp.where(lanes >= LANES // 2, rim, outer)

    for comp in range(3):
        own, own_rim = state_ref[comp, :, :], rim_ref[comp, :, :]
        body, side = moved_rows(
            own[top], own_rim[top], above_ref[comp, :, 0:cols], above_ref[comp, :, right], (rc, rc_left, rc_right)
        )
        for part, body, side in (
            (top, body, side),
            (slice(SLAB, rows), own[SLAB:rows], own_rim[SLAB:rows]),
        ):
            first, second, outer = moved_cols(body, side, cc, cc_right)
            moved_ref[comp, part, 0:LANES] = first
            moved_ref[comp, part, LANES:cols] = second
            at = slice(part.start + 8, part.stop + 8)
            wide[comp, at, 0:LANES] = first
            wide[comp, at, LANES:cols] = second
            wide[comp, at, right] = outer
        first, second, outer = moved_cols(
            above_ref[comp, SLAB - 8 : SLAB, 0:cols], above_ref[comp, SLAB - 8 : SLAB, right], cc_above, cc_above_right
        )
        wide[comp, 0:8, 0:LANES] = first
        wide[comp, 0:8, LANES:cols] = second
        wide[comp, 0:8, right] = outer
        body, side = moved_rows(
            below_ref[comp, :, 0:cols], below_ref[comp, :, right], own[slab], own_rim[slab],
            (rc_below, rc_below_left, rc_below_right),
        )
        first, second, outer = moved_cols(body, side, cc_below, cc_below_right)
        wide[comp, rows + 8 : rows + 16, 0:LANES] = first
        wide[comp, rows + 8 : rows + 16, LANES:cols] = second
        wide[comp, rows + 8 : rows + 16, right] = outer

    row_start = patch_pos[0, 0, 0] + 4
    base = pl.multiple_of(row_start // 8 * 8, 8)
    width = cols + LANES
    for comp in range(3):
        near = wide[comp, pl.ds(base, 80), :]
        near = pltpu.roll(near, (80 - (row_start - base)) % 80, 0)
        near = pltpu.roll(near, (width + 2 - patch_pos[0, 0, 1]) % width, 1)
        window[comp, :, :] = near[0:72, 0:LANES]

    fine_rows, fine_cols = 2 * patch_ext[0, 0, 0], 2 * patch_ext[0, 0, 1]

    def patch_block(block, carry):
        start = pl.multiple_of(16 * block, 8)
        cells = [window[c, pl.ds(start, 24), :] for c in range(3)]
        fine = patch_rows(cells)
        lanes, ids = lane_ids(16), row_ids(16)
        for a in range(2):
            inside = (2 * (ids + start) + a < fine_rows) & (lanes < fine_cols)
            for c in range(3):
                patch_ref[c, pl.ds(2 * start + a, 16, stride=2), :] = jnp.where(inside, fine[a][c], 0.0)
        return carry

    lax.fori_loop(0, PATCH // 16, patch_block, 0)


def around(axis, by):
    devices = lax.axis_size(axis)
    return [(i, (i + by) % devices) for i in range(devices)]


def per_device(state, row_count, col_count, patch_pos, patch_ext):
    rows, cols = state.shape[1], state.shape[2]
    width = cols + LANES
    first_tile = pl.BlockSpec((3, rows, LANES), lambda i: (0, 0, 0))
    last_tile = pl.BlockSpec((3, rows, LANES), lambda i: (0, 0, cols // LANES - 1))
    to_right, to_left = pl.pallas_call(
        pack_cols,
        grid=(1,),
        out_shape=(f32(3, rows // 2 + 8, LANES), f32(8, LANES)),
        in_specs=[SMEM, SMEM, last_tile, first_tile],
        out_specs=(VMEM, VMEM),
        name="pack_cols",
    )(row_count, col_count, state, state)
    from_left = lax.ppermute(to_right, "col", around("col", 1))
    from_right = lax.ppermute(to_left, "col", around("col", -1))
    rim, to_below, to_above = pl.pallas_call(
        pack_rows,
        out_shape=(f32(3, rows, LANES), f32(3, SLAB, width), f32(3, 8, width)),
        in_specs=[SMEM, SMEM, VMEM, VMEM, VMEM],
        out_specs=(VMEM, VMEM, VMEM),
        name="pack_rows",
    )(row_count, col_count, from_left, from_right, state)
    from_above = lax.ppermute(to_below, "row", around("row", 1))
    from_below = lax.ppermute(to_above, "row", around("row", -1))
    inner = pl.pallas_call(
        inner_error,
        out_shape=f32(rows // 2, cols // 2),
        in_specs=[VMEM, VMEM],
        out_specs=VMEM,
        scratch_shapes=[pltpu.VMEM((2, 16, LANES), jnp.float32)],
        cost_estimate=pl.CostEstimate(flops=30_000_000, bytes_accessed=600_000, transcendentals=0),
        name="inner_error",
    )(state, rim)
    return pl.pallas_call(
        finish,
        out_shape=(f32(rows // 2, cols // 2), f32(3, rows, cols), f32(3, 2 * PATCH, 2 * PATCH)),
        in_specs=[SMEM] * 4 + [VMEM] * 5,
        out_specs=(VMEM, VMEM, VMEM),
        scratch_shapes=[
            pltpu.VMEM((2, 3, 32, width), jnp.float32),
            pltpu.VMEM((3, rows + 16, width), jnp.float32),
            pltpu.VMEM((3, 72, LANES), jnp.float32),
            pltpu.VMEM((2, 16, LANES), jnp.float32),
        ],
        compiler_params=PARAMS,
        name="finish",
    )(row_count, col_count, patch_pos, patch_ext, state, rim, from_above, from_below, inner)


def solution(mesh):
    placed = (
        P(None, "row", "col"),
        P("row", "col"),
        P("row", "col"),
        P("row", "col", None),
        P("row", "col", None),
    )
    return jax.shard_map(
        per_device,
        mesh=mesh,
        in_specs=placed,
        out_specs=(P("row", "col"), P(None, "row", "col"), P(None, "row", "col")),
        check_vma=False,
    )
```

```python
import jax
import jax.numpy as jnp
from jax import lax
from jax.experimental import pallas as pl
from jax.experimental.pallas import tpu as pltpu
from jax.sharding import PartitionSpec as P

SLAB = 64
PATCH = 64
LANES = 128

RATIO = 0.1
ERR_SCALE = 10.0

RIGHT_ROWS, RIGHT_COLS, LEFT_ROWS, LEFT_COLS, OWN_ROWS, OWN_COLS = 6, 7, 8, 9, 10, 11

VMEM = pl.BlockSpec(memory_space=pltpu.VMEM)
PARAMS = pltpu.CompilerParams(vmem_limit_bytes=32 * 1024 * 1024)


def f32(*shape):
    return jax.ShapeDtypeStruct(shape, jnp.float32)


def lane_ids(rows, width=LANES):
    return lax.broadcasted_iota(jnp.int32, (rows, width), 1)


def row_ids(rows, width=LANES):
    return lax.broadcasted_iota(jnp.int32, (rows, width), 0)


def roll(value, by, axis):
    return pltpu.roll(value, by % value.shape[axis], axis)


def cell_terms(depth, first, second):
    inverse_root = lax.rsqrt(depth)
    wave = depth * inverse_root
    inverse = inverse_root * inverse_root
    first_vel = first * inverse
    second_vel = second * inverse
    pressure = 0.5 * depth * depth
    cross = first * second_vel
    row_terms = (first, first * first_vel + pressure, cross, jnp.abs(first_vel) + wave)
    col_terms = (second, cross, second * second_vel + pressure, jnp.abs(second_vel) + wave)
    return row_terms, col_terms


def doubled_flux(left, right, left_terms, right_terms):
    speed = jnp.maximum(left_terms[3], right_terms[3])
    return [(left_terms[c] + right_terms[c]) - speed * (right[c] - left[c]) for c in range(3)]


def spread_step(fields, row_by, col_by):
    row_terms, col_terms = cell_terms(*fields)
    total = None
    for terms, by, axis in ((row_terms, row_by, 0), (col_terms, col_by, 1)):
        lower = [roll(f, by, axis) for f in fields]
        momentum = lower[1 + axis]
        lower_terms = [momentum if c == 0 else roll(terms[c], by, axis) for c in range(4)]
        flux = doubled_flux(lower, fields, lower_terms, terms)
        change = [roll(f, -by, axis) - f for f in flux]
        total = change if total is None else [t + c for t, c in zip(total, change)]
    return [f - (0.5 * RATIO) * t for f, t in zip(fields, total)]


def pair_change(near, far, near_terms, far_terms, axis):
    inner = doubled_flux(near, far, near_terms, far_terms)
    before = [roll(f, 1, axis) for f in far]
    before_terms = [before[1 + axis] if c == 0 else roll(far_terms[c], 1, axis) for c in range(4)]
    outer = doubled_flux(before, near, before_terms, near_terms)
    near_change = [i - o for i, o in zip(inner, outer)]
    far_change = [roll(o, -1, axis) - i for i, o in zip(inner, outer)]
    return near_change, far_change


def paired_step(phases):
    terms = [[cell_terms(*phases[x][y]) for y in range(2)] for x in range(2)]
    along_first = [
        pair_change(phases[0][y], phases[1][y], terms[0][y][0], terms[1][y][0], 0) for y in range(2)
    ]
    along_second = [
        pair_change(phases[x][0], phases[x][1], terms[x][0][1], terms[x][1][1], 1) for x in range(2)
    ]
    return [
        [
            [
                phases[x][y][c] - (0.5 * RATIO) * (along_first[y][x][c] + along_second[x][y][c])
                for c in range(3)
            ]
            for y in range(2)
        ]
        for x in range(2)
    ]


def block_mean(phases):
    return [
        0.25 * ((phases[0][0][c] + phases[1][0][c]) + (phases[0][1][c] + phases[1][1][c])) for c in range(3)
    ]


def coarse_error(phases):
    fine = block_mean(paired_step(paired_step(phases)))
    coarse = spread_step(block_mean(phases), 1, 1)
    parts = [jnp.abs(f - c) for f, c in zip(fine, coarse)]
    return ERR_SCALE * ((parts[0] + parts[1]) + parts[2])


def every_other(first, second, parity):
    lanes = lane_ids(first.shape[0])
    pick = (2 * lanes + parity) % LANES
    low = jnp.take_along_axis(first, pick, axis=1)
    high = jnp.take_along_axis(second, pick, axis=1)
    return jnp.where(lanes < LANES // 2, low, high)


def pack_cols(numbers_ref, state_ref, left_ref, right_ref, strip_ref):
    rows, cols = state_ref.shape[1], state_ref.shape[2]
    half = rows // 2
    numbers = numbers_ref[...].astype(jnp.float32)
    rc, cc = numbers[:, 0:1], numbers[:, 1:2]
    lanes = lane_ids(half)
    for comp in range(3):
        upper = state_ref[comp, 0:half, cols - LANES : cols]
        lower = roll(state_ref[comp, half:rows, cols - LANES : cols], LANES // 2, 1)
        left_ref[comp * half : (comp + 1) * half, :] = jnp.where(lanes >= LANES // 2, upper, lower)
    lanes = lane_ids(rows)
    packed = None
    for comp in range(3):
        ends = jnp.where(lanes < LANES // 2, state_ref[comp, :, 0:LANES], state_ref[comp, :, cols - LANES : cols])
        ends = roll(ends, 8 * comp + 4, 1)
        packed = ends if packed is None else jnp.where(lanes >= 8 * comp, ends, packed)
    strip_ref[0:24, :] = packed.T[0:24]
    ids = row_ids(8)
    spread = jnp.broadcast_to(numbers[:, 5:6], (8, LANES))
    for k in range(5):
        spread = jnp.where(ids == k, numbers[:, k : k + 1], spread)
    strip_ref[24:32, :] = spread
    counts = jnp.where(ids == 6, rc, cc)
    for ref, base, at in ((left_ref, 3 * half, 2), (right_ref, 0, 4)):
        ref[base : base + 8, :] = counts
        for comp in range(3):
            ref[base + 2 * comp : base + 2 * comp + 2, :] = strip_ref[8 * comp + at : 8 * comp + at + 2, :]


def pack_rows(strip_ref, left_ref, right_ref, state_ref, rim_ref, down_ref, up_ref):
    rows, cols = state_ref.shape[1], state_ref.shape[2]
    half = rows // 2
    rc, cc = strip_ref[24:25, :], strip_ref[25:26, :]
    right = jnp.concatenate([right_ref[...], jnp.zeros((LANES - 8, LANES), jnp.float32)], axis=0).T
    lanes = lane_ids(rows)
    left_rc = left_ref[3 * half + 6 : 3 * half + 7, :]
    left_cc = left_ref[3 * half + 7 : 3 * half + 8, :]
    counts = jnp.where(lanes == OWN_ROWS, rc, cc)
    counts = jnp.where(lanes == LEFT_COLS, left_cc, counts)
    counts = jnp.where(lanes == LEFT_ROWS, left_rc, counts)
    for comp in range(3):
        packed = left_ref[comp * half : (comp + 1) * half, :]
        left = jnp.concatenate([packed, roll(packed, LANES // 2, 1)], axis=0)
        inner = right if comp == 0 else roll(right, -2 * comp, 1)
        inner = jnp.where(lanes < LEFT_ROWS, inner, counts)
        rim = jnp.where(lanes >= LANES // 2, left, inner)
        rim_ref[comp] = rim
        down_ref[comp, :, 0:cols] = state_ref[comp, rows - SLAB : rows, :]
        down_ref[comp, :, cols : cols + LANES] = rim[rows - SLAB : rows]
        up_ref[comp, :, 0:cols] = state_ref[comp, 0:8, :]
        up_ref[comp, :, cols : cols + LANES] = rim[0:8]


def inner_error(state_ref, error_ref, columns):
    rows = state_ref.shape[1]
    half = rows // 2
    for comp in range(3):
        first, second = state_ref[comp, :, 0:LANES], state_ref[comp, :, LANES : 2 * LANES]
        for parity in range(2):
            columns[comp, parity] = every_other(first, second, parity)
    size = 24
    for start in range(0, half - 2, size - 4):
        start = min(start, half - size)
        phases = [
            [
                [columns[c, y, pl.ds(2 * start + x, size, stride=2), :] for c in range(3)]
                for y in range(2)
            ]
            for x in range(2)
        ]
        error = coarse_error(phases)
        low = 0 if start == 0 else 2
        error_ref[start + low : start + size, :] = error[low:size]


def edge_phases(state_ref, above_ref, below_ref, left_ref, right_ref, strip_ref, near_rows, columns, strips):
    rows, cols = state_ref.shape[1], state_ref.shape[2]
    right = slice(cols, cols + LANES)
    left_base = left_ref.shape[0] - 8
    lanes = lane_ids(8)
    packed_up, packed_down = None, None
    for comp in range(3):
        near_rows[comp, 0:2, :] = above_ref[comp, SLAB - 2 : SLAB, 0:cols]
        near_rows[comp, 2:6, :] = state_ref[comp, 0:4, :]
        near_rows[comp, 6:10, :] = state_ref[comp, rows - 4 : rows, :]
        near_rows[comp, 10:12, :] = below_ref[comp, 0:2, 0:cols]
        near_rows[comp, 12:16, :] = state_ref[comp, 0:4, :]
        first, second = near_rows[comp, :, 0:LANES], near_rows[comp, :, LANES : 2 * LANES]
        for parity in range(2):
            columns[comp, parity] = every_other(first, second, parity)

        def around_corner(ref, part):
            rim = ref[comp, part, right]
            start = jnp.where(lanes < LANES // 2, ref[comp, part, 0:LANES], rim)
            end = jnp.where(lanes < LANES // 2, rim, ref[comp, part, cols - LANES : cols])
            return jnp.where(
                (lanes >= 12 * comp) & (lanes < 12 * comp + 6), roll(start, 12 * comp + 2, 1), roll(end, 12 * comp + 10, 1)
            )

        up, down = around_corner(above_ref, slice(SLAB - 8, SLAB)), around_corner(below_ref, slice(0, 8))
        packed_up = up if comp == 0 else jnp.where(lanes >= 12 * comp, up, packed_up)
        packed_down = down if comp == 0 else jnp.where(lanes >= 12 * comp, down, packed_down)
    corners = jnp.concatenate([packed_down, jnp.ones((LANES - 16, LANES), jnp.float32), packed_up], axis=0).T
    for comp in range(3):
        strips[comp, 0, 0:2, :] = left_ref[left_base + 2 * comp : left_base + 2 * comp + 2, :]
        strips[comp, 0, 2:6, :] = strip_ref[8 * comp + 4 : 8 * comp + 8, :]
        strips[comp, 0, 6:10, :] = strip_ref[8 * comp : 8 * comp + 4, :]
        strips[comp, 0, 10:12, :] = right_ref[2 * comp : 2 * comp + 2, :]
        strips[comp, 0, 12:16, :] = strip_ref[8 * comp + 4 : 8 * comp + 8, :]
        strips[comp, 1, 0:12, :] = corners[12 * comp : 12 * comp + 12, :]
        strips[comp, 1, 12:16, :] = strip_ref[8 * comp + 4 : 8 * comp + 8, :]
    phases = []
    for x in range(2):
        phases.append([])
        for y in range(2):
            cells = []
            for comp, turned in ((0, 0), (1, 2), (2, 1)):
                by_row = columns[comp, y, pl.ds(x, 8, stride=2), :]
                own, outer = [strips[turned, k, pl.ds(x, 8, stride=2), :] for k in range(2)]
                cells.append(jnp.concatenate([by_row, every_other(own, outer, y)], axis=0))
            phases[-1].append(cells)
    return phases


def put_edges(error, edges):
    half_rows = error.shape[0]
    turned = jnp.concatenate([edges, jnp.zeros((LANES - 16, LANES), jnp.float32)], axis=0).T[0:half_rows]
    lanes, ids = lane_ids(half_rows), row_ids(half_rows)
    error = jnp.where(ids == 0, edges[1:2], jnp.where(ids == half_rows - 1, edges[4:5], error))
    return jnp.where(
        lanes == 0, roll(turned, -9, 1), jnp.where(lanes == LANES - 1, roll(turned, LANES - 13, 1), error)
    )


def minmod(lower_diff, upper_diff):
    return jnp.maximum(jnp.minimum(lower_diff, upper_diff), 0.0) + jnp.minimum(
        jnp.maximum(lower_diff, upper_diff), 0.0
    )


def paired_change(near, far, axis):
    down = lambda v: roll(v, 1, axis)
    up = lambda v: roll(v, -1, axis)
    inner = [f - n for n, f in zip(near, far)]
    outer = [n - down(f) for n, f in zip(near, far)]
    near_half = [0.5 * minmod(o, i) for o, i in zip(outer, inner)]
    far_half = [0.5 * minmod(i, up(o)) for o, i in zip(outer, inner)]
    near_hi = [n + s for n, s in zip(near, near_half)]
    near_lo = [n - s for n, s in zip(near, near_half)]
    far_hi = [down(f + s) for f, s in zip(far, far_half)]
    far_lo = [f - s for f, s in zip(far, far_half)]
    terms = lambda cells: cell_terms(*cells)[axis]
    inner_flux = doubled_flux(near_hi, far_lo, terms(near_hi), terms(far_lo))
    outer_flux = doubled_flux(far_hi, near_lo, terms(far_hi), terms(near_lo))
    near_change = [i - o for i, o in zip(inner_flux, outer_flux)]
    far_change = [up(o) - i for i, o in zip(inner_flux, outer_flux)]
    return near_change, far_change


def doubled_first_step(cells):
    all_terms = cell_terms(*cells)
    changes = []
    for axis in (0, 1):
        terms = all_terms[axis]
        lower = [roll(f, 1, axis) for f in cells]
        lower_terms = [lower[1 + axis] if c == 0 else roll(terms[c], 1, axis) for c in range(4)]
        flux = doubled_flux(lower, cells, lower_terms, terms)
        own = [2.0 * terms[c] for c in range(3)]
        changes.append(
            (
                [o - f for o, f in zip(own, flux)],
                [roll(f, -1, axis) - o for o, f in zip(own, flux)],
            )
        )
    rows, cols = changes
    return [
        [
            [cells[c] - (0.5 * RATIO) * (rows[a][c] + cols[b][c]) for c in range(3)]
            for b in range(2)
        ]
        for a in range(2)
    ]


def patch_rows(cells):
    half = doubled_first_step(cells)
    by_row = [paired_change(half[0][b], half[1][b], 0) for b in range(2)]
    by_col = [paired_change(half[a][0], half[a][1], 1) for a in range(2)]
    lanes = lane_ids(16)
    result = []
    for a in range(2):
        fine = [
            [half[a][b][c] - (0.5 * RATIO) * (by_row[b][a][c] + by_col[a][b][c]) for c in range(3)]
            for b in range(2)
        ]
        parts = []
        for c in range(3):
            pick = lanes // 2 + 2
            even = jnp.take_along_axis(fine[0][c][4:20], pick, axis=1)
            odd = jnp.take_along_axis(fine[1][c][4:20], pick, axis=1)
            parts.append(jnp.where(lanes % 2 == 0, even, odd))
        result.append(parts)
    return result


def finish(
    state_ref, rim_ref, above_ref, below_ref, inner_ref, left_ref, right_ref,
    strip_ref, error_ref, moved_ref, patch_ref, wide, window, near_rows, columns, strips,
):
    rows, cols = state_ref.shape[1], state_ref.shape[2]
    slab = slice(rows - SLAB, rows)
    top = slice(0, SLAB)
    right = slice(cols, cols + LANES)

    rim_counts = rim_ref[0, 0:8, :]
    above_counts = above_ref[0, 0:8, right]
    below_counts = below_ref[0, 0:8, right]
    get = lambda counts, lane: counts[0, lane].astype(jnp.int32)
    rc, cc, rc_left, rc_right, cc_right = [
        get(rim_counts, k) for k in (OWN_ROWS, OWN_COLS, LEFT_ROWS, RIGHT_ROWS, RIGHT_COLS)
    ]
    cc_above, cc_above_right = [get(above_counts, k) for k in (OWN_COLS, RIGHT_COLS)]
    rc_below, cc_below, rc_below_left, rc_below_right, cc_below_right = [
        get(below_counts, k) for k in (OWN_ROWS, OWN_COLS, LEFT_ROWS, RIGHT_ROWS, RIGHT_COLS)
    ]
    numbers = strip_ref[24:32, :]
    pos_row, pos_col, ext_row, ext_col = [numbers[k, 0].astype(jnp.int32) for k in range(2, 6)]

    edges = coarse_error(
        edge_phases(state_ref, above_ref, below_ref, left_ref, right_ref, strip_ref, near_rows, columns, strips)
    )
    error_ref[...] = put_edges(inner_ref[...], edges)

    def moved_rows(own, own_rim, slab_rows, slab_rim, counts):
        here, left, right_count = counts
        size = own.shape[0]
        aligned = roll_by(slab_rows, here)[0:size]
        lanes, ids = lane_ids(size), row_ids(size)
        body = jnp.where(row_ids(size, cols) < here, aligned, own)
        on_left = lanes >= LANES // 2
        side = jnp.where(on_left, roll_by(slab_rim, left)[0:size], roll_by(slab_rim, right_count)[0:size])
        taken = ids < jnp.where(on_left, left, right_count)
        return body, jnp.where(taken, side, own_rim)

    def roll_by(value, by):
        return pltpu.roll(value, by & (SLAB - 1), 0)

    def moved_cols(body, rim, here, right_count):
        lanes = lane_ids(rim.shape[0])
        first = jnp.where(lanes < here, pltpu.roll(rim, here, 1), body[:, 0:LANES])
        outer = jnp.where(lanes < right_count, pltpu.roll(body[:, cols - LANES : cols], right_count, 1), rim)
        return first, body[:, LANES:cols], jnp.where(lanes >= LANES // 2, rim, outer)

    for comp in range(3):
        own, own_rim = state_ref[comp, :, :], rim_ref[comp, :, :]
        body, side = moved_rows(
            own[top], own_rim[top], above_ref[comp, :, 0:cols], above_ref[comp, :, right], (rc, rc_left, rc_right)
        )
        for part, body, side in (
            (top, body, side),
            (slice(SLAB, rows), own[SLAB:rows], own_rim[SLAB:rows]),
        ):
            first, second, outer = moved_cols(body, side, cc, cc_right)
            moved_ref[comp, part, 0:LANES] = first
            moved_ref[comp, part, LANES:cols] = second
            at = slice(part.start + 8, part.stop + 8)
            wide[comp, at, 0:LANES] = first
            wide[comp, at, LANES:cols] = second
            wide[comp, at, right] = outer
        first, second, outer = moved_cols(
            above_ref[comp, SLAB - 8 : SLAB, 0:cols], above_ref[comp, SLAB - 8 : SLAB, right], cc_above, cc_above_right
        )
        wide[comp, 0:8, 0:LANES] = first
        wide[comp, 0:8, LANES:cols] = second
        wide[comp, 0:8, right] = outer
        body, side = moved_rows(
            below_ref[comp, :, 0:cols], below_ref[comp, :, right], own[slab], own_rim[slab],
            (rc_below, rc_below_left, rc_below_right),
        )
        first, second, outer = moved_cols(body, side, cc_below, cc_below_right)
        wide[comp, rows + 8 : rows + 16, 0:LANES] = first
        wide[comp, rows + 8 : rows + 16, LANES:cols] = second
        wide[comp, rows + 8 : rows + 16, right] = outer

    row_start = pos_row + 4
    base = pl.multiple_of(row_start // 8 * 8, 8)
    width = cols + LANES
    for comp in range(3):
        near = wide[comp, pl.ds(base, 80), :]
        near = pltpu.roll(near, (80 - (row_start - base)) % 80, 0)
        near = pltpu.roll(near, (width + 2 - pos_col) % width, 1)
        window[comp, :, :] = near[0:72, 0:LANES]

    fine_rows, fine_cols = 2 * ext_row, 2 * ext_col

    def patch_block(block, carry):
        start = pl.multiple_of(16 * block, 8)
        cells = [window[c, pl.ds(start, 24), :] for c in range(3)]
        fine = patch_rows(cells)
        lanes, ids = lane_ids(16), row_ids(16)
        for a in range(2):
            inside = (2 * (ids + start) + a < fine_rows) & (lanes < fine_cols)
            for c in range(3):
                patch_ref[c, pl.ds(2 * start + a, 16, stride=2), :] = jnp.where(inside, fine[a][c], 0.0)
        return carry

    lax.fori_loop(0, PATCH // 16, patch_block, 0, unroll=True)


def around(axis, by):
    devices = lax.axis_size(axis)
    return [(i, (i + by) % devices) for i in range(devices)]


def in_vmem(value):
    return pltpu.with_memory_space_constraint(value, pltpu.VMEM)


def vmem(*shape):
    return pltpu.VMEM(shape, jnp.float32)


def per_device(state, row_count, col_count, patch_pos, patch_ext):
    rows, cols = state.shape[1], state.shape[2]
    width = cols + LANES
    half = rows // 2
    numbers = jnp.concatenate([row_count, col_count, patch_pos[0], patch_ext[0]], axis=1)
    to_right, to_left, strip = pl.pallas_call(
        pack_cols,
        out_shape=(vmem(3 * half + 8, LANES), vmem(8, LANES), vmem(32, LANES)),
        in_specs=[VMEM] * 2,
        out_specs=(VMEM,) * 3,
        name="pack_cols",
    )(numbers, state)
    from_left = in_vmem(lax.ppermute(to_right, "col", around("col", 1)))
    from_right = in_vmem(lax.ppermute(to_left, "col", around("col", -1)))
    inner = pl.pallas_call(
        inner_error,
        out_shape=vmem(half, cols // 2),
        in_specs=[VMEM],
        out_specs=VMEM,
        scratch_shapes=[vmem(3, 2, rows, LANES)],
        cost_estimate=pl.CostEstimate(flops=30_000_000, bytes_accessed=600_000, transcendentals=0),
        name="inner_error",
    )(state)
    rim, to_below, to_above = pl.pallas_call(
        pack_rows,
        out_shape=(vmem(3, rows, LANES), vmem(3, SLAB, width), vmem(3, 8, width)),
        in_specs=[VMEM] * 4,
        out_specs=(VMEM,) * 3,
        name="pack_rows",
    )(strip, from_left, from_right, state)
    from_above = in_vmem(lax.ppermute(to_below, "row", around("row", 1)))
    from_below = in_vmem(lax.ppermute(to_above, "row", around("row", -1)))
    return pl.pallas_call(
        finish,
        out_shape=(f32(half, cols // 2), f32(3, rows, cols), f32(3, 2 * PATCH, 2 * PATCH)),
        in_specs=[VMEM] * 8,
        out_specs=(VMEM,) * 3,
        scratch_shapes=[
            vmem(3, rows + 16, width),
            vmem(3, 72, LANES),
            vmem(3, 16, cols),
            vmem(3, 2, 16, LANES),
            vmem(3, 2, 16, LANES),
        ],
        compiler_params=PARAMS,
        name="finish",
    )(state, rim, from_above, from_below, inner, from_left, from_right, strip)


def solution(mesh):
    placed = (
        P(None, "row", "col"),
        P("row", "col"),
        P("row", "col"),
        P("row", "col", None),
        P("row", "col", None),
    )
    return jax.shard_map(
        per_device,
        mesh=mesh,
        in_specs=placed,
        out_specs=(P("row", "col"), P(None, "row", "col"), P(None, "row", "col")),
        check_vma=False,
    )
```

```python
import jax
import jax.numpy as jnp
from jax import lax
from jax.experimental import pallas as pl
from jax.experimental.pallas import tpu as pltpu
from jax.sharding import PartitionSpec as P

SLAB = 64
PATCH = 64
LANES = 128

RATIO = 0.1
ERR_SCALE = 10.0

RIGHT_ROWS, RIGHT_COLS, LEFT_ROWS, LEFT_COLS, OWN_ROWS, OWN_COLS = 6, 7, 8, 9, 10, 11

VMEM = pl.BlockSpec(memory_space=pltpu.VMEM)
PARAMS = pltpu.CompilerParams(vmem_limit_bytes=32 * 1024 * 1024)


def f32(*shape):
    return jax.ShapeDtypeStruct(shape, jnp.float32)


def lane_ids(rows, width=LANES):
    return lax.broadcasted_iota(jnp.int32, (rows, width), 1)


def row_ids(rows, width=LANES):
    return lax.broadcasted_iota(jnp.int32, (rows, width), 0)


def roll(value, by, axis):
    return pltpu.roll(value, by % value.shape[axis], axis)


def cell_terms(depth, first, second):
    inverse_root = lax.rsqrt(depth)
    wave = depth * inverse_root
    inverse = inverse_root * inverse_root
    first_vel = first * inverse
    second_vel = second * inverse
    pressure = 0.5 * depth * depth
    cross = first * second_vel
    row_terms = (first, first * first_vel + pressure, cross, jnp.abs(first_vel) + wave)
    col_terms = (second, cross, second * second_vel + pressure, jnp.abs(second_vel) + wave)
    return row_terms, col_terms


def doubled_flux(left, right, left_terms, right_terms):
    speed = jnp.maximum(left_terms[3], right_terms[3])
    return [(left_terms[c] + right_terms[c]) - speed * (right[c] - left[c]) for c in range(3)]


def spread_step(fields, row_by, col_by):
    row_terms, col_terms = cell_terms(*fields)
    total = None
    for terms, by, axis in ((row_terms, row_by, 0), (col_terms, col_by, 1)):
        lower = [roll(f, by, axis) for f in fields]
        momentum = lower[1 + axis]
        lower_terms = [momentum if c == 0 else roll(terms[c], by, axis) for c in range(4)]
        flux = doubled_flux(lower, fields, lower_terms, terms)
        change = [roll(f, -by, axis) - f for f in flux]
        total = change if total is None else [t + c for t, c in zip(total, change)]
    return [f - (0.5 * RATIO) * t for f, t in zip(fields, total)]


def pair_change(near, far, near_terms, far_terms, axis):
    inner = doubled_flux(near, far, near_terms, far_terms)
    before = [roll(f, 1, axis) for f in far]
    before_terms = [before[1 + axis] if c == 0 else roll(far_terms[c], 1, axis) for c in range(4)]
    outer = doubled_flux(before, near, before_terms, near_terms)
    near_change = [i - o for i, o in zip(inner, outer)]
    far_change = [roll(o, -1, axis) - i for i, o in zip(inner, outer)]
    return near_change, far_change


def paired_step(phases):
    terms = [[cell_terms(*phases[x][y]) for y in range(2)] for x in range(2)]
    along_first = [
        pair_change(phases[0][y], phases[1][y], terms[0][y][0], terms[1][y][0], 0) for y in range(2)
    ]
    along_second = [
        pair_change(phases[x][0], phases[x][1], terms[x][0][1], terms[x][1][1], 1) for x in range(2)
    ]
    return [
        [
            [
                phases[x][y][c] - (0.5 * RATIO) * (along_first[y][x][c] + along_second[x][y][c])
                for c in range(3)
            ]
            for y in range(2)
        ]
        for x in range(2)
    ]


def block_mean(phases):
    return [
        0.25 * ((phases[0][0][c] + phases[1][0][c]) + (phases[0][1][c] + phases[1][1][c])) for c in range(3)
    ]


def coarse_error(phases):
    fine = block_mean(paired_step(paired_step(phases)))
    coarse = spread_step(block_mean(phases), 1, 1)
    parts = [jnp.abs(f - c) for f, c in zip(fine, coarse)]
    return ERR_SCALE * ((parts[0] + parts[1]) + parts[2])


def every_other(first, second, parity):
    lanes = lane_ids(first.shape[0])
    pick = (2 * lanes + parity) % LANES
    low = jnp.take_along_axis(first, pick, axis=1)
    high = jnp.take_along_axis(second, pick, axis=1)
    return jnp.where(lanes < LANES // 2, low, high)


def pack_cols(row_count, col_count, patch_pos, patch_ext, state_ref, left_ref, right_ref, strip_ref, slab_ref):
    rows, cols = state_ref.shape[1], state_ref.shape[2]
    half = rows // 2
    rc, cc = row_count[...].astype(jnp.float32), col_count[...].astype(jnp.float32)
    lanes = lane_ids(half)
    for comp in range(3):
        upper = state_ref[comp, 0:half, cols - LANES : cols]
        lower = roll(state_ref[comp, half:rows, cols - LANES : cols], LANES // 2, 1)
        left_ref[comp * half : (comp + 1) * half, :] = jnp.where(lanes >= LANES // 2, upper, lower)
    lanes = lane_ids(rows)
    packed = None
    for comp in range(3):
        ends = jnp.where(lanes < LANES // 2, state_ref[comp, :, 0:LANES], state_ref[comp, :, cols - LANES : cols])
        ends = roll(ends, 8 * comp + 4, 1)
        packed = ends if packed is None else jnp.where(lanes >= 8 * comp, ends, packed)
    strip_ref[0:24, :] = packed.T[0:24]
    ids = row_ids(8)
    pos, ext = patch_pos[0].astype(jnp.float32), patch_ext[0].astype(jnp.float32)
    spread = jnp.broadcast_to(ext[:, 1:2], (8, LANES))
    for k, number in enumerate((rc, cc, pos[:, 0:1], pos[:, 1:2], ext[:, 0:1])):
        spread = jnp.where(ids == k, number, spread)
    strip_ref[24:32, :] = spread
    counts = jnp.where(ids == 6, rc, cc)
    for ref, base, at in ((left_ref, 3 * half, 2), (right_ref, 0, 4)):
        ref[base : base + 8, :] = counts
        for comp in range(3):
            ref[base + 2 * comp : base + 2 * comp + 2, :] = strip_ref[8 * comp + at : 8 * comp + at + 2, :]
    slab_ref[...] = state_ref[:, rows - SLAB : rows, :]


def pack_rows(strip_ref, left_ref, right_ref, state_ref, rim_ref, down_ref, up_ref, edge_ref):
    rows, cols = state_ref.shape[1], state_ref.shape[2]
    half = rows // 2
    rc, cc = strip_ref[24:25, :], strip_ref[25:26, :]
    right = jnp.concatenate([right_ref[...], jnp.zeros((LANES - 8, LANES), jnp.float32)], axis=0).T
    lanes = lane_ids(rows)
    left_rc = left_ref[3 * half + 6 : 3 * half + 7, :]
    left_cc = left_ref[3 * half + 7 : 3 * half + 8, :]
    counts = jnp.where(lanes == OWN_ROWS, rc, cc)
    counts = jnp.where(lanes == LEFT_COLS, left_cc, counts)
    counts = jnp.where(lanes == LEFT_ROWS, left_rc, counts)
    for comp in range(3):
        packed = left_ref[comp * half : (comp + 1) * half, :]
        left = jnp.concatenate([packed, roll(packed, LANES // 2, 1)], axis=0)
        inner = right if comp == 0 else roll(right, -2 * comp, 1)
        inner = jnp.where(lanes < LEFT_ROWS, inner, counts)
        rim = jnp.where(lanes >= LANES // 2, left, inner)
        rim_ref[comp] = rim
        down_ref[comp] = rim[rows - SLAB : rows]
        up_ref[comp, :, 0:cols] = state_ref[comp, 0:8, :]
        up_ref[comp, :, cols : cols + LANES] = rim[0:8]
        edge_ref[comp, 0:2, :] = left_ref[3 * half + 2 * comp : 3 * half + 2 * comp + 2, :]
        edge_ref[comp, 2:6, :] = strip_ref[8 * comp + 4 : 8 * comp + 8, :]
        edge_ref[comp, 6:10, :] = strip_ref[8 * comp : 8 * comp + 4, :]
        edge_ref[comp, 10:12, :] = right_ref[2 * comp : 2 * comp + 2, :]
        edge_ref[comp, 12:16, :] = strip_ref[8 * comp + 4 : 8 * comp + 8, :]
    edge_ref[3, 0:8, :] = strip_ref[24:32, :]


def inner_error(state_ref, error_ref, columns):
    rows = state_ref.shape[1]
    half = rows // 2
    for comp in range(3):
        first, second = state_ref[comp, :, 0:LANES], state_ref[comp, :, LANES : 2 * LANES]
        for parity in range(2):
            columns[comp, parity] = every_other(first, second, parity)
    size = 24
    for start in range(0, half - 2, size - 4):
        start = min(start, half - size)
        phases = [
            [
                [columns[c, y, pl.ds(2 * start + x, size, stride=2), :] for c in range(3)]
                for y in range(2)
            ]
            for x in range(2)
        ]
        error = coarse_error(phases)
        low = 0 if start == 0 else 2
        error_ref[start + low : start + size, :] = error[low:size]


def edge_phases(state_ref, slab_ref, above_ref, below_ref, edge_ref, near_rows, columns, corners_ref):
    rows, cols = state_ref.shape[1], state_ref.shape[2]
    right = slice(cols, cols + LANES)
    lanes = lane_ids(8)
    packed_up, packed_down = None, None
    for comp in range(3):
        near_rows[comp, 0:2, :] = slab_ref[comp, SLAB - 2 : SLAB, :]
        near_rows[comp, 2:6, :] = state_ref[comp, 0:4, :]
        near_rows[comp, 6:10, :] = state_ref[comp, rows - 4 : rows, :]
        near_rows[comp, 10:12, :] = below_ref[comp, 0:2, 0:cols]
        near_rows[comp, 12:16, :] = state_ref[comp, 0:4, :]
        first, second = near_rows[comp, :, 0:LANES], near_rows[comp, :, LANES : 2 * LANES]
        for parity in range(2):
            columns[comp, parity] = every_other(first, second, parity)

        def around_corner(body, rim):
            start = jnp.where(lanes < LANES // 2, body[:, 0:LANES], rim)
            end = jnp.where(lanes < LANES // 2, rim, body[:, cols - LANES : cols])
            first_six = (lanes >= 12 * comp) & (lanes < 12 * comp + 6)
            return jnp.where(first_six, roll(start, 12 * comp + 2, 1), roll(end, 12 * comp + 10, 1))

        up = around_corner(slab_ref[comp, SLAB - 8 : SLAB, :], above_ref[comp, SLAB - 8 : SLAB, :])
        down = around_corner(below_ref[comp, :, 0:cols], below_ref[comp, :, right])
        packed_up = up if comp == 0 else jnp.where(lanes >= 12 * comp, up, packed_up)
        packed_down = down if comp == 0 else jnp.where(lanes >= 12 * comp, down, packed_down)
    corners = jnp.concatenate([packed_down, jnp.ones((LANES - 16, LANES), jnp.float32), packed_up], axis=0).T
    for comp in range(3):
        corners_ref[comp, 0:12, :] = corners[12 * comp : 12 * comp + 12, :]
        corners_ref[comp, 12:16, :] = edge_ref[comp, 12:16, :]
    phases = []
    for x in range(2):
        phases.append([])
        for y in range(2):
            cells = []
            for comp, turned in ((0, 0), (1, 2), (2, 1)):
                by_row = columns[comp, y, pl.ds(x, 8, stride=2), :]
                own, outer = [ref[turned, pl.ds(x, 8, stride=2), :] for ref in (edge_ref, corners_ref)]
                cells.append(jnp.concatenate([by_row, every_other(own, outer, y)], axis=0))
            phases[-1].append(cells)
    return phases


def put_edges(error, edges):
    half_rows = error.shape[0]
    turned = jnp.concatenate([edges, jnp.zeros((LANES - 16, LANES), jnp.float32)], axis=0).T[0:half_rows]
    lanes, ids = lane_ids(half_rows), row_ids(half_rows)
    error = jnp.where(ids == 0, edges[1:2], jnp.where(ids == half_rows - 1, edges[4:5], error))
    return jnp.where(
        lanes == 0, roll(turned, -9, 1), jnp.where(lanes == LANES - 1, roll(turned, LANES - 13, 1), error)
    )


def minmod(lower_diff, upper_diff):
    return jnp.maximum(jnp.minimum(lower_diff, upper_diff), 0.0) + jnp.minimum(
        jnp.maximum(lower_diff, upper_diff), 0.0
    )


def paired_change(near, far, axis):
    down = lambda v: roll(v, 1, axis)
    up = lambda v: roll(v, -1, axis)
    inner = [f - n for n, f in zip(near, far)]
    outer = [n - down(f) for n, f in zip(near, far)]
    near_half = [0.5 * minmod(o, i) for o, i in zip(outer, inner)]
    far_half = [0.5 * minmod(i, up(o)) for o, i in zip(outer, inner)]
    near_hi = [n + s for n, s in zip(near, near_half)]
    near_lo = [n - s for n, s in zip(near, near_half)]
    far_hi = [down(f + s) for f, s in zip(far, far_half)]
    far_lo = [f - s for f, s in zip(far, far_half)]
    terms = lambda cells: cell_terms(*cells)[axis]
    inner_flux = doubled_flux(near_hi, far_lo, terms(near_hi), terms(far_lo))
    outer_flux = doubled_flux(far_hi, near_lo, terms(far_hi), terms(near_lo))
    near_change = [i - o for i, o in zip(inner_flux, outer_flux)]
    far_change = [up(o) - i for i, o in zip(inner_flux, outer_flux)]
    return near_change, far_change


def doubled_first_step(cells):
    all_terms = cell_terms(*cells)
    changes = []
    for axis in (0, 1):
        terms = all_terms[axis]
        lower = [roll(f, 1, axis) for f in cells]
        lower_terms = [lower[1 + axis] if c == 0 else roll(terms[c], 1, axis) for c in range(4)]
        flux = doubled_flux(lower, cells, lower_terms, terms)
        own = [2.0 * terms[c] for c in range(3)]
        changes.append(
            (
                [o - f for o, f in zip(own, flux)],
                [roll(f, -1, axis) - o for o, f in zip(own, flux)],
            )
        )
    rows, cols = changes
    return [
        [
            [cells[c] - (0.5 * RATIO) * (rows[a][c] + cols[b][c]) for c in range(3)]
            for b in range(2)
        ]
        for a in range(2)
    ]


def patch_rows(cells):
    half = doubled_first_step(cells)
    by_row = [paired_change(half[0][b], half[1][b], 0) for b in range(2)]
    by_col = [paired_change(half[a][0], half[a][1], 1) for a in range(2)]
    lanes = lane_ids(16)
    result = []
    for a in range(2):
        fine = [
            [half[a][b][c] - (0.5 * RATIO) * (by_row[b][a][c] + by_col[a][b][c]) for c in range(3)]
            for b in range(2)
        ]
        parts = []
        for c in range(3):
            pick = lanes // 2 + 2
            even = jnp.take_along_axis(fine[0][c][4:20], pick, axis=1)
            odd = jnp.take_along_axis(fine[1][c][4:20], pick, axis=1)
            parts.append(jnp.where(lanes % 2 == 0, even, odd))
        result.append(parts)
    return result


def finish(
    state_ref, rim_ref, slab_ref, above_ref, below_ref, inner_ref, edge_ref,
    error_ref, moved_ref, patch_ref, wide, window, near_rows, columns, corners,
):
    rows, cols = state_ref.shape[1], state_ref.shape[2]
    bottom = slice(rows - SLAB, rows)
    top = slice(0, SLAB)
    right = slice(cols, cols + LANES)

    rim_counts = rim_ref[0, 0:8, :]
    above_counts = above_ref[0, 0:8, :]
    below_counts = below_ref[0, 0:8, right]
    get = lambda counts, lane: counts[0, lane].astype(jnp.int32)
    rc, cc, rc_left, rc_right, cc_right = [
        get(rim_counts, k) for k in (OWN_ROWS, OWN_COLS, LEFT_ROWS, RIGHT_ROWS, RIGHT_COLS)
    ]
    cc_above, cc_above_right = [get(above_counts, k) for k in (OWN_COLS, RIGHT_COLS)]
    rc_below, cc_below, rc_below_left, rc_below_right, cc_below_right = [
        get(below_counts, k) for k in (OWN_ROWS, OWN_COLS, LEFT_ROWS, RIGHT_ROWS, RIGHT_COLS)
    ]
    numbers = edge_ref[3, 0:8, :]
    pos_row, pos_col, ext_row, ext_col = [numbers[k, 0].astype(jnp.int32) for k in range(2, 6)]

    edges = coarse_error(
        edge_phases(state_ref, slab_ref, above_ref, below_ref, edge_ref, near_rows, columns, corners)
    )
    error_ref[...] = put_edges(inner_ref[...], edges)

    def moved_rows(own, own_rim, slab_rows, slab_rim, counts):
        here, left, right_count = counts
        size = own.shape[0]
        aligned = roll_by(slab_rows, here)[0:size]
        lanes, ids = lane_ids(size), row_ids(size)
        body = jnp.where(row_ids(size, cols) < here, aligned, own)
        on_left = lanes >= LANES // 2
        side = jnp.where(on_left, roll_by(slab_rim, left)[0:size], roll_by(slab_rim, right_count)[0:size])
        taken = ids < jnp.where(on_left, left, right_count)
        return body, jnp.where(taken, side, own_rim)

    def roll_by(value, by):
        return pltpu.roll(value, by & (SLAB - 1), 0)

    def moved_cols(body, rim, here, right_count):
        lanes = lane_ids(rim.shape[0])
        first = jnp.where(lanes < here, pltpu.roll(rim, here, 1), body[:, 0:LANES])
        outer = jnp.where(lanes < right_count, pltpu.roll(body[:, cols - LANES : cols], right_count, 1), rim)
        return first, body[:, LANES:cols], jnp.where(lanes >= LANES // 2, rim, outer)

    for comp in range(3):
        own, own_rim = state_ref[comp, :, :], rim_ref[comp, :, :]
        body, side = moved_rows(
            own[top], own_rim[top], slab_ref[comp, :, :], above_ref[comp, :, :], (rc, rc_left, rc_right)
        )
        for part, body, side in (
            (top, body, side),
            (slice(SLAB, rows), own[SLAB:rows], own_rim[SLAB:rows]),
        ):
            first, second, outer = moved_cols(body, side, cc, cc_right)
            moved_ref[comp, part, 0:LANES] = first
            moved_ref[comp, part, LANES:cols] = second
            at = slice(part.start + 8, part.stop + 8)
            wide[comp, at, 0:LANES] = first
            wide[comp, at, LANES:cols] = second
            wide[comp, at, right] = outer
        first, second, outer = moved_cols(
            slab_ref[comp, SLAB - 8 : SLAB, :], above_ref[comp, SLAB - 8 : SLAB, :], cc_above, cc_above_right
        )
        wide[comp, 0:8, 0:LANES] = first
        wide[comp, 0:8, LANES:cols] = second
        wide[comp, 0:8, right] = outer
        body, side = moved_rows(
            below_ref[comp, :, 0:cols], below_ref[comp, :, right], own[bottom], own_rim[bottom],
            (rc_below, rc_below_left, rc_below_right),
        )
        first, second, outer = moved_cols(body, side, cc_below, cc_below_right)
        wide[comp, rows + 8 : rows + 16, 0:LANES] = first
        wide[comp, rows + 8 : rows + 16, LANES:cols] = second
        wide[comp, rows + 8 : rows + 16, right] = outer

    row_start = pos_row + 4
    base = pl.multiple_of(row_start // 8 * 8, 8)
    width = cols + LANES
    for comp in range(3):
        near = wide[comp, pl.ds(base, 80), :]
        near = pltpu.roll(near, (80 - (row_start - base)) % 80, 0)
        near = pltpu.roll(near, (width + 2 - pos_col) % width, 1)
        window[comp, :, :] = near[0:72, 0:LANES]

    fine_rows, fine_cols = 2 * ext_row, 2 * ext_col

    def patch_block(block, carry):
        start = pl.multiple_of(16 * block, 8)
        cells = [window[c, pl.ds(start, 24), :] for c in range(3)]
        fine = patch_rows(cells)
        lanes, ids = lane_ids(16), row_ids(16)
        for a in range(2):
            inside = (2 * (ids + start) + a < fine_rows) & (lanes < fine_cols)
            for c in range(3):
                patch_ref[c, pl.ds(2 * start + a, 16, stride=2), :] = jnp.where(inside, fine[a][c], 0.0)
        return carry

    lax.fori_loop(0, PATCH // 16, patch_block, 0, unroll=True)


def around(axis, by):
    devices = lax.axis_size(axis)
    return [(i, (i + by) % devices) for i in range(devices)]


def in_vmem(value):
    return pltpu.with_memory_space_constraint(value, pltpu.VMEM)


def in_hbm(value):
    return pltpu.with_memory_space_constraint(value, pltpu.HBM)


def vmem(*shape):
    return pltpu.VMEM(shape, jnp.float32)


def per_device(state, row_count, col_count, patch_pos, patch_ext):
    rows, cols = state.shape[1], state.shape[2]
    width = cols + LANES
    half = rows // 2
    patch_pos, patch_ext = in_hbm(patch_pos), in_hbm(patch_ext)
    to_right, to_left, strip, slab = pl.pallas_call(
        pack_cols,
        out_shape=(vmem(3 * half + 8, LANES), vmem(8, LANES), vmem(32, LANES), vmem(3, SLAB, cols)),
        in_specs=[VMEM] * 5,
        out_specs=(VMEM,) * 4,
        name="pack_cols",
    )(row_count, col_count, patch_pos, patch_ext, state)
    strip, here = in_vmem(strip), in_vmem(state)
    from_left = in_vmem(lax.ppermute(to_right, "col", around("col", 1)))
    from_right = in_vmem(lax.ppermute(to_left, "col", around("col", -1)))
    slab_above = in_vmem(lax.ppermute(slab, "row", around("row", 1)))
    inner = pl.pallas_call(
        inner_error,
        out_shape=vmem(half, cols // 2),
        in_specs=[VMEM],
        out_specs=VMEM,
        scratch_shapes=[vmem(3, 2, rows, LANES)],
        cost_estimate=pl.CostEstimate(flops=30_000_000, bytes_accessed=600_000, transcendentals=0),
        name="inner_error",
    )(here)
    rim, to_below, to_above, edge = pl.pallas_call(
        pack_rows,
        out_shape=(vmem(3, rows, LANES), vmem(3, SLAB, LANES), vmem(3, 8, width), vmem(4, 16, LANES)),
        in_specs=[VMEM] * 4,
        out_specs=(VMEM,) * 4,
        name="pack_rows",
    )(strip, from_left, from_right, here)
    from_above = in_vmem(lax.ppermute(to_below, "row", around("row", 1)))
    from_below = in_vmem(lax.ppermute(to_above, "row", around("row", -1)))
    return pl.pallas_call(
        finish,
        out_shape=(f32(half, cols // 2), f32(3, rows, cols), f32(3, 2 * PATCH, 2 * PATCH)),
        in_specs=[VMEM] * 7,
        out_specs=(VMEM,) * 3,
        scratch_shapes=[
            vmem(3, rows + 16, width),
            vmem(3, 72, LANES),
            vmem(3, 16, cols),
            vmem(3, 2, 16, LANES),
            vmem(3, 16, LANES),
        ],
        compiler_params=PARAMS,
        name="finish",
    )(here, rim, slab_above, from_above, from_below, inner, edge)


def solution(mesh):
    placed = (
        P(None, "row", "col"),
        P("row", "col"),
        P("row", "col"),
        P("row", "col", None),
        P("row", "col", None),
    )
    return jax.shard_map(
        per_device,
        mesh=mesh,
        in_specs=placed,
        out_specs=(P("row", "col"), P(None, "row", "col"), P(None, "row", "col")),
        check_vma=False,
    )
```

```python
import jax
import jax.numpy as jnp
from jax import lax
from jax.experimental import pallas as pl
from jax.experimental.pallas import tpu as pltpu
from jax.sharding import PartitionSpec as P

SLAB = 64
PATCH = 64
LANES = 128
PATCH_ROWS = 64

RATIO = 0.1
ERR_SCALE = 10.0

RIGHT_ROWS, RIGHT_COLS, LEFT_ROWS, OWN_ROWS, OWN_COLS = 6, 7, 8, 10, 11
DOWN_ROWS = 3 * SLAB // 2 + 8

VMEM = pl.BlockSpec(memory_space=pltpu.VMEM)
SMEM = pl.BlockSpec(memory_space=pltpu.SMEM)
ANY = pl.BlockSpec(memory_space=pl.ANY)
PARAMS = pltpu.CompilerParams(vmem_limit_bytes=32 * 1024 * 1024)


def f32(*shape):
    return jax.ShapeDtypeStruct(shape, jnp.float32)


def lane_ids(rows, width=LANES):
    return lax.broadcasted_iota(jnp.int32, (rows, width), 1)


def row_ids(rows, width=LANES):
    return lax.broadcasted_iota(jnp.int32, (rows, width), 0)


def roll(value, by, axis):
    return pltpu.roll(value, by % value.shape[axis], axis)


def cell_terms(depth, first, second):
    inverse_root = lax.rsqrt(depth)
    wave = depth * inverse_root
    inverse = inverse_root * inverse_root
    first_vel = first * inverse
    second_vel = second * inverse
    pressure = 0.5 * depth * depth
    cross = first * second_vel
    row_terms = (first, first * first_vel + pressure, cross, jnp.abs(first_vel) + wave)
    col_terms = (second, cross, second * second_vel + pressure, jnp.abs(second_vel) + wave)
    return row_terms, col_terms


def doubled_flux(left, right, left_terms, right_terms):
    speed = jnp.maximum(left_terms[3], right_terms[3])
    return [(left_terms[c] + right_terms[c]) - speed * (right[c] - left[c]) for c in range(3)]


def spread_step(fields, row_by, col_by):
    row_terms, col_terms = cell_terms(*fields)
    total = None
    for terms, by, axis in ((row_terms, row_by, 0), (col_terms, col_by, 1)):
        lower = [roll(f, by, axis) for f in fields]
        momentum = lower[1 + axis]
        lower_terms = [momentum if c == 0 else roll(terms[c], by, axis) for c in range(4)]
        flux = doubled_flux(lower, fields, lower_terms, terms)
        change = [roll(f, -by, axis) - f for f in flux]
        total = change if total is None else [t + c for t, c in zip(total, change)]
    return [f - (0.5 * RATIO) * t for f, t in zip(fields, total)]


def pair_change(near, far, near_terms, far_terms, axis):
    inner = doubled_flux(near, far, near_terms, far_terms)
    before = [roll(f, 1, axis) for f in far]
    before_terms = [before[1 + axis] if c == 0 else roll(far_terms[c], 1, axis) for c in range(4)]
    outer = doubled_flux(before, near, before_terms, near_terms)
    near_change = [i - o for i, o in zip(inner, outer)]
    far_change = [roll(o, -1, axis) - i for i, o in zip(inner, outer)]
    return near_change, far_change


def paired_step(phases):
    terms = [[cell_terms(*phases[x][y]) for y in range(2)] for x in range(2)]
    along_first = [
        pair_change(phases[0][y], phases[1][y], terms[0][y][0], terms[1][y][0], 0) for y in range(2)
    ]
    along_second = [
        pair_change(phases[x][0], phases[x][1], terms[x][0][1], terms[x][1][1], 1) for x in range(2)
    ]
    return [
        [
            [
                phases[x][y][c] - (0.5 * RATIO) * (along_first[y][x][c] + along_second[x][y][c])
                for c in range(3)
            ]
            for y in range(2)
        ]
        for x in range(2)
    ]


def block_mean(phases):
    return [
        0.25 * ((phases[0][0][c] + phases[1][0][c]) + (phases[0][1][c] + phases[1][1][c])) for c in range(3)
    ]


def coarse_error(phases):
    fine = block_mean(paired_step(paired_step(phases)))
    coarse = spread_step(block_mean(phases), 1, 1)
    parts = [jnp.abs(f - c) for f, c in zip(fine, coarse)]
    return ERR_SCALE * ((parts[0] + parts[1]) + parts[2])


def every_other(first, second, parity):
    lanes = lane_ids(first.shape[0])
    pick = (2 * lanes + parity) % LANES
    low = jnp.take_along_axis(first, pick, axis=1)
    high = jnp.take_along_axis(second, pick, axis=1)
    return jnp.where(lanes < LANES // 2, low, high)


def pack_cols(row_count, state_ref, left_ref, strip_ref, slab_ref):
    rows, cols = state_ref.shape[1], state_ref.shape[2]
    half = rows // 2
    rc = row_count[0, 0].astype(jnp.float32)
    lanes = lane_ids(half)
    for comp in range(3):
        upper = state_ref[comp, 0:half, cols - LANES : cols]
        lower = roll(state_ref[comp, half:rows, cols - LANES : cols], LANES // 2, 1)
        left_ref[comp * half : (comp + 1) * half, :] = jnp.where(lanes >= LANES // 2, upper, lower)
    lanes = lane_ids(rows)
    packed = None
    for comp in range(3):
        ends = jnp.where(lanes < LANES // 2, state_ref[comp, :, 0:LANES], state_ref[comp, :, cols - LANES : cols])
        ends = roll(ends, 8 * comp + 4, 1)
        packed = ends if packed is None else jnp.where(lanes >= 8 * comp, ends, packed)
    strip_ref[0:24, :] = packed.T[0:24]
    strip_ref[24:32, :] = jnp.full((8, LANES), rc)
    left_ref[3 * half : 3 * half + 8, :] = jnp.full((8, LANES), rc)
    for comp in range(3):
        left_ref[3 * half + 2 * comp : 3 * half + 2 * comp + 2, :] = strip_ref[8 * comp + 2 : 8 * comp + 4, :]
    slab_ref[...] = state_ref[:, rows - SLAB : rows, :]


def pack_right(col_count, strip_ref, right_ref, counts_ref):
    cc = col_count[0, 0].astype(jnp.float32)
    counts = jnp.where(row_ids(8) == 6, strip_ref[24:32, :], cc)
    counts_ref[...] = counts
    right_ref[...] = counts
    for comp in range(3):
        right_ref[2 * comp : 2 * comp + 2, :] = strip_ref[8 * comp + 4 : 8 * comp + 6, :]


def is_odd():
    return lax.axis_index("row") % 2 == 1


def pack_rows(counts_ref, strip_ref, left_ref, right_ref, state_ref, inner_ref, rim_ref, within_ref, across_ref, edge_ref):
    rows, cols = state_ref.shape[1], state_ref.shape[2]
    half = rows // 2
    rc, cc = counts_ref[6:7, :], counts_ref[7:8, :]
    right = jnp.concatenate([right_ref[...], jnp.zeros((LANES - 8, LANES), jnp.float32)], axis=0).T
    lanes = lane_ids(rows)
    left_rc = left_ref[3 * half + 6 : 3 * half + 7, :]
    counts = jnp.where(lanes == LEFT_ROWS, left_rc, jnp.where(lanes == OWN_ROWS, rc, cc))
    odd = is_odd()
    packed_half = SLAB // 2
    low = lane_ids(packed_half) < LANES // 2

    def put(at, down, up):
        size = down.shape[0]
        within_ref[at : at + size, :] = jnp.where(odd, up, down)
        across_ref[at : at + size, :] = jnp.where(odd, down, up)

    ups, downs = [], []
    for comp in range(3):
        packed = left_ref[comp * half : (comp + 1) * half, :]
        left = jnp.concatenate([packed, roll(packed, LANES // 2, 1)], axis=0)
        inner = right if comp == 0 else roll(right, -2 * comp, 1)
        inner = jnp.where(lanes < LEFT_ROWS, inner, counts)
        rim = jnp.where(lanes >= LANES // 2, left, inner)
        rim_ref[comp] = rim
        last = packed[half - SLAB : half]
        downs.append(jnp.where(low, last[0:packed_half], roll(last[packed_half:SLAB], LANES // 2, 1)))
        ups += [state_ref[comp, 0:8, LANES * t : LANES * (t + 1)] for t in range(cols // LANES)] + [rim[0:8]]
        edge_ref[comp, 0:2, :] = left_ref[3 * half + 2 * comp : 3 * half + 2 * comp + 2, :]
        edge_ref[comp, 2:6, :] = strip_ref[8 * comp + 4 : 8 * comp + 8, :]
        edge_ref[comp, 6:10, :] = strip_ref[8 * comp : 8 * comp + 4, :]
        edge_ref[comp, 10:12, :] = right_ref[2 * comp : 2 * comp + 2, :]
        edge_ref[comp, 12:16, :] = strip_ref[8 * comp + 4 : 8 * comp + 8, :]
    downs.append(jnp.where(row_ids(8) == 6, cc, right_ref[...]))
    down = jnp.concatenate(downs, axis=0)
    up = jnp.concatenate(ups, axis=0)
    size = up.shape[0]
    put(0, down[0:size], up)
    put(size, down[size:DOWN_ROWS], down[size:DOWN_ROWS])
    across_ref[DOWN_ROWS : DOWN_ROWS + 8, :] = jnp.zeros((8, LANES), jnp.float32)


def inner_error(pos_ref, ext_ref, state_ref, error_ref, numbers_ref, columns, pos, ext, sems):
    rows = state_ref.shape[1]
    half = rows // 2
    copies = [pltpu.make_async_copy(src, dst, sems.at[k]) for k, (src, dst) in enumerate(((pos_ref, pos), (ext_ref, ext)))]
    for copy in copies:
        copy.start()
    for comp in range(3):
        first, second = state_ref[comp, :, 0:LANES], state_ref[comp, :, LANES : 2 * LANES]
        for parity in range(2):
            columns[comp, parity] = every_other(first, second, parity)
    size = 24
    for start in range(0, half - 2, size - 4):
        start = min(start, half - size)
        phases = [
            [
                [columns[c, y, pl.ds(2 * start + x, size, stride=2), :] for c in range(3)]
                for y in range(2)
            ]
            for x in range(2)
        ]
        error = coarse_error(phases)
        low = 0 if start == 0 else 2
        error_ref[start + low : start + size, :] = error[low:size]
    for copy in copies:
        copy.wait()
    pair = [v[0].astype(jnp.float32) for v in (pos, ext)]
    numbers = jnp.broadcast_to(pair[1][:, 1:2], (8, LANES))
    for k, number in enumerate((pair[0][:, 0:1], pair[0][:, 1:2], pair[1][:, 0:1])):
        numbers = jnp.where(row_ids(8) == k, number, numbers)
    numbers_ref[...] = numbers


def edge_phases(state_ref, slab_ref, above_rim, below, edge_ref, near_rows, columns, corners_ref):
    rows, cols = state_ref.shape[1], state_ref.shape[2]
    right = slice(cols, cols + LANES)
    lanes = lane_ids(8)
    packed_up, packed_down = None, None
    for comp in range(3):
        near_rows[comp, 0:2, :] = slab_ref[comp, SLAB - 2 : SLAB, :]
        near_rows[comp, 2:6, :] = state_ref[comp, 0:4, :]
        near_rows[comp, 6:10, :] = state_ref[comp, rows - 4 : rows, :]
        near_rows[comp, 10:12, :] = below[comp, 0:2, 0:cols]
        near_rows[comp, 12:16, :] = state_ref[comp, 0:4, :]
        first, second = near_rows[comp, :, 0:LANES], near_rows[comp, :, LANES : 2 * LANES]
        for parity in range(2):
            columns[comp, parity] = every_other(first, second, parity)

        def around_corner(body, rim):
            start = jnp.where(lanes < LANES // 2, body[:, 0:LANES], rim)
            end = jnp.where(lanes < LANES // 2, rim, body[:, cols - LANES : cols])
            first_six = (lanes >= 12 * comp) & (lanes < 12 * comp + 6)
            return jnp.where(first_six, roll(start, 12 * comp + 2, 1), roll(end, 12 * comp + 10, 1))

        up = around_corner(slab_ref[comp, SLAB - 8 : SLAB, :], above_rim[comp, SLAB - 8 : SLAB, :])
        down = around_corner(below[comp, :, 0:cols], below[comp, :, right])
        packed_up = up if comp == 0 else jnp.where(lanes >= 12 * comp, up, packed_up)
        packed_down = down if comp == 0 else jnp.where(lanes >= 12 * comp, down, packed_down)
    corners = jnp.concatenate([packed_down, jnp.ones((LANES - 16, LANES), jnp.float32), packed_up], axis=0).T
    for comp in range(3):
        corners_ref[comp, 0:12, :] = corners[12 * comp : 12 * comp + 12, :]
        corners_ref[comp, 12:16, :] = edge_ref[comp, 12:16, :]
    phases = []
    for x in range(2):
        phases.append([])
        for y in range(2):
            cells = []
            for comp, turned in ((0, 0), (1, 2), (2, 1)):
                by_row = columns[comp, y, pl.ds(x, 8, stride=2), :]
                own, outer = [ref[turned, pl.ds(x, 8, stride=2), :] for ref in (edge_ref, corners_ref)]
                cells.append(jnp.concatenate([by_row, every_other(own, outer, y)], axis=0))
            phases[-1].append(cells)
    return phases


def put_edges(error, edges):
    half_rows = error.shape[0]
    turned = jnp.concatenate([edges, jnp.zeros((LANES - 16, LANES), jnp.float32)], axis=0).T[0:half_rows]
    lanes, ids = lane_ids(half_rows), row_ids(half_rows)
    error = jnp.where(ids == 0, edges[1:2], jnp.where(ids == half_rows - 1, edges[4:5], error))
    return jnp.where(
        lanes == 0, roll(turned, -9, 1), jnp.where(lanes == LANES - 1, roll(turned, LANES - 13, 1), error)
    )


def minmod(lower_diff, upper_diff):
    smaller, larger = jnp.minimum(lower_diff, upper_diff), jnp.maximum(lower_diff, upper_diff)
    return jnp.maximum(smaller, jnp.minimum(larger, 0.0))


def axis_terms(cells, axis):
    depth, normal, tangent = cells[0], cells[1 + axis], cells[2 - axis]
    inverse_root = lax.rsqrt(depth)
    velocity = normal * (inverse_root * inverse_root)
    along = normal * velocity + 0.5 * depth * depth
    beside = tangent * velocity
    speed = jnp.abs(velocity) + depth * inverse_root
    return (normal, along, beside, speed) if axis == 0 else (normal, beside, along, speed)


def paired_change(near, far, axis):
    down = lambda v: roll(v, 1, axis)
    up = lambda v: roll(v, -1, axis)
    inner = [f - n for n, f in zip(near, far)]
    outer = [n - down(f) for n, f in zip(near, far)]
    near_half = [0.5 * minmod(o, i) for o, i in zip(outer, inner)]
    far_half = [0.5 * minmod(i, up(o)) for o, i in zip(outer, inner)]
    near_hi = [n + s for n, s in zip(near, near_half)]
    near_lo = [n - s for n, s in zip(near, near_half)]
    far_hi = [down(f + s) for f, s in zip(far, far_half)]
    far_lo = [f - s for f, s in zip(far, far_half)]
    terms = lambda cells: axis_terms(cells, axis)
    inner_flux = doubled_flux(near_hi, far_lo, terms(near_hi), terms(far_lo))
    outer_flux = doubled_flux(far_hi, near_lo, terms(far_hi), terms(near_lo))
    near_change = [i - o for i, o in zip(inner_flux, outer_flux)]
    far_change = [up(o) - i for i, o in zip(inner_flux, outer_flux)]
    return near_change, far_change


def doubled_first_step(cells):
    all_terms = cell_terms(*cells)
    changes = []
    for axis in (0, 1):
        terms = all_terms[axis]
        lower = [roll(f, 1, axis) for f in cells]
        lower_terms = [lower[1 + axis] if c == 0 else roll(terms[c], 1, axis) for c in range(4)]
        flux = doubled_flux(lower, cells, lower_terms, terms)
        own = [2.0 * terms[c] for c in range(3)]
        changes.append(
            (
                [o - f for o, f in zip(own, flux)],
                [roll(f, -1, axis) - o for o, f in zip(own, flux)],
            )
        )
    rows, cols = changes
    return [
        [
            [cells[c] - (0.5 * RATIO) * (rows[a][c] + cols[b][c]) for c in range(3)]
            for b in range(2)
        ]
        for a in range(2)
    ]


def patch_rows(cells):
    half = doubled_first_step(cells)
    by_row = [paired_change(half[0][b], half[1][b], 0) for b in range(2)]
    by_col = [paired_change(half[a][0], half[a][1], 1) for a in range(2)]
    size = cells[0].shape[0] - 8
    lanes = lane_ids(size)
    result = []
    for a in range(2):
        fine = [
            [half[a][b][c] - (0.5 * RATIO) * (by_row[b][a][c] + by_col[a][b][c]) for c in range(3)]
            for b in range(2)
        ]
        parts = []
        for c in range(3):
            pick = lanes // 2 + 2
            even = jnp.take_along_axis(fine[0][c][4 : 4 + size], pick, axis=1)
            odd = jnp.take_along_axis(fine[1][c][4 : 4 + size], pick, axis=1)
            parts.append(jnp.where(lanes % 2 == 0, even, odd))
        result.append(parts)
    return result


def sliding(load, start, size):
    group, shift = start // 8, start % 8
    turn = (8 - shift) % 8
    parts = [pltpu.roll(load(group + k), turn, 0) for k in range(size // 8 + 1)]
    keep = row_ids(8, parts[0].shape[1]) < 8 - shift
    return [jnp.where(keep, parts[k], parts[k + 1]) for k in range(size // 8)]


def scalar(values, row, lane):
    return values[row, lane].astype(jnp.int32)


def slab_rows(ref, first, count, size):
    last = SLAB // 8 - 1
    load = lambda k: ref[pl.ds(pl.multiple_of(first + 8 * jnp.minimum(k, last), 8), 8), :]
    return sliding(load, SLAB - count, size)


def column_move(first_cols, last_cols, side, here, right_count):
    lanes = lane_ids(8)
    head = jnp.where(lanes < here, pltpu.roll(side, here, 1), first_cols)
    outer = jnp.where(lanes < right_count, pltpu.roll(last_cols, right_count, 1), side)
    return head, jnp.where(lanes >= LANES // 2, side, outer)


def move_rows(state_ref, rim_ref, slab_ref, wide_ref):
    rows, cols = state_ref.shape[1], state_ref.shape[2]
    counts = rim_ref[0, 0:8, :]
    rc, cc, cc_right = [scalar(counts, 0, k) for k in (OWN_ROWS, OWN_COLS, RIGHT_COLS)]
    for comp in range(3):
        bodies = slab_rows(slab_ref.at[comp], 0, rc, SLAB)
        for k in range(rows // 8):
            part, at = slice(8 * k, 8 * k + 8), slice(8 * k + 8, 8 * k + 16)
            body = state_ref[comp, part, :]
            if 8 * k < SLAB:
                body = jnp.where(row_ids(8, cols) + 8 * k < rc, bodies[k], body)
                wide_ref[comp, at, LANES : LANES + cols] = body
                continue
            head, outer = column_move(
                body[:, 0:LANES], body[:, cols - LANES : cols], rim_ref[comp, part, :], cc, cc_right
            )
            wide_ref[comp, at, 0:LANES] = outer
            wide_ref[comp, at, LANES : 2 * LANES] = head
            wide_ref[comp, at, 2 * LANES : LANES + cols] = body[:, LANES:cols]
            wide_ref[comp, at, LANES + cols : 2 * LANES + cols] = outer


def finish(
    state_ref, rim_ref, slab_ref, rows_ref, within_ref, across_ref, inner_ref, edge_ref, numbers_ref,
    error_out, moved_out, patch_out,
    wide, window, near_rows, columns, corners, above_rim, below, error, patch, sems,
):
    rows, cols = state_ref.shape[1], state_ref.shape[2]
    right = slice(cols, cols + LANES)
    inside_wide = slice(LANES, LANES + cols)
    on_left = lane_ids(8) >= LANES // 2
    copies = [
        pltpu.make_async_copy(rows_ref.at[:, SLAB + 8 : rows + 8, inside_wide], moved_out.at[:, SLAB:rows, :], sems.at[0])
    ]
    copies[-1].start()

    odd = is_odd()
    packed_half = SLAB // 2
    beside = jnp.where(odd, within_ref[DOWN_ROWS - 8 : DOWN_ROWS, :], across_ref[DOWN_ROWS - 8 : DOWN_ROWS, :])
    turned = jnp.concatenate([beside, jnp.zeros((LANES - 8, LANES), jnp.float32)], axis=0).T[rows - SLAB : rows]
    lanes = lane_ids(packed_half)
    tiles = cols // LANES + 1
    for comp in range(3):
        at = slice(comp * packed_half, (comp + 1) * packed_half)
        packed = jnp.where(odd, within_ref[at, :], across_ref[at, :])
        inner = turned if comp == 0 else roll(turned, -2 * comp, 1)
        upper = jnp.where(lanes >= LANES // 2, roll(packed, LANES // 2, 1), inner[0:packed_half])
        lower = jnp.where(lanes >= LANES // 2, packed, inner[packed_half:SLAB])
        above_rim[comp, 0:packed_half, :] = upper
        above_rim[comp, packed_half:SLAB, :] = lower
        for t in range(tiles):
            at = slice(8 * (comp * tiles + t), 8 * (comp * tiles + t) + 8)
            below[comp, :, LANES * t : LANES * (t + 1)] = jnp.where(odd, across_ref[at, :], within_ref[at, :])

    edges = coarse_error(
        edge_phases(state_ref, slab_ref, above_rim, below, edge_ref, near_rows, columns, corners)
    )
    error[...] = put_edges(inner_ref[...], edges)

    own_counts, below_counts, numbers = rim_ref[0, 0:8, :], below[0, :, right], numbers_ref[...]
    cc, rc_left, rc_right, cc_right = [
        scalar(own_counts, 0, k) for k in (OWN_COLS, LEFT_ROWS, RIGHT_ROWS, RIGHT_COLS)
    ]
    cc_above, cc_above_right = [scalar(beside, k, 0) for k in (6, 7)]
    rc_below, cc_below, rc_below_left, rc_below_right, cc_below_right = [
        scalar(below_counts, 0, k) for k in (OWN_ROWS, OWN_COLS, LEFT_ROWS, RIGHT_ROWS, RIGHT_COLS)
    ]
    pos_row, pos_col, ext_row, ext_col = [scalar(numbers, k, 0) for k in range(4)]

    def put(comp, at, body, side, here, right_count):
        tail = body[:, LANES:cols]
        head, outer = column_move(body[:, 0:LANES], tail[:, cols - 2 * LANES :], side, here, right_count)
        wide[comp, at : at + 8, 0:LANES] = outer
        wide[comp, at : at + 8, LANES : 2 * LANES] = head
        wide[comp, at : at + 8, 2 * LANES : LANES + cols] = tail
        wide[comp, at : at + 8, LANES + cols : 2 * LANES + cols] = outer

    def moved_rim(ref, first, left, right_count, size):
        from_left = slab_rows(ref, first, left, size)
        from_right = slab_rows(ref, first, right_count, size)
        return [jnp.where(on_left, a, b) for a, b in zip(from_left, from_right)]

    for comp in range(3):
        sides = moved_rim(above_rim.at[comp], 0, rc_left, rc_right, SLAB)
        for k in range(SLAB // 8):
            side = rim_ref[comp, 8 * k : 8 * k + 8, :]
            side = jnp.where(row_ids(8) + 8 * k < jnp.where(on_left, rc_left, rc_right), sides[k], side)
            put(comp, 8 * k + 8, rows_ref[comp, 8 * k + 8 : 8 * k + 16, inside_wide], side, cc, cc_right)
        wide[comp, SLAB + 8 : rows + 8, :] = rows_ref[comp, SLAB + 8 : rows + 8, :]
        put(comp, 0, slab_ref[comp, SLAB - 8 : SLAB, :], above_rim[comp, SLAB - 8 : SLAB, :], cc_above, cc_above_right)
        (body,) = slab_rows(state_ref.at[comp], rows - SLAB, rc_below, 8)
        (side,) = moved_rim(rim_ref.at[comp], rows - SLAB, rc_below_left, rc_below_right, 8)
        body = jnp.where(row_ids(8, cols) < rc_below, body, below[comp, :, 0:cols])
        side = jnp.where(
            row_ids(8) < jnp.where(on_left, rc_below_left, rc_below_right), side, below[comp, :, right]
        )
        put(comp, rows + 8, body, side, cc_below, cc_below_right)
    copies += [
        pltpu.make_async_copy(wide.at[:, 8 : SLAB + 8, inside_wide], moved_out.at[:, 0:SLAB, :], sems.at[1]),
        pltpu.make_async_copy(error, error_out, sems.at[2]),
    ]

    first_lane = pos_col + LANES - 2
    tile, shift = first_lane // LANES, first_lane % LANES
    turn = (LANES - shift) % LANES
    keep = lane_ids(8) < LANES - shift
    for comp in range(3):

        def load(k):
            group = pl.ds(pl.multiple_of(8 * k, 8), 8)
            near = wide[comp, group, pl.ds(pl.multiple_of(LANES * tile, LANES), LANES)]
            far = wide[comp, group, pl.ds(pl.multiple_of(LANES * tile + LANES, LANES), LANES)]
            return jnp.where(keep, pltpu.roll(near, turn, 1), pltpu.roll(far, turn, 1))

        for k, part in enumerate(sliding(load, pos_row + 4, 72)):
            window[comp, 8 * k : 8 * k + 8, :] = part

    fine_rows, fine_cols = 2 * ext_row, 2 * ext_col
    size = PATCH_ROWS
    for start in range(0, PATCH, size):
        cells = [window[c, start : start + size + 8, :] for c in range(3)]
        fine = patch_rows(cells)
        lanes, ids = lane_ids(size), row_ids(size)
        for a in range(2):
            inside = (2 * (ids + start) + a < fine_rows) & (lanes < fine_cols)
            for c in range(3):
                patch[c, pl.ds(2 * start + a, size, stride=2), :] = jnp.where(inside, fine[a][c], 0.0)
        part = pl.ds(2 * start, 2 * size)
        copies.append(
            pltpu.make_async_copy(patch.at[:, part, :], patch_out.at[:, part, :], sems.at[3 + start // size])
        )
        copies[-1].start()
    for copy in copies[1:3]:
        copy.start()
    for copy in copies:
        copy.wait()


def around(axis, by):
    devices = lax.axis_size(axis)
    return [(i, (i + by) % devices) for i in range(devices)]


def in_vmem(value):
    return pltpu.with_memory_space_constraint(value, pltpu.VMEM)


def in_hbm(value):
    return pltpu.with_memory_space_constraint(value, pltpu.HBM)


def vmem(*shape):
    return pltpu.VMEM(shape, jnp.float32)


def per_device(state, row_count, col_count, patch_pos, patch_ext):
    rows, cols = state.shape[1], state.shape[2]
    width = cols + LANES
    half = rows // 2
    here = in_vmem(state)
    to_right, strip, slab = pl.pallas_call(
        pack_cols,
        out_shape=(vmem(3 * half + 8, LANES), vmem(32, LANES), vmem(3, SLAB, cols)),
        in_specs=[SMEM, VMEM],
        out_specs=(VMEM,) * 3,
        name="pack_cols",
    )(row_count, here)
    strip = in_vmem(strip)
    to_left, counts = pl.pallas_call(
        pack_right, out_shape=(vmem(8, LANES), vmem(8, LANES)), in_specs=[SMEM, VMEM], out_specs=(VMEM,) * 2, name="pack_right"
    )(col_count, strip)
    from_left = in_vmem(lax.ppermute(to_right, "col", around("col", 1)))
    from_right = in_vmem(lax.ppermute(to_left, "col", around("col", -1)))
    slab_above = in_vmem(lax.ppermute(slab, "row", around("row", 1)))
    inner, numbers = pl.pallas_call(
        inner_error,
        out_shape=(vmem(half, cols // 2), vmem(8, LANES)),
        in_specs=[ANY, ANY, VMEM],
        out_specs=(VMEM,) * 2,
        scratch_shapes=[
            vmem(3, 2, rows, LANES),
            pltpu.VMEM(patch_pos.shape, jnp.int32),
            pltpu.VMEM(patch_ext.shape, jnp.int32),
            pltpu.SemaphoreType.DMA((2,)),
        ],
        cost_estimate=pl.CostEstimate(flops=30_000_000, bytes_accessed=600_000, transcendentals=0),
        name="inner_error",
    )(in_hbm(patch_pos), in_hbm(patch_ext), here)
    inner = in_vmem(inner)
    rim, within, across, edge = pl.pallas_call(
        pack_rows,
        out_shape=(vmem(3, rows, LANES), vmem(DOWN_ROWS, LANES), vmem(DOWN_ROWS + 8, LANES), vmem(3, 16, LANES)),
        in_specs=[VMEM] * 6,
        out_specs=(VMEM,) * 4,
        name="pack_rows",
    )(in_vmem(counts), strip, from_left, from_right, here, inner)
    rim = in_vmem(rim)
    devices = lax.axis_size("row")
    from_within = in_vmem(lax.ppermute(within, "row", [(i, i ^ 1) for i in range(devices)]))
    from_across = in_vmem(
        lax.ppermute(across, "row", [(i, (i + (1 if i % 2 else -1)) % devices) for i in range(devices)])
    )
    moved_rows = in_vmem(pl.pallas_call(
        move_rows,
        out_shape=vmem(3, rows + 16, width + LANES),
        in_specs=[VMEM] * 3,
        out_specs=VMEM,
        cost_estimate=pl.CostEstimate(flops=3_000_000, bytes_accessed=1_000_000, transcendentals=0),
        name="move_rows",
    )(here, rim, slab_above))
    return pl.pallas_call(
        finish,
        out_shape=(f32(half, cols // 2), f32(3, rows, cols), f32(3, 2 * PATCH, 2 * PATCH)),
        in_specs=[VMEM] * 9,
        out_specs=(ANY,) * 3,
        scratch_shapes=[
            vmem(3, rows + 16, width + LANES),
            vmem(3, 72, LANES),
            vmem(3, 16, cols),
            vmem(3, 2, 16, LANES),
            vmem(3, 16, LANES),
            vmem(3, SLAB, LANES),
            vmem(3, 8, width),
            vmem(half, cols // 2),
            vmem(3, 2 * PATCH, 2 * PATCH),
            pltpu.SemaphoreType.DMA((3 + PATCH // PATCH_ROWS,)),
        ],
        compiler_params=PARAMS,
        name="finish",
    )(here, rim, slab_above, moved_rows, from_within, from_across, inner, edge, numbers)


def solution(mesh):
    placed = (
        P(None, "row", "col"),
        P("row", "col"),
        P("row", "col"),
        P("row", "col", None),
        P("row", "col", None),
    )
    return jax.shard_map(
        per_device,
        mesh=mesh,
        in_specs=placed,
        out_specs=(P("row", "col"), P(None, "row", "col"), P(None, "row", "col")),
        check_vma=False,
    )
```

```python
import jax
import jax.numpy as jnp
from jax import lax
from jax.experimental import pallas as pl
from jax.experimental.pallas import tpu as pltpu
from jax.sharding import PartitionSpec as P

SLAB = 64
PATCH = 64
LANES = 128
PATCH_ROWS = 64
UPPER = 32

RATIO = 0.1
ERR_SCALE = 10.0

RIGHT_ROWS, RIGHT_COLS, LEFT_ROWS, OWN_ROWS, OWN_COLS = 6, 7, 8, 10, 11
DOWN_ROWS = 3 * SLAB // 2 + 8

VMEM = pl.BlockSpec(memory_space=pltpu.VMEM)
SMEM = pl.BlockSpec(memory_space=pltpu.SMEM)
ANY = pl.BlockSpec(memory_space=pl.ANY)
PARAMS = pltpu.CompilerParams(vmem_limit_bytes=32 * 1024 * 1024)


def f32(*shape):
    return jax.ShapeDtypeStruct(shape, jnp.float32)


def lane_ids(rows, width=LANES):
    return lax.broadcasted_iota(jnp.int32, (rows, width), 1)


def row_ids(rows, width=LANES):
    return lax.broadcasted_iota(jnp.int32, (rows, width), 0)


def roll(value, by, axis):
    return pltpu.roll(value, by % value.shape[axis], axis)


def cell_terms(depth, first, second):
    inverse_root = lax.rsqrt(depth)
    wave = depth * inverse_root
    inverse = inverse_root * inverse_root
    first_vel = first * inverse
    second_vel = second * inverse
    pressure = 0.5 * depth * depth
    cross = first * second_vel
    row_terms = (first, first * first_vel + pressure, cross, jnp.abs(first_vel) + wave)
    col_terms = (second, cross, second * second_vel + pressure, jnp.abs(second_vel) + wave)
    return row_terms, col_terms


def doubled_flux(left, right, left_terms, right_terms):
    speed = jnp.maximum(left_terms[3], right_terms[3])
    return [(left_terms[c] + right_terms[c]) - speed * (right[c] - left[c]) for c in range(3)]


def spread_step(fields, row_by, col_by):
    row_terms, col_terms = cell_terms(*fields)
    total = None
    for terms, by, axis in ((row_terms, row_by, 0), (col_terms, col_by, 1)):
        lower = [roll(f, by, axis) for f in fields]
        momentum = lower[1 + axis]
        lower_terms = [momentum if c == 0 else roll(terms[c], by, axis) for c in range(4)]
        flux = doubled_flux(lower, fields, lower_terms, terms)
        change = [roll(f, -by, axis) - f for f in flux]
        total = change if total is None else [t + c for t, c in zip(total, change)]
    return [f - (0.5 * RATIO) * t for f, t in zip(fields, total)]


def pair_change(near, far, near_terms, far_terms, axis):
    inner = doubled_flux(near, far, near_terms, far_terms)
    before = [roll(f, 1, axis) for f in far]
    before_terms = [before[1 + axis] if c == 0 else roll(far_terms[c], 1, axis) for c in range(4)]
    outer = doubled_flux(before, near, before_terms, near_terms)
    near_change = [i - o for i, o in zip(inner, outer)]
    far_change = [roll(o, -1, axis) - i for i, o in zip(inner, outer)]
    return near_change, far_change


def paired_step(phases):
    terms = [[cell_terms(*phases[x][y]) for y in range(2)] for x in range(2)]
    along_first = [
        pair_change(phases[0][y], phases[1][y], terms[0][y][0], terms[1][y][0], 0) for y in range(2)
    ]
    along_second = [
        pair_change(phases[x][0], phases[x][1], terms[x][0][1], terms[x][1][1], 1) for x in range(2)
    ]
    return [
        [
            [
                phases[x][y][c] - (0.5 * RATIO) * (along_first[y][x][c] + along_second[x][y][c])
                for c in range(3)
            ]
            for y in range(2)
        ]
        for x in range(2)
    ]


def block_mean(phases):
    return [
        0.25 * ((phases[0][0][c] + phases[1][0][c]) + (phases[0][1][c] + phases[1][1][c])) for c in range(3)
    ]


def coarse_error(phases):
    fine = block_mean(paired_step(paired_step(phases)))
    coarse = spread_step(block_mean(phases), 1, 1)
    parts = [jnp.abs(f - c) for f, c in zip(fine, coarse)]
    return ERR_SCALE * ((parts[0] + parts[1]) + parts[2])


def every_other(first, second, parity):
    lanes = lane_ids(first.shape[0])
    pick = (2 * lanes + parity) % LANES
    low = jnp.take_along_axis(first, pick, axis=1)
    high = jnp.take_along_axis(second, pick, axis=1)
    return jnp.where(lanes < LANES // 2, low, high)


def blank(out_ref):
    out_ref[...] = jnp.zeros(out_ref.shape, jnp.float32)


def pack_cols(row_count, blank_ref, state_ref, left_ref, strip_ref, slab_ref):
    rows, cols = state_ref.shape[1], state_ref.shape[2]
    half = rows // 2
    rc = row_count[0, 0].astype(jnp.float32)
    lanes = lane_ids(half)
    for comp in range(3):
        upper = state_ref[comp, 0:half, cols - LANES : cols]
        lower = roll(state_ref[comp, half:rows, cols - LANES : cols], LANES // 2, 1)
        left_ref[comp * half : (comp + 1) * half, :] = jnp.where(lanes >= LANES // 2, upper, lower)
    lanes = lane_ids(rows)
    packed = None
    for comp in range(3):
        ends = jnp.where(lanes < LANES // 2, state_ref[comp, :, 0:LANES], state_ref[comp, :, cols - LANES : cols])
        ends = roll(ends, 8 * comp + 4, 1)
        packed = ends if packed is None else jnp.where(lanes >= 8 * comp, ends, packed)
    strip_ref[0:24, :] = packed.T[0:24]
    strip_ref[24:32, :] = jnp.full((8, LANES), rc)
    left_ref[3 * half : 3 * half + 8, :] = jnp.full((8, LANES), rc)
    for comp in range(3):
        left_ref[3 * half + 2 * comp : 3 * half + 2 * comp + 2, :] = strip_ref[8 * comp + 2 : 8 * comp + 4, :]
    slab_ref[...] = state_ref[:, rows - SLAB : rows, :]


def pack_right(col_count, strip_ref, right_ref, counts_ref):
    cc = col_count[0, 0].astype(jnp.float32)
    counts = jnp.where(row_ids(8) == 6, strip_ref[24:32, :], cc)
    counts_ref[...] = counts
    right_ref[...] = counts
    for comp in range(3):
        right_ref[2 * comp : 2 * comp + 2, :] = strip_ref[8 * comp + 4 : 8 * comp + 6, :]


def is_odd():
    return lax.axis_index("row") % 2 == 1


def pack_rows(counts_ref, strip_ref, left_ref, right_ref, state_ref, upper_ref, rim_ref, within_ref, across_ref, edge_ref):
    rows, cols = state_ref.shape[1], state_ref.shape[2]
    half = rows // 2
    rc, cc = counts_ref[6:7, :], counts_ref[7:8, :]
    right = jnp.concatenate([right_ref[...], jnp.zeros((LANES - 8, LANES), jnp.float32)], axis=0).T
    lanes = lane_ids(rows)
    left_rc = left_ref[3 * half + 6 : 3 * half + 7, :]
    counts = jnp.where(lanes == LEFT_ROWS, left_rc, jnp.where(lanes == OWN_ROWS, rc, cc))
    odd = is_odd()
    packed_half = SLAB // 2
    low = lane_ids(packed_half) < LANES // 2

    def put(at, down, up):
        size = down.shape[0]
        within_ref[at : at + size, :] = jnp.where(odd, up, down)
        across_ref[at : at + size, :] = jnp.where(odd, down, up)

    ups, downs = [], []
    for comp in range(3):
        packed = left_ref[comp * half : (comp + 1) * half, :]
        left = jnp.concatenate([packed, roll(packed, LANES // 2, 1)], axis=0)
        inner = right if comp == 0 else roll(right, -2 * comp, 1)
        inner = jnp.where(lanes < LEFT_ROWS, inner, counts)
        rim = jnp.where(lanes >= LANES // 2, left, inner)
        rim_ref[comp] = rim
        last = packed[half - SLAB : half]
        downs.append(jnp.where(low, last[0:packed_half], roll(last[packed_half:SLAB], LANES // 2, 1)))
        ups += [state_ref[comp, 0:8, LANES * t : LANES * (t + 1)] for t in range(cols // LANES)] + [rim[0:8]]
        edge_ref[comp, 0:2, :] = left_ref[3 * half + 2 * comp : 3 * half + 2 * comp + 2, :]
        edge_ref[comp, 2:6, :] = strip_ref[8 * comp + 4 : 8 * comp + 8, :]
        edge_ref[comp, 6:10, :] = strip_ref[8 * comp : 8 * comp + 4, :]
        edge_ref[comp, 10:12, :] = right_ref[2 * comp : 2 * comp + 2, :]
        edge_ref[comp, 12:16, :] = strip_ref[8 * comp + 4 : 8 * comp + 8, :]
    downs.append(jnp.where(row_ids(8) == 6, cc, right_ref[...]))
    down = jnp.concatenate(downs, axis=0)
    up = jnp.concatenate(ups, axis=0)
    size = up.shape[0]
    put(0, down[0:size], up)
    put(size, down[size:DOWN_ROWS], down[size:DOWN_ROWS])
    across_ref[DOWN_ROWS : DOWN_ROWS + 8, :] = jnp.zeros((8, LANES), jnp.float32)


def inner_error(state_ref, first, size, columns):
    part = slice(2 * first, 2 * (first + size))
    for comp in range(3):
        left, right = state_ref[comp, part, 0:LANES], state_ref[comp, part, LANES : 2 * LANES]
        for parity in range(2):
            columns[comp, parity] = every_other(left, right, parity)
    phases = [
        [[columns[c, y, pl.ds(x, size, stride=2), :] for c in range(3)] for y in range(2)]
        for x in range(2)
    ]
    return coarse_error(phases)


def upper_error(state_ref, error_ref, columns):
    rows = error_ref.shape[0]
    error_ref[...] = inner_error(state_ref, 0, rows + 8, columns)[0:rows]


def lower_error(pos_ref, ext_ref, state_ref, rim_ref, error_ref, numbers_ref, columns, pos, ext, sems):
    copies = [pltpu.make_async_copy(src, dst, sems.at[k]) for k, (src, dst) in enumerate(((pos_ref, pos), (ext_ref, ext)))]
    for copy in copies:
        copy.start()
    rows = error_ref.shape[0]
    error_ref[...] = inner_error(state_ref, state_ref.shape[1] // 2 - rows - 8, rows + 8, columns)[8 : rows + 8]
    for copy in copies:
        copy.wait()
    pair = [v[0].astype(jnp.float32) for v in (pos, ext)]
    numbers = jnp.broadcast_to(pair[1][:, 1:2], (8, LANES))
    for k, number in enumerate((pair[0][:, 0:1], pair[0][:, 1:2], pair[1][:, 0:1])):
        numbers = jnp.where(row_ids(8) == k, number, numbers)
    numbers_ref[...] = numbers


def edge_phases(state_ref, slab_ref, above_rim, below, edge_ref, near_rows, columns, corners_ref):
    rows, cols = state_ref.shape[1], state_ref.shape[2]
    right = slice(cols, cols + LANES)
    lanes = lane_ids(8)
    packed_up, packed_down = None, None
    for comp in range(3):
        near_rows[comp, 0:2, :] = slab_ref[comp, SLAB - 2 : SLAB, :]
        near_rows[comp, 2:6, :] = state_ref[comp, 0:4, :]
        near_rows[comp, 6:10, :] = state_ref[comp, rows - 4 : rows, :]
        near_rows[comp, 10:12, :] = below[comp, 0:2, 0:cols]
        near_rows[comp, 12:16, :] = state_ref[comp, 0:4, :]
        first, second = near_rows[comp, :, 0:LANES], near_rows[comp, :, LANES : 2 * LANES]
        for parity in range(2):
            columns[comp, parity] = every_other(first, second, parity)

        def around_corner(body, rim):
            start = jnp.where(lanes < LANES // 2, body[:, 0:LANES], rim)
            end = jnp.where(lanes < LANES // 2, rim, body[:, cols - LANES : cols])
            first_six = (lanes >= 12 * comp) & (lanes < 12 * comp + 6)
            return jnp.where(first_six, roll(start, 12 * comp + 2, 1), roll(end, 12 * comp + 10, 1))

        up = around_corner(slab_ref[comp, SLAB - 8 : SLAB, :], above_rim[comp, SLAB - 8 : SLAB, :])
        down = around_corner(below[comp, :, 0:cols], below[comp, :, right])
        packed_up = up if comp == 0 else jnp.where(lanes >= 12 * comp, up, packed_up)
        packed_down = down if comp == 0 else jnp.where(lanes >= 12 * comp, down, packed_down)
    corners = jnp.concatenate([packed_down, jnp.ones((LANES - 16, LANES), jnp.float32), packed_up], axis=0).T
    for comp in range(3):
        corners_ref[comp, 0:12, :] = corners[12 * comp : 12 * comp + 12, :]
        corners_ref[comp, 12:16, :] = edge_ref[comp, 12:16, :]
    phases = []
    for x in range(2):
        phases.append([])
        for y in range(2):
            cells = []
            for comp, turned in ((0, 0), (1, 2), (2, 1)):
                by_row = columns[comp, y, pl.ds(x, 8, stride=2), :]
                own, outer = [ref[turned, pl.ds(x, 8, stride=2), :] for ref in (edge_ref, corners_ref)]
                cells.append(jnp.concatenate([by_row, every_other(own, outer, y)], axis=0))
            phases[-1].append(cells)
    return phases


def put_edges(error, edges):
    half_rows = error.shape[0]
    turned = jnp.concatenate([edges, jnp.zeros((LANES - 16, LANES), jnp.float32)], axis=0).T[0:half_rows]
    lanes, ids = lane_ids(half_rows), row_ids(half_rows)
    error = jnp.where(ids == 0, edges[1:2], jnp.where(ids == half_rows - 1, edges[4:5], error))
    return jnp.where(
        lanes == 0, roll(turned, -9, 1), jnp.where(lanes == LANES - 1, roll(turned, LANES - 13, 1), error)
    )


def minmod(lower_diff, upper_diff):
    smaller, larger = jnp.minimum(lower_diff, upper_diff), jnp.maximum(lower_diff, upper_diff)
    return jnp.maximum(smaller, jnp.minimum(larger, 0.0))


def axis_terms(cells, axis):
    depth, normal, tangent = cells[0], cells[1 + axis], cells[2 - axis]
    inverse_root = lax.rsqrt(depth)
    velocity = normal * (inverse_root * inverse_root)
    along = normal * velocity + 0.5 * depth * depth
    beside = tangent * velocity
    speed = jnp.abs(velocity) + depth * inverse_root
    return (normal, along, beside, speed) if axis == 0 else (normal, beside, along, speed)


def paired_change(near, far, axis):
    down = lambda v: roll(v, 1, axis)
    up = lambda v: roll(v, -1, axis)
    inner = [f - n for n, f in zip(near, far)]
    outer = [n - down(f) for n, f in zip(near, far)]
    near_half = [0.5 * minmod(o, i) for o, i in zip(outer, inner)]
    far_half = [0.5 * minmod(i, up(o)) for o, i in zip(outer, inner)]
    near_hi = [n + s for n, s in zip(near, near_half)]
    near_lo = [n - s for n, s in zip(near, near_half)]
    far_hi = [down(f + s) for f, s in zip(far, far_half)]
    far_lo = [f - s for f, s in zip(far, far_half)]
    terms = lambda cells: axis_terms(cells, axis)
    inner_flux = doubled_flux(near_hi, far_lo, terms(near_hi), terms(far_lo))
    outer_flux = doubled_flux(far_hi, near_lo, terms(far_hi), terms(near_lo))
    near_change = [i - o for i, o in zip(inner_flux, outer_flux)]
    far_change = [up(o) - i for i, o in zip(inner_flux, outer_flux)]
    return near_change, far_change


def doubled_first_step(cells):
    all_terms = cell_terms(*cells)
    changes = []
    for axis in (0, 1):
        terms = all_terms[axis]
        lower = [roll(f, 1, axis) for f in cells]
        lower_terms = [lower[1 + axis] if c == 0 else roll(terms[c], 1, axis) for c in range(4)]
        flux = doubled_flux(lower, cells, lower_terms, terms)
        own = [2.0 * terms[c] for c in range(3)]
        changes.append(
            (
                [o - f for o, f in zip(own, flux)],
                [roll(f, -1, axis) - o for o, f in zip(own, flux)],
            )
        )
    rows, cols = changes
    return [
        [
            [cells[c] - (0.5 * RATIO) * (rows[a][c] + cols[b][c]) for c in range(3)]
            for b in range(2)
        ]
        for a in range(2)
    ]


def patch_rows(cells):
    half = doubled_first_step(cells)
    by_row = [paired_change(half[0][b], half[1][b], 0) for b in range(2)]
    by_col = [paired_change(half[a][0], half[a][1], 1) for a in range(2)]
    size = cells[0].shape[0] - 8
    lanes = lane_ids(size)
    result = []
    for a in range(2):
        fine = [
            [half[a][b][c] - (0.5 * RATIO) * (by_row[b][a][c] + by_col[a][b][c]) for c in range(3)]
            for b in range(2)
        ]
        parts = []
        for c in range(3):
            pick = lanes // 2 + 2
            even = jnp.take_along_axis(fine[0][c][4 : 4 + size], pick, axis=1)
            odd = jnp.take_along_axis(fine[1][c][4 : 4 + size], pick, axis=1)
            parts.append(jnp.where(lanes % 2 == 0, even, odd))
        result.append(parts)
    return result


def sliding(load, start, size):
    group, shift = start // 8, start % 8
    turn = (8 - shift) % 8
    parts = [pltpu.roll(load(group + k), turn, 0) for k in range(size // 8 + 1)]
    keep = row_ids(8, parts[0].shape[1]) < 8 - shift
    return [jnp.where(keep, parts[k], parts[k + 1]) for k in range(size // 8)]


def scalar(values, row, lane):
    return values[row, lane].astype(jnp.int32)


def slab_rows(ref, first, count, size):
    last = SLAB // 8 - 1
    load = lambda k: ref[pl.ds(pl.multiple_of(first + 8 * jnp.minimum(k, last), 8), 8), :]
    return sliding(load, SLAB - count, size)


def column_move(first_cols, last_cols, side, here, right_count):
    lanes = lane_ids(8)
    head = jnp.where(lanes < here, pltpu.roll(side, here, 1), first_cols)
    outer = jnp.where(lanes < right_count, pltpu.roll(last_cols, right_count, 1), side)
    return head, jnp.where(lanes >= LANES // 2, side, outer)


def move_rows(state_ref, rim_ref, slab_ref, wide_ref):
    rows, cols = state_ref.shape[1], state_ref.shape[2]
    counts = rim_ref[0, 0:8, :]
    rc, cc, cc_right = [scalar(counts, 0, k) for k in (OWN_ROWS, OWN_COLS, RIGHT_COLS)]
    for comp in range(3):
        bodies = slab_rows(slab_ref.at[comp], 0, rc, SLAB)
        for k in range(rows // 8):
            part, at = slice(8 * k, 8 * k + 8), slice(8 * k + 8, 8 * k + 16)
            body = state_ref[comp, part, :]
            if 8 * k < SLAB:
                body = jnp.where(row_ids(8, cols) + 8 * k < rc, bodies[k], body)
                wide_ref[comp, at, LANES : LANES + cols] = body
                continue
            head, outer = column_move(
                body[:, 0:LANES], body[:, cols - LANES : cols], rim_ref[comp, part, :], cc, cc_right
            )
            wide_ref[comp, at, 0:LANES] = outer
            wide_ref[comp, at, LANES : 2 * LANES] = head
            wide_ref[comp, at, 2 * LANES : LANES + cols] = body[:, LANES:cols]
            wide_ref[comp, at, LANES + cols : 2 * LANES + cols] = outer


def finish(
    state_ref, rim_ref, slab_ref, rows_ref, within_ref, across_ref, upper_ref, lower_ref, edge_ref, numbers_ref,
    error_out, moved_out, patch_out,
    wide, window, near_rows, columns, corners, above_rim, below, error, patch, sems,
):
    rows, cols = state_ref.shape[1], state_ref.shape[2]
    right = slice(cols, cols + LANES)
    inside_wide = slice(LANES, LANES + cols)
    on_left = lane_ids(8) >= LANES // 2
    copies = [
        pltpu.make_async_copy(rows_ref.at[:, SLAB + 8 : rows + 8, inside_wide], moved_out.at[:, SLAB:rows, :], sems.at[0])
    ]
    copies[-1].start()

    odd = is_odd()
    packed_half = SLAB // 2
    beside = jnp.where(odd, within_ref[DOWN_ROWS - 8 : DOWN_ROWS, :], across_ref[DOWN_ROWS - 8 : DOWN_ROWS, :])
    turned = jnp.concatenate([beside, jnp.zeros((LANES - 8, LANES), jnp.float32)], axis=0).T[rows - SLAB : rows]
    lanes = lane_ids(packed_half)
    tiles = cols // LANES + 1
    for comp in range(3):
        at = slice(comp * packed_half, (comp + 1) * packed_half)
        packed = jnp.where(odd, within_ref[at, :], across_ref[at, :])
        inner = turned if comp == 0 else roll(turned, -2 * comp, 1)
        upper = jnp.where(lanes >= LANES // 2, roll(packed, LANES // 2, 1), inner[0:packed_half])
        lower = jnp.where(lanes >= LANES // 2, packed, inner[packed_half:SLAB])
        above_rim[comp, 0:packed_half, :] = upper
        above_rim[comp, packed_half:SLAB, :] = lower
        for t in range(tiles):
            at = slice(8 * (comp * tiles + t), 8 * (comp * tiles + t) + 8)
            below[comp, :, LANES * t : LANES * (t + 1)] = jnp.where(odd, across_ref[at, :], within_ref[at, :])

    edges = coarse_error(
        edge_phases(state_ref, slab_ref, above_rim, below, edge_ref, near_rows, columns, corners)
    )
    error[...] = put_edges(jnp.concatenate([upper_ref[...], lower_ref[...]], axis=0), edges)

    own_counts, below_counts, numbers = rim_ref[0, 0:8, :], below[0, :, right], numbers_ref[...]
    cc, rc_left, rc_right, cc_right = [
        scalar(own_counts, 0, k) for k in (OWN_COLS, LEFT_ROWS, RIGHT_ROWS, RIGHT_COLS)
    ]
    cc_above, cc_above_right = [scalar(beside, k, 0) for k in (6, 7)]
    rc_below, cc_below, rc_below_left, rc_below_right, cc_below_right = [
        scalar(below_counts, 0, k) for k in (OWN_ROWS, OWN_COLS, LEFT_ROWS, RIGHT_ROWS, RIGHT_COLS)
    ]
    pos_row, pos_col, ext_row, ext_col = [scalar(numbers, k, 0) for k in range(4)]

    def put(comp, at, body, side, here, right_count):
        tail = body[:, LANES:cols]
        head, outer = column_move(body[:, 0:LANES], tail[:, cols - 2 * LANES :], side, here, right_count)
        wide[comp, at : at + 8, 0:LANES] = outer
        wide[comp, at : at + 8, LANES : 2 * LANES] = head
        wide[comp, at : at + 8, 2 * LANES : LANES + cols] = tail
        wide[comp, at : at + 8, LANES + cols : 2 * LANES + cols] = outer

    def moved_rim(ref, first, left, right_count, size):
        from_left = slab_rows(ref, first, left, size)
        from_right = slab_rows(ref, first, right_count, size)
        return [jnp.where(on_left, a, b) for a, b in zip(from_left, from_right)]

    for comp in range(3):
        sides = moved_rim(above_rim.at[comp], 0, rc_left, rc_right, SLAB)
        for k in range(SLAB // 8):
            side = rim_ref[comp, 8 * k : 8 * k + 8, :]
            side = jnp.where(row_ids(8) + 8 * k < jnp.where(on_left, rc_left, rc_right), sides[k], side)
            put(comp, 8 * k + 8, rows_ref[comp, 8 * k + 8 : 8 * k + 16, inside_wide], side, cc, cc_right)
        wide[comp, SLAB + 8 : rows + 8, :] = rows_ref[comp, SLAB + 8 : rows + 8, :]
        put(comp, 0, slab_ref[comp, SLAB - 8 : SLAB, :], above_rim[comp, SLAB - 8 : SLAB, :], cc_above, cc_above_right)
        (body,) = slab_rows(state_ref.at[comp], rows - SLAB, rc_below, 8)
        (side,) = moved_rim(rim_ref.at[comp], rows - SLAB, rc_below_left, rc_below_right, 8)
        body = jnp.where(row_ids(8, cols) < rc_below, body, below[comp, :, 0:cols])
        side = jnp.where(
            row_ids(8) < jnp.where(on_left, rc_below_left, rc_below_right), side, below[comp, :, right]
        )
        put(comp, rows + 8, body, side, cc_below, cc_below_right)
    copies += [
        pltpu.make_async_copy(wide.at[:, 8 : SLAB + 8, inside_wide], moved_out.at[:, 0:SLAB, :], sems.at[1]),
        pltpu.make_async_copy(error, error_out, sems.at[2]),
    ]

    first_lane = pos_col + LANES - 2
    tile, shift = first_lane // LANES, first_lane % LANES
    turn = (LANES - shift) % LANES
    keep = lane_ids(8) < LANES - shift
    for comp in range(3):

        def load(k):
            group = pl.ds(pl.multiple_of(8 * k, 8), 8)
            near = wide[comp, group, pl.ds(pl.multiple_of(LANES * tile, LANES), LANES)]
            far = wide[comp, group, pl.ds(pl.multiple_of(LANES * tile + LANES, LANES), LANES)]
            return jnp.where(keep, pltpu.roll(near, turn, 1), pltpu.roll(far, turn, 1))

        for k, part in enumerate(sliding(load, pos_row + 4, 72)):
            window[comp, 8 * k : 8 * k + 8, :] = part

    fine_rows, fine_cols = 2 * ext_row, 2 * ext_col
    size = PATCH_ROWS
    for start in range(0, PATCH, size):
        cells = [window[c, start : start + size + 8, :] for c in range(3)]
        fine = patch_rows(cells)
        lanes, ids = lane_ids(size), row_ids(size)
        for a in range(2):
            inside = (2 * (ids + start) + a < fine_rows) & (lanes < fine_cols)
            for c in range(3):
                patch[c, pl.ds(2 * start + a, size, stride=2), :] = jnp.where(inside, fine[a][c], 0.0)
        part = pl.ds(2 * start, 2 * size)
        copies.append(
            pltpu.make_async_copy(patch.at[:, part, :], patch_out.at[:, part, :], sems.at[3 + start // size])
        )
        copies[-1].start()
    for copy in copies[1:3]:
        copy.start()
    for copy in copies:
        copy.wait()


def around(axis, by):
    devices = lax.axis_size(axis)
    return [(i, (i + by) % devices) for i in range(devices)]


def in_vmem(value):
    return pltpu.with_memory_space_constraint(value, pltpu.VMEM)


def in_hbm(value):
    return pltpu.with_memory_space_constraint(value, pltpu.HBM)


def vmem(*shape):
    return pltpu.VMEM(shape, jnp.float32)


def per_device(state, row_count, col_count, patch_pos, patch_ext):
    rows, cols = state.shape[1], state.shape[2]
    width = cols + LANES
    half = rows // 2
    here = in_vmem(state)
    ahead = pl.pallas_call(
        blank,
        out_shape=vmem(8, LANES),
        out_specs=VMEM,
        cost_estimate=pl.CostEstimate(flops=10_000_000_000, bytes_accessed=10_000_000, transcendentals=0),
        name="ahead",
    )()
    to_right, strip, slab = pl.pallas_call(
        pack_cols,
        out_shape=(vmem(3 * half + 8, LANES), vmem(32, LANES), vmem(3, SLAB, cols)),
        in_specs=[SMEM, VMEM, VMEM],
        out_specs=(VMEM,) * 3,
        name="pack_cols",
    )(row_count, in_vmem(ahead), here)
    strip = in_vmem(strip)
    to_left, counts = pl.pallas_call(
        pack_right, out_shape=(vmem(8, LANES), vmem(8, LANES)), in_specs=[SMEM, VMEM], out_specs=(VMEM,) * 2, name="pack_right"
    )(col_count, strip)
    from_left = in_vmem(lax.ppermute(to_right, "col", around("col", 1)))
    from_right = in_vmem(lax.ppermute(to_left, "col", around("col", -1)))
    slab_above = in_vmem(lax.ppermute(slab, "row", around("row", 1)))
    upper = in_vmem(pl.pallas_call(
        upper_error,
        out_shape=vmem(UPPER, cols // 2),
        in_specs=[VMEM],
        out_specs=VMEM,
        scratch_shapes=[vmem(3, 2, 2 * UPPER + 16, LANES)],
        cost_estimate=pl.CostEstimate(flops=15_000_000, bytes_accessed=300_000, transcendentals=0),
        name="upper_error",
    )(here))
    rim, within, across, edge = pl.pallas_call(
        pack_rows,
        out_shape=(vmem(3, rows, LANES), vmem(DOWN_ROWS, LANES), vmem(DOWN_ROWS + 8, LANES), vmem(3, 16, LANES)),
        in_specs=[VMEM] * 6,
        out_specs=(VMEM,) * 4,
        name="pack_rows",
    )(in_vmem(counts), strip, from_left, from_right, here, upper)
    rim = in_vmem(rim)
    lower, numbers = pl.pallas_call(
        lower_error,
        out_shape=(vmem(half - UPPER, cols // 2), vmem(8, LANES)),
        in_specs=[ANY, ANY, VMEM, VMEM],
        out_specs=(VMEM,) * 2,
        scratch_shapes=[
            vmem(3, 2, 2 * (half - UPPER) + 16, LANES),
            pltpu.VMEM(patch_pos.shape, jnp.int32),
            pltpu.VMEM(patch_ext.shape, jnp.int32),
            pltpu.SemaphoreType.DMA((2,)),
        ],
        cost_estimate=pl.CostEstimate(flops=15_000_000, bytes_accessed=300_000, transcendentals=0),
        name="lower_error",
    )(in_hbm(patch_pos), in_hbm(patch_ext), here, rim)
    devices = lax.axis_size("row")
    from_within = in_vmem(lax.ppermute(within, "row", [(i, i ^ 1) for i in range(devices)]))
    from_across = in_vmem(
        lax.ppermute(across, "row", [(i, (i + (1 if i % 2 else -1)) % devices) for i in range(devices)])
    )
    moved_rows = in_vmem(pl.pallas_call(
        move_rows,
        out_shape=vmem(3, rows + 16, width + LANES),
        in_specs=[VMEM] * 3,
        out_specs=VMEM,
        cost_estimate=pl.CostEstimate(flops=3_000_000, bytes_accessed=1_000_000, transcendentals=0),
        name="move_rows",
    )(here, rim, slab_above))
    return pl.pallas_call(
        finish,
        out_shape=(f32(half, cols // 2), f32(3, rows, cols), f32(3, 2 * PATCH, 2 * PATCH)),
        in_specs=[VMEM] * 10,
        out_specs=(ANY,) * 3,
        scratch_shapes=[
            vmem(3, rows + 16, width + LANES),
            vmem(3, 72, LANES),
            vmem(3, 16, cols),
            vmem(3, 2, 16, LANES),
            vmem(3, 16, LANES),
            vmem(3, SLAB, LANES),
            vmem(3, 8, width),
            vmem(half, cols // 2),
            vmem(3, 2 * PATCH, 2 * PATCH),
            pltpu.SemaphoreType.DMA((3 + PATCH // PATCH_ROWS,)),
        ],
        compiler_params=PARAMS,
        name="finish",
    )(here, rim, slab_above, moved_rows, from_within, from_across, upper, lower, edge, numbers)


def solution(mesh):
    placed = (
        P(None, "row", "col"),
        P("row", "col"),
        P("row", "col"),
        P("row", "col", None),
        P("row", "col", None),
    )
    return jax.shard_map(
        per_device,
        mesh=mesh,
        in_specs=placed,
        out_specs=(P("row", "col"), P(None, "row", "col"), P(None, "row", "col")),
        check_vma=False,
    )
```

```python
import jax
import jax.numpy as jnp
from jax import lax
from jax.experimental import pallas as pl
from jax.experimental.pallas import tpu as pltpu
from jax.sharding import PartitionSpec as P

SLAB = 64
PATCH = 64
LANES = 128
PATCH_ROWS = 64
UPPER = 32

RATIO = 0.1
ERR_SCALE = 10.0

RIGHT_ROWS, RIGHT_COLS, LEFT_ROWS, OWN_ROWS, OWN_COLS = 6, 7, 8, 10, 11
DOWN_ROWS = 3 * SLAB // 2 + 8

VMEM = pl.BlockSpec(memory_space=pltpu.VMEM)
SMEM = pl.BlockSpec(memory_space=pltpu.SMEM)
ANY = pl.BlockSpec(memory_space=pl.ANY)
PARAMS = pltpu.CompilerParams(vmem_limit_bytes=32 * 1024 * 1024)


def f32(*shape):
    return jax.ShapeDtypeStruct(shape, jnp.float32)


def lane_ids(rows, width=LANES):
    return lax.broadcasted_iota(jnp.int32, (rows, width), 1)


def row_ids(rows, width=LANES):
    return lax.broadcasted_iota(jnp.int32, (rows, width), 0)


def roll(value, by, axis):
    return pltpu.roll(value, by % value.shape[axis], axis)


def cell_terms(depth, first, second):
    inverse_root = lax.rsqrt(depth)
    wave = depth * inverse_root
    inverse = inverse_root * inverse_root
    first_vel = first * inverse
    second_vel = second * inverse
    pressure = 0.5 * depth * depth
    cross = first * second_vel
    row_terms = (first, first * first_vel + pressure, cross, jnp.abs(first_vel) + wave)
    col_terms = (second, cross, second * second_vel + pressure, jnp.abs(second_vel) + wave)
    return row_terms, col_terms


def doubled_flux(left, right, left_terms, right_terms):
    speed = jnp.maximum(left_terms[3], right_terms[3])
    return [(left_terms[c] + right_terms[c]) - speed * (right[c] - left[c]) for c in range(3)]


def spread_step(fields, row_by, col_by):
    row_terms, col_terms = cell_terms(*fields)
    total = None
    for terms, by, axis in ((row_terms, row_by, 0), (col_terms, col_by, 1)):
        lower = [roll(f, by, axis) for f in fields]
        momentum = lower[1 + axis]
        lower_terms = [momentum if c == 0 else roll(terms[c], by, axis) for c in range(4)]
        flux = doubled_flux(lower, fields, lower_terms, terms)
        change = [roll(f, -by, axis) - f for f in flux]
        total = change if total is None else [t + c for t, c in zip(total, change)]
    return [f - (0.5 * RATIO) * t for f, t in zip(fields, total)]


def pair_change(near, far, near_terms, far_terms, axis):
    inner = doubled_flux(near, far, near_terms, far_terms)
    before = [roll(f, 1, axis) for f in far]
    before_terms = [before[1 + axis] if c == 0 else roll(far_terms[c], 1, axis) for c in range(4)]
    outer = doubled_flux(before, near, before_terms, near_terms)
    near_change = [i - o for i, o in zip(inner, outer)]
    far_change = [roll(o, -1, axis) - i for i, o in zip(inner, outer)]
    return near_change, far_change


def paired_step(phases):
    terms = [[cell_terms(*phases[x][y]) for y in range(2)] for x in range(2)]
    along_first = [
        pair_change(phases[0][y], phases[1][y], terms[0][y][0], terms[1][y][0], 0) for y in range(2)
    ]
    along_second = [
        pair_change(phases[x][0], phases[x][1], terms[x][0][1], terms[x][1][1], 1) for x in range(2)
    ]
    return [
        [
            [
                phases[x][y][c] - (0.5 * RATIO) * (along_first[y][x][c] + along_second[x][y][c])
                for c in range(3)
            ]
            for y in range(2)
        ]
        for x in range(2)
    ]


def block_mean(phases):
    return [
        0.25 * ((phases[0][0][c] + phases[1][0][c]) + (phases[0][1][c] + phases[1][1][c])) for c in range(3)
    ]


def coarse_error(phases):
    fine = block_mean(paired_step(paired_step(phases)))
    coarse = spread_step(block_mean(phases), 1, 1)
    parts = [jnp.abs(f - c) for f, c in zip(fine, coarse)]
    return ERR_SCALE * ((parts[0] + parts[1]) + parts[2])


def every_other(first, second, parity):
    lanes = lane_ids(first.shape[0])
    pick = (2 * lanes + parity) % LANES
    low = jnp.take_along_axis(first, pick, axis=1)
    high = jnp.take_along_axis(second, pick, axis=1)
    return jnp.where(lanes < LANES // 2, low, high)


def blank(out_ref):
    out_ref[...] = jnp.zeros(out_ref.shape, jnp.float32)


def pack_cols(row_count, blank_ref, state_ref, left_ref, strip_ref, slab_ref):
    rows, cols = state_ref.shape[1], state_ref.shape[2]
    half = rows // 2
    rc = row_count[0, 0].astype(jnp.float32)
    lanes = lane_ids(half)
    for comp in range(3):
        upper = state_ref[comp, 0:half, cols - LANES : cols]
        lower = roll(state_ref[comp, half:rows, cols - LANES : cols], LANES // 2, 1)
        left_ref[comp * half : (comp + 1) * half, :] = jnp.where(lanes >= LANES // 2, upper, lower)
    lanes = lane_ids(rows)
    packed = None
    for comp in range(3):
        ends = jnp.where(lanes < LANES // 2, state_ref[comp, :, 0:LANES], state_ref[comp, :, cols - LANES : cols])
        ends = roll(ends, 8 * comp + 4, 1)
        packed = ends if packed is None else jnp.where(lanes >= 8 * comp, ends, packed)
    strip_ref[0:24, :] = packed.T[0:24]
    strip_ref[24:32, :] = jnp.full((8, LANES), rc)
    left_ref[3 * half : 3 * half + 8, :] = jnp.full((8, LANES), rc)
    for comp in range(3):
        left_ref[3 * half + 2 * comp : 3 * half + 2 * comp + 2, :] = strip_ref[8 * comp + 2 : 8 * comp + 4, :]
    slab_ref[...] = state_ref[:, rows - SLAB : rows, :]


def pack_right(col_count, strip_ref, right_ref, counts_ref):
    cc = col_count[0, 0].astype(jnp.float32)
    counts = jnp.where(row_ids(8) == 6, strip_ref[24:32, :], cc)
    counts_ref[...] = counts
    right_ref[...] = counts
    for comp in range(3):
        right_ref[2 * comp : 2 * comp + 2, :] = strip_ref[8 * comp + 4 : 8 * comp + 6, :]


def is_odd():
    return lax.axis_index("row") % 2 == 1


def pack_rows(counts_ref, strip_ref, left_ref, right_ref, state_ref, upper_ref, rim_ref, within_ref, across_ref, edge_ref):
    rows, cols = state_ref.shape[1], state_ref.shape[2]
    half = rows // 2
    rc, cc = counts_ref[6:7, :], counts_ref[7:8, :]
    right = jnp.concatenate([right_ref[...], jnp.zeros((LANES - 8, LANES), jnp.float32)], axis=0).T
    lanes = lane_ids(rows)
    left_rc = left_ref[3 * half + 6 : 3 * half + 7, :]
    counts = jnp.where(lanes == LEFT_ROWS, left_rc, jnp.where(lanes == OWN_ROWS, rc, cc))
    odd = is_odd()
    packed_half = SLAB // 2
    low = lane_ids(packed_half) < LANES // 2

    def put(at, down, up):
        size = down.shape[0]
        within_ref[at : at + size, :] = jnp.where(odd, up, down)
        across_ref[at : at + size, :] = jnp.where(odd, down, up)

    ups, downs = [], []
    for comp in range(3):
        packed = left_ref[comp * half : (comp + 1) * half, :]
        left = jnp.concatenate([packed, roll(packed, LANES // 2, 1)], axis=0)
        inner = right if comp == 0 else roll(right, -2 * comp, 1)
        inner = jnp.where(lanes < LEFT_ROWS, inner, counts)
        rim = jnp.where(lanes >= LANES // 2, left, inner)
        rim_ref[comp] = rim
        last = packed[half - SLAB : half]
        downs.append(jnp.where(low, last[0:packed_half], roll(last[packed_half:SLAB], LANES // 2, 1)))
        ups += [state_ref[comp, 0:8, LANES * t : LANES * (t + 1)] for t in range(cols // LANES)] + [rim[0:8]]
        edge_ref[comp, 0:2, :] = left_ref[3 * half + 2 * comp : 3 * half + 2 * comp + 2, :]
        edge_ref[comp, 2:6, :] = strip_ref[8 * comp + 4 : 8 * comp + 8, :]
        edge_ref[comp, 6:10, :] = strip_ref[8 * comp : 8 * comp + 4, :]
        edge_ref[comp, 10:12, :] = right_ref[2 * comp : 2 * comp + 2, :]
        edge_ref[comp, 12:16, :] = strip_ref[8 * comp + 4 : 8 * comp + 8, :]
    downs.append(jnp.where(row_ids(8) == 6, cc, right_ref[...]))
    down = jnp.concatenate(downs, axis=0)
    up = jnp.concatenate(ups, axis=0)
    size = up.shape[0]
    put(0, down[0:size], up)
    put(size, down[size:DOWN_ROWS], down[size:DOWN_ROWS])
    across_ref[DOWN_ROWS : DOWN_ROWS + 8, :] = jnp.zeros((8, LANES), jnp.float32)


def inner_error(state_ref, first, size, columns):
    part = slice(2 * first, 2 * (first + size))
    for comp in range(3):
        left, right = state_ref[comp, part, 0:LANES], state_ref[comp, part, LANES : 2 * LANES]
        for parity in range(2):
            columns[comp, parity] = every_other(left, right, parity)
    phases = [
        [[columns[c, y, pl.ds(x, size, stride=2), :] for c in range(3)] for y in range(2)]
        for x in range(2)
    ]
    return coarse_error(phases)


def upper_error(state_ref, error_ref, columns):
    rows = error_ref.shape[0]
    error_ref[...] = inner_error(state_ref, 0, rows + 8, columns)[0:rows]


def lower_error(pos_ref, ext_ref, state_ref, rim_ref, error_ref, numbers_ref, columns, pos, ext, sems):
    copies = [pltpu.make_async_copy(src, dst, sems.at[k]) for k, (src, dst) in enumerate(((pos_ref, pos), (ext_ref, ext)))]
    for copy in copies:
        copy.start()
    rows = error_ref.shape[0]
    error_ref[...] = inner_error(state_ref, state_ref.shape[1] // 2 - rows - 8, rows + 8, columns)[8 : rows + 8]
    for copy in copies:
        copy.wait()
    pair = [v[0].astype(jnp.float32) for v in (pos, ext)]
    numbers = jnp.broadcast_to(pair[1][:, 1:2], (8, LANES))
    for k, number in enumerate((pair[0][:, 0:1], pair[0][:, 1:2], pair[1][:, 0:1])):
        numbers = jnp.where(row_ids(8) == k, number, numbers)
    numbers_ref[...] = numbers


def edge_phases(state_ref, slab_ref, above_rim, below, edge_ref, near_rows, columns, corners_ref):
    rows, cols = state_ref.shape[1], state_ref.shape[2]
    right = slice(cols, cols + LANES)
    lanes = lane_ids(8)
    packed_up, packed_down = None, None
    for comp in range(3):
        near_rows[comp, 0:2, :] = slab_ref[comp, SLAB - 2 : SLAB, :]
        near_rows[comp, 2:6, :] = state_ref[comp, 0:4, :]
        near_rows[comp, 6:10, :] = state_ref[comp, rows - 4 : rows, :]
        near_rows[comp, 10:12, :] = below[comp, 0:2, 0:cols]
        near_rows[comp, 12:16, :] = state_ref[comp, 0:4, :]
        first, second = near_rows[comp, :, 0:LANES], near_rows[comp, :, LANES : 2 * LANES]
        for parity in range(2):
            columns[comp, parity] = every_other(first, second, parity)

        def around_corner(body, rim):
            start = jnp.where(lanes < LANES // 2, body[:, 0:LANES], rim)
            end = jnp.where(lanes < LANES // 2, rim, body[:, cols - LANES : cols])
            first_six = (lanes >= 12 * comp) & (lanes < 12 * comp + 6)
            return jnp.where(first_six, roll(start, 12 * comp + 2, 1), roll(end, 12 * comp + 10, 1))

        up = around_corner(slab_ref[comp, SLAB - 8 : SLAB, :], above_rim[comp, SLAB - 8 : SLAB, :])
        down = around_corner(below[comp, :, 0:cols], below[comp, :, right])
        packed_up = up if comp == 0 else jnp.where(lanes >= 12 * comp, up, packed_up)
        packed_down = down if comp == 0 else jnp.where(lanes >= 12 * comp, down, packed_down)
    corners = jnp.concatenate([packed_down, jnp.ones((LANES - 16, LANES), jnp.float32), packed_up], axis=0).T
    for comp in range(3):
        corners_ref[comp, 0:12, :] = corners[12 * comp : 12 * comp + 12, :]
        corners_ref[comp, 12:16, :] = edge_ref[comp, 12:16, :]
    phases = []
    for x in range(2):
        phases.append([])
        for y in range(2):
            cells = []
            for comp, turned in ((0, 0), (1, 2), (2, 1)):
                by_row = columns[comp, y, pl.ds(x, 8, stride=2), :]
                own, outer = [ref[turned, pl.ds(x, 8, stride=2), :] for ref in (edge_ref, corners_ref)]
                cells.append(jnp.concatenate([by_row, every_other(own, outer, y)], axis=0))
            phases[-1].append(cells)
    return phases


def put_edges(error, edges):
    half_rows = error.shape[0]
    turned = jnp.concatenate([edges, jnp.zeros((LANES - 16, LANES), jnp.float32)], axis=0).T[0:half_rows]
    lanes, ids = lane_ids(half_rows), row_ids(half_rows)
    error = jnp.where(ids == 0, edges[1:2], jnp.where(ids == half_rows - 1, edges[4:5], error))
    return jnp.where(
        lanes == 0, roll(turned, -9, 1), jnp.where(lanes == LANES - 1, roll(turned, LANES - 13, 1), error)
    )


def minmod(lower_diff, upper_diff):
    smaller, larger = jnp.minimum(lower_diff, upper_diff), jnp.maximum(lower_diff, upper_diff)
    return jnp.maximum(smaller, jnp.minimum(larger, 0.0))


def axis_terms(cells, axis):
    depth, normal, tangent = cells[0], cells[1 + axis], cells[2 - axis]
    inverse_root = lax.rsqrt(depth)
    velocity = normal * (inverse_root * inverse_root)
    along = normal * velocity + 0.5 * depth * depth
    beside = tangent * velocity
    speed = jnp.abs(velocity) + depth * inverse_root
    return (normal, along, beside, speed) if axis == 0 else (normal, beside, along, speed)


def paired_change(near, far, axis):
    down = lambda v: roll(v, 1, axis)
    up = lambda v: roll(v, -1, axis)
    inner = [f - n for n, f in zip(near, far)]
    outer = [n - down(f) for n, f in zip(near, far)]
    near_half = [0.5 * minmod(o, i) for o, i in zip(outer, inner)]
    far_half = [0.5 * minmod(i, up(o)) for o, i in zip(outer, inner)]
    near_hi = [n + s for n, s in zip(near, near_half)]
    near_lo = [n - s for n, s in zip(near, near_half)]
    far_hi = [down(f + s) for f, s in zip(far, far_half)]
    far_lo = [f - s for f, s in zip(far, far_half)]
    terms = lambda cells: axis_terms(cells, axis)
    inner_flux = doubled_flux(near_hi, far_lo, terms(near_hi), terms(far_lo))
    outer_flux = doubled_flux(far_hi, near_lo, terms(far_hi), terms(near_lo))
    near_change = [i - o for i, o in zip(inner_flux, outer_flux)]
    far_change = [up(o) - i for i, o in zip(inner_flux, outer_flux)]
    return near_change, far_change


def doubled_first_step(cells):
    all_terms = cell_terms(*cells)
    changes = []
    for axis in (0, 1):
        terms = all_terms[axis]
        lower = [roll(f, 1, axis) for f in cells]
        lower_terms = [lower[1 + axis] if c == 0 else roll(terms[c], 1, axis) for c in range(4)]
        flux = doubled_flux(lower, cells, lower_terms, terms)
        own = [2.0 * terms[c] for c in range(3)]
        changes.append(
            (
                [o - f for o, f in zip(own, flux)],
                [roll(f, -1, axis) - o for o, f in zip(own, flux)],
            )
        )
    rows, cols = changes
    return [
        [
            [cells[c] - (0.5 * RATIO) * (rows[a][c] + cols[b][c]) for c in range(3)]
            for b in range(2)
        ]
        for a in range(2)
    ]


def patch_rows(cells):
    half = doubled_first_step(cells)
    by_row = [paired_change(half[0][b], half[1][b], 0) for b in range(2)]
    by_col = [paired_change(half[a][0], half[a][1], 1) for a in range(2)]
    size = cells[0].shape[0] - 8
    lanes = lane_ids(size)
    result = []
    for a in range(2):
        fine = [
            [half[a][b][c] - (0.5 * RATIO) * (by_row[b][a][c] + by_col[a][b][c]) for c in range(3)]
            for b in range(2)
        ]
        parts = []
        for c in range(3):
            pick = lanes // 2 + 2
            even = jnp.take_along_axis(fine[0][c][4 : 4 + size], pick, axis=1)
            odd = jnp.take_along_axis(fine[1][c][4 : 4 + size], pick, axis=1)
            parts.append(jnp.where(lanes % 2 == 0, even, odd))
        result.append(parts)
    return result


def sliding(load, start, size):
    group, shift = start // 8, start % 8
    turn = (8 - shift) % 8
    parts = [pltpu.roll(load(group + k), turn, 0) for k in range(size // 8 + 1)]
    keep = row_ids(8, parts[0].shape[1]) < 8 - shift
    return [jnp.where(keep, parts[k], parts[k + 1]) for k in range(size // 8)]


def scalar(values, row, lane):
    return values[row, lane].astype(jnp.int32)


def slab_rows(ref, first, count, size):
    last = SLAB // 8 - 1
    load = lambda k: ref[pl.ds(pl.multiple_of(first + 8 * jnp.minimum(k, last), 8), 8), :]
    return sliding(load, SLAB - count, size)


def column_move(first_cols, last_cols, side, here, right_count):
    lanes = lane_ids(8)
    head = jnp.where(lanes < here, pltpu.roll(side, here, 1), first_cols)
    outer = jnp.where(lanes < right_count, pltpu.roll(last_cols, right_count, 1), side)
    return head, jnp.where(lanes >= LANES // 2, side, outer)


def move_rows(state_ref, rim_ref, slab_ref, wide_ref):
    rows, cols = state_ref.shape[1], state_ref.shape[2]
    counts = rim_ref[0, 0:8, :]
    rc, cc, cc_right = [scalar(counts, 0, k) for k in (OWN_ROWS, OWN_COLS, RIGHT_COLS)]
    for comp in range(3):
        bodies = slab_rows(slab_ref.at[comp], 0, rc, SLAB)
        for k in range(rows // 8):
            part, at = slice(8 * k, 8 * k + 8), slice(8 * k + 8, 8 * k + 16)
            body = state_ref[comp, part, :]
            if 8 * k < SLAB:
                body = jnp.where(row_ids(8, cols) + 8 * k < rc, bodies[k], body)
                wide_ref[comp, at, LANES : LANES + cols] = body
                continue
            head, outer = column_move(
                body[:, 0:LANES], body[:, cols - LANES : cols], rim_ref[comp, part, :], cc, cc_right
            )
            wide_ref[comp, at, 0:LANES] = outer
            wide_ref[comp, at, LANES : 2 * LANES] = head
            wide_ref[comp, at, 2 * LANES : LANES + cols] = body[:, LANES:cols]
            wide_ref[comp, at, LANES + cols : 2 * LANES + cols] = outer


def finish(
    state_ref, rim_ref, slab_ref, rows_ref, within_ref, across_ref, upper_ref, lower_ref, edge_ref, numbers_ref,
    error_out, moved_out, patch_out,
    wide, window, near_rows, columns, corners, above_rim, below, error, patch, sems,
):
    rows, cols = state_ref.shape[1], state_ref.shape[2]
    right = slice(cols, cols + LANES)
    inside_wide = slice(LANES, LANES + cols)
    on_left = lane_ids(8) >= LANES // 2
    copies = [
        pltpu.make_async_copy(rows_ref.at[:, SLAB + 8 : rows + 8, inside_wide], moved_out.at[:, SLAB:rows, :], sems.at[0])
    ]
    copies[-1].start()

    odd = is_odd()
    packed_half = SLAB // 2
    beside = jnp.where(odd, within_ref[DOWN_ROWS - 8 : DOWN_ROWS, :], across_ref[DOWN_ROWS - 8 : DOWN_ROWS, :])
    turned = jnp.concatenate([beside, jnp.zeros((LANES - 8, LANES), jnp.float32)], axis=0).T[rows - SLAB : rows]
    lanes = lane_ids(packed_half)
    tiles = cols // LANES + 1
    for comp in range(3):
        at = slice(comp * packed_half, (comp + 1) * packed_half)
        packed = jnp.where(odd, within_ref[at, :], across_ref[at, :])
        inner = turned if comp == 0 else roll(turned, -2 * comp, 1)
        upper = jnp.where(lanes >= LANES // 2, roll(packed, LANES // 2, 1), inner[0:packed_half])
        lower = jnp.where(lanes >= LANES // 2, packed, inner[packed_half:SLAB])
        above_rim[comp, 0:packed_half, :] = upper
        above_rim[comp, packed_half:SLAB, :] = lower
        for t in range(tiles):
            at = slice(8 * (comp * tiles + t), 8 * (comp * tiles + t) + 8)
            below[comp, :, LANES * t : LANES * (t + 1)] = jnp.where(odd, across_ref[at, :], within_ref[at, :])

    edges = coarse_error(
        edge_phases(state_ref, slab_ref, above_rim, below, edge_ref, near_rows, columns, corners)
    )
    error[...] = put_edges(jnp.concatenate([upper_ref[...], lower_ref[...]], axis=0), edges)

    own_counts, below_counts, numbers = rim_ref[0, 0:8, :], below[0, :, right], numbers_ref[...]
    cc, rc_left, rc_right, cc_right = [
        scalar(own_counts, 0, k) for k in (OWN_COLS, LEFT_ROWS, RIGHT_ROWS, RIGHT_COLS)
    ]
    cc_above, cc_above_right = [scalar(beside, k, 0) for k in (6, 7)]
    rc_below, cc_below, rc_below_left, rc_below_right, cc_below_right = [
        scalar(below_counts, 0, k) for k in (OWN_ROWS, OWN_COLS, LEFT_ROWS, RIGHT_ROWS, RIGHT_COLS)
    ]
    pos_row, pos_col, ext_row, ext_col = [scalar(numbers, k, 0) for k in range(4)]

    def put(comp, at, body, side, here, right_count):
        tail = body[:, LANES:cols]
        head, outer = column_move(body[:, 0:LANES], tail[:, cols - 2 * LANES :], side, here, right_count)
        wide[comp, at : at + 8, 0:LANES] = outer
        wide[comp, at : at + 8, LANES : 2 * LANES] = head
        wide[comp, at : at + 8, 2 * LANES : LANES + cols] = tail
        wide[comp, at : at + 8, LANES + cols : 2 * LANES + cols] = outer

    def moved_rim(ref, first, left, right_count, size):
        from_left = slab_rows(ref, first, left, size)
        from_right = slab_rows(ref, first, right_count, size)
        return [jnp.where(on_left, a, b) for a, b in zip(from_left, from_right)]

    for comp in range(3):
        sides = moved_rim(above_rim.at[comp], 0, rc_left, rc_right, SLAB)
        for k in range(SLAB // 8):
            side = rim_ref[comp, 8 * k : 8 * k + 8, :]
            side = jnp.where(row_ids(8) + 8 * k < jnp.where(on_left, rc_left, rc_right), sides[k], side)
            put(comp, 8 * k + 8, rows_ref[comp, 8 * k + 8 : 8 * k + 16, inside_wide], side, cc, cc_right)
        wide[comp, SLAB + 8 : rows + 8, :] = rows_ref[comp, SLAB + 8 : rows + 8, :]
        put(comp, 0, slab_ref[comp, SLAB - 8 : SLAB, :], above_rim[comp, SLAB - 8 : SLAB, :], cc_above, cc_above_right)
        (body,) = slab_rows(state_ref.at[comp], rows - SLAB, rc_below, 8)
        (side,) = moved_rim(rim_ref.at[comp], rows - SLAB, rc_below_left, rc_below_right, 8)
        body = jnp.where(row_ids(8, cols) < rc_below, body, below[comp, :, 0:cols])
        side = jnp.where(
            row_ids(8) < jnp.where(on_left, rc_below_left, rc_below_right), side, below[comp, :, right]
        )
        put(comp, rows + 8, body, side, cc_below, cc_below_right)
    copies += [
        pltpu.make_async_copy(wide.at[:, 8 : SLAB + 8, inside_wide], moved_out.at[:, 0:SLAB, :], sems.at[1]),
        pltpu.make_async_copy(error, error_out, sems.at[2]),
    ]

    first_lane = pos_col + LANES - 2
    tile, shift = first_lane // LANES, first_lane % LANES
    turn = (LANES - shift) % LANES
    keep = lane_ids(8) < LANES - shift
    for comp in range(3):

        def load(k):
            group = pl.ds(pl.multiple_of(8 * k, 8), 8)
            near = wide[comp, group, pl.ds(pl.multiple_of(LANES * tile, LANES), LANES)]
            far = wide[comp, group, pl.ds(pl.multiple_of(LANES * tile + LANES, LANES), LANES)]
            return jnp.where(keep, pltpu.roll(near, turn, 1), pltpu.roll(far, turn, 1))

        for k, part in enumerate(sliding(load, pos_row + 4, 72)):
            window[comp, 8 * k : 8 * k + 8, :] = part

    fine_rows, fine_cols = 2 * ext_row, 2 * ext_col
    size = PATCH_ROWS
    for start in range(0, PATCH, size):
        cells = [window[c, start : start + size + 8, :] for c in range(3)]
        fine = patch_rows(cells)
        lanes, ids = lane_ids(size), row_ids(size)
        for a in range(2):
            inside = (2 * (ids + start) + a < fine_rows) & (lanes < fine_cols)
            for c in range(3):
                patch[c, pl.ds(2 * start + a, size, stride=2), :] = jnp.where(inside, fine[a][c], 0.0)
        part = pl.ds(2 * start, 2 * size)
        for c in range(3):
            copies.append(pltpu.make_async_copy(patch.at[c, part, :], patch_out.at[c, part, :], sems.at[3 + c]))
            copies[-1].start()
    for copy in copies[1:3]:
        copy.start()
    for copy in copies:
        copy.wait()


def around(axis, by):
    devices = lax.axis_size(axis)
    return [(i, (i + by) % devices) for i in range(devices)]


def in_vmem(value):
    return pltpu.with_memory_space_constraint(value, pltpu.VMEM)


def in_hbm(value):
    return pltpu.with_memory_space_constraint(value, pltpu.HBM)


def vmem(*shape):
    return pltpu.VMEM(shape, jnp.float32)


def per_device(state, row_count, col_count, patch_pos, patch_ext):
    rows, cols = state.shape[1], state.shape[2]
    width = cols + LANES
    half = rows // 2
    here = in_vmem(state)
    ahead = pl.pallas_call(
        blank,
        out_shape=vmem(8, LANES),
        out_specs=VMEM,
        cost_estimate=pl.CostEstimate(flops=10_000_000_000, bytes_accessed=10_000_000, transcendentals=0),
        name="ahead",
    )()
    to_right, strip, slab = pl.pallas_call(
        pack_cols,
        out_shape=(vmem(3 * half + 8, LANES), vmem(32, LANES), vmem(3, SLAB, cols)),
        in_specs=[SMEM, VMEM, VMEM],
        out_specs=(VMEM,) * 3,
        name="pack_cols",
    )(row_count, in_vmem(ahead), here)
    strip = in_vmem(strip)
    to_left, counts = pl.pallas_call(
        pack_right, out_shape=(vmem(8, LANES), vmem(8, LANES)), in_specs=[SMEM, VMEM], out_specs=(VMEM,) * 2, name="pack_right"
    )(col_count, strip)
    from_left = in_vmem(lax.ppermute(to_right, "col", around("col", 1)))
    from_right = in_vmem(lax.ppermute(to_left, "col", around("col", -1)))
    slab_above = in_vmem(lax.ppermute(slab, "row", around("row", 1)))
    upper = in_vmem(pl.pallas_call(
        upper_error,
        out_shape=vmem(UPPER, cols // 2),
        in_specs=[VMEM],
        out_specs=VMEM,
        scratch_shapes=[vmem(3, 2, 2 * UPPER + 16, LANES)],
        cost_estimate=pl.CostEstimate(flops=15_000_000, bytes_accessed=300_000, transcendentals=0),
        name="upper_error",
    )(here))
    rim, within, across, edge = pl.pallas_call(
        pack_rows,
        out_shape=(vmem(3, rows, LANES), vmem(DOWN_ROWS, LANES), vmem(DOWN_ROWS + 8, LANES), vmem(3, 16, LANES)),
        in_specs=[VMEM] * 6,
        out_specs=(VMEM,) * 4,
        cost_estimate=pl.CostEstimate(flops=3_000_000_000, bytes_accessed=600_000, transcendentals=0),
        name="pack_rows",
    )(in_vmem(counts), strip, from_left, from_right, here, upper)
    rim = in_vmem(rim)
    lower, numbers = pl.pallas_call(
        lower_error,
        out_shape=(vmem(half - UPPER, cols // 2), vmem(8, LANES)),
        in_specs=[ANY, ANY, VMEM, VMEM],
        out_specs=(VMEM,) * 2,
        scratch_shapes=[
            vmem(3, 2, 2 * (half - UPPER) + 16, LANES),
            pltpu.VMEM(patch_pos.shape, jnp.int32),
            pltpu.VMEM(patch_ext.shape, jnp.int32),
            pltpu.SemaphoreType.DMA((2,)),
        ],
        cost_estimate=pl.CostEstimate(flops=15_000_000, bytes_accessed=300_000, transcendentals=0),
        name="lower_error",
    )(in_hbm(patch_pos), in_hbm(patch_ext), here, rim)
    devices = lax.axis_size("row")
    from_within = in_vmem(lax.ppermute(within, "row", [(i, i ^ 1) for i in range(devices)]))
    from_across = in_vmem(
        lax.ppermute(across, "row", [(i, (i + (1 if i % 2 else -1)) % devices) for i in range(devices)])
    )
    moved_rows = in_vmem(pl.pallas_call(
        move_rows,
        out_shape=vmem(3, rows + 16, width + LANES),
        in_specs=[VMEM] * 3,
        out_specs=VMEM,
        cost_estimate=pl.CostEstimate(flops=3_000_000, bytes_accessed=1_000_000, transcendentals=0),
        name="move_rows",
    )(here, rim, slab_above))
    return pl.pallas_call(
        finish,
        out_shape=(f32(half, cols // 2), f32(3, rows, cols), f32(3, 2 * PATCH, 2 * PATCH)),
        in_specs=[VMEM] * 10,
        out_specs=(ANY,) * 3,
        scratch_shapes=[
            vmem(3, rows + 16, width + LANES),
            vmem(3, 72, LANES),
            vmem(3, 16, cols),
            vmem(3, 2, 16, LANES),
            vmem(3, 16, LANES),
            vmem(3, SLAB, LANES),
            vmem(3, 8, width),
            vmem(half, cols // 2),
            vmem(3, 2 * PATCH, 2 * PATCH),
            pltpu.SemaphoreType.DMA((6,)),
        ],
        compiler_params=PARAMS,
        name="finish",
    )(here, rim, slab_above, moved_rows, from_within, from_across, upper, lower, edge, numbers)


def solution(mesh):
    placed = (
        P(None, "row", "col"),
        P("row", "col"),
        P("row", "col"),
        P("row", "col", None),
        P("row", "col", None),
    )
    return jax.shard_map(
        per_device,
        mesh=mesh,
        in_specs=placed,
        out_specs=(P("row", "col"), P(None, "row", "col"), P(None, "row", "col")),
        check_vma=False,
    )
```

```python
import jax
import jax.numpy as jnp
from jax import lax
from jax.experimental import pallas as pl
from jax.experimental.pallas import tpu as pltpu
from jax.sharding import PartitionSpec as P

SLAB = 64
PATCH = 64
LANES = 128
PATCH_ROWS = 64
UPPER = 32

RATIO = 0.1
ERR_SCALE = 10.0

RIGHT_ROWS, RIGHT_COLS, LEFT_ROWS, OWN_ROWS, OWN_COLS = 6, 7, 8, 10, 11
DOWN_ROWS = 3 * SLAB // 2 + 8

VMEM = pl.BlockSpec(memory_space=pltpu.VMEM)
SMEM = pl.BlockSpec(memory_space=pltpu.SMEM)
ANY = pl.BlockSpec(memory_space=pl.ANY)
PARAMS = pltpu.CompilerParams(vmem_limit_bytes=32 * 1024 * 1024)


def f32(*shape):
    return jax.ShapeDtypeStruct(shape, jnp.float32)


def lane_ids(rows, width=LANES):
    return lax.broadcasted_iota(jnp.int32, (rows, width), 1)


def row_ids(rows, width=LANES):
    return lax.broadcasted_iota(jnp.int32, (rows, width), 0)


def roll(value, by, axis):
    return pltpu.roll(value, by % value.shape[axis], axis)


def cell_terms(depth, first, second):
    inverse_root = lax.rsqrt(depth)
    wave = depth * inverse_root
    inverse = inverse_root * inverse_root
    first_vel = first * inverse
    second_vel = second * inverse
    pressure = 0.5 * depth * depth
    cross = first * second_vel
    row_terms = (first, first * first_vel + pressure, cross, jnp.abs(first_vel) + wave)
    col_terms = (second, cross, second * second_vel + pressure, jnp.abs(second_vel) + wave)
    return row_terms, col_terms


def doubled_flux(left, right, left_terms, right_terms):
    speed = jnp.maximum(left_terms[3], right_terms[3])
    return [(left_terms[c] + right_terms[c]) - speed * (right[c] - left[c]) for c in range(3)]


def spread_step(fields, row_by, col_by):
    row_terms, col_terms = cell_terms(*fields)
    total = None
    for terms, by, axis in ((row_terms, row_by, 0), (col_terms, col_by, 1)):
        lower = [roll(f, by, axis) for f in fields]
        momentum = lower[1 + axis]
        lower_terms = [momentum if c == 0 else roll(terms[c], by, axis) for c in range(4)]
        flux = doubled_flux(lower, fields, lower_terms, terms)
        change = [roll(f, -by, axis) - f for f in flux]
        total = change if total is None else [t + c for t, c in zip(total, change)]
    return [f - (0.5 * RATIO) * t for f, t in zip(fields, total)]


def pair_change(near, far, near_terms, far_terms, axis):
    inner = doubled_flux(near, far, near_terms, far_terms)
    before = [roll(f, 1, axis) for f in far]
    before_terms = [before[1 + axis] if c == 0 else roll(far_terms[c], 1, axis) for c in range(4)]
    outer = doubled_flux(before, near, before_terms, near_terms)
    near_change = [i - o for i, o in zip(inner, outer)]
    far_change = [roll(o, -1, axis) - i for i, o in zip(inner, outer)]
    return near_change, far_change


def paired_step(phases):
    terms = [[cell_terms(*phases[x][y]) for y in range(2)] for x in range(2)]
    along_first = [
        pair_change(phases[0][y], phases[1][y], terms[0][y][0], terms[1][y][0], 0) for y in range(2)
    ]
    along_second = [
        pair_change(phases[x][0], phases[x][1], terms[x][0][1], terms[x][1][1], 1) for x in range(2)
    ]
    return [
        [
            [
                phases[x][y][c] - (0.5 * RATIO) * (along_first[y][x][c] + along_second[x][y][c])
                for c in range(3)
            ]
            for y in range(2)
        ]
        for x in range(2)
    ]


def block_mean(phases):
    return [
        0.25 * ((phases[0][0][c] + phases[1][0][c]) + (phases[0][1][c] + phases[1][1][c])) for c in range(3)
    ]


def coarse_error(phases):
    fine = block_mean(paired_step(paired_step(phases)))
    coarse = spread_step(block_mean(phases), 1, 1)
    parts = [jnp.abs(f - c) for f, c in zip(fine, coarse)]
    return ERR_SCALE * ((parts[0] + parts[1]) + parts[2])


def every_other(first, second, parity):
    lanes = lane_ids(first.shape[0])
    pick = (2 * lanes + parity) % LANES
    low = jnp.take_along_axis(first, pick, axis=1)
    high = jnp.take_along_axis(second, pick, axis=1)
    return jnp.where(lanes < LANES // 2, low, high)


def blank(out_ref):
    out_ref[...] = jnp.zeros(out_ref.shape, jnp.float32)


def pack_cols(row_count, blank_ref, state_ref, left_ref, strip_ref, slab_ref):
    rows, cols = state_ref.shape[1], state_ref.shape[2]
    half = rows // 2
    rc = row_count[0, 0].astype(jnp.float32)
    lanes = lane_ids(half)
    for comp in range(3):
        upper = state_ref[comp, 0:half, cols - LANES : cols]
        lower = roll(state_ref[comp, half:rows, cols - LANES : cols], LANES // 2, 1)
        left_ref[comp * half : (comp + 1) * half, :] = jnp.where(lanes >= LANES // 2, upper, lower)
    lanes = lane_ids(rows)
    packed = None
    for comp in range(3):
        ends = jnp.where(lanes < LANES // 2, state_ref[comp, :, 0:LANES], state_ref[comp, :, cols - LANES : cols])
        ends = roll(ends, 8 * comp + 4, 1)
        packed = ends if packed is None else jnp.where(lanes >= 8 * comp, ends, packed)
    strip_ref[0:24, :] = packed.T[0:24]
    strip_ref[24:32, :] = jnp.full((8, LANES), rc)
    left_ref[3 * half : 3 * half + 8, :] = jnp.full((8, LANES), rc)
    for comp in range(3):
        left_ref[3 * half + 2 * comp : 3 * half + 2 * comp + 2, :] = strip_ref[8 * comp + 2 : 8 * comp + 4, :]
    slab_ref[...] = state_ref[:, rows - SLAB : rows, :]


def pack_right(col_count, strip_ref, right_ref, counts_ref):
    cc = col_count[0, 0].astype(jnp.float32)
    counts = jnp.where(row_ids(8) == 6, strip_ref[24:32, :], cc)
    counts_ref[...] = counts
    right_ref[...] = counts
    for comp in range(3):
        right_ref[2 * comp : 2 * comp + 2, :] = strip_ref[8 * comp + 4 : 8 * comp + 6, :]


def is_odd():
    return lax.axis_index("row") % 2 == 1


def pack_rows(counts_ref, strip_ref, left_ref, right_ref, state_ref, upper_ref, rim_ref, within_ref, across_ref, edge_ref):
    rows, cols = state_ref.shape[1], state_ref.shape[2]
    half = rows // 2
    rc, cc = counts_ref[6:7, :], counts_ref[7:8, :]
    right = jnp.concatenate([right_ref[...], jnp.zeros((LANES - 8, LANES), jnp.float32)], axis=0).T
    lanes = lane_ids(rows)
    left_rc = left_ref[3 * half + 6 : 3 * half + 7, :]
    counts = jnp.where(lanes == LEFT_ROWS, left_rc, jnp.where(lanes == OWN_ROWS, rc, cc))
    odd = is_odd()
    packed_half = SLAB // 2
    low = lane_ids(packed_half) < LANES // 2

    def put(at, down, up):
        size = down.shape[0]
        within_ref[at : at + size, :] = jnp.where(odd, up, down)
        across_ref[at : at + size, :] = jnp.where(odd, down, up)

    ups, downs = [], []
    for comp in range(3):
        packed = left_ref[comp * half : (comp + 1) * half, :]
        left = jnp.concatenate([packed, roll(packed, LANES // 2, 1)], axis=0)
        inner = right if comp == 0 else roll(right, -2 * comp, 1)
        inner = jnp.where(lanes < LEFT_ROWS, inner, counts)
        rim = jnp.where(lanes >= LANES // 2, left, inner)
        rim_ref[comp] = rim
        last = packed[half - SLAB : half]
        downs.append(jnp.where(low, last[0:packed_half], roll(last[packed_half:SLAB], LANES // 2, 1)))
        ups += [state_ref[comp, 0:8, LANES * t : LANES * (t + 1)] for t in range(cols // LANES)] + [rim[0:8]]
        edge_ref[comp, 0:2, :] = left_ref[3 * half + 2 * comp : 3 * half + 2 * comp + 2, :]
        edge_ref[comp, 2:6, :] = strip_ref[8 * comp + 4 : 8 * comp + 8, :]
        edge_ref[comp, 6:10, :] = strip_ref[8 * comp : 8 * comp + 4, :]
        edge_ref[comp, 10:12, :] = right_ref[2 * comp : 2 * comp + 2, :]
        edge_ref[comp, 12:16, :] = strip_ref[8 * comp + 4 : 8 * comp + 8, :]
    downs.append(jnp.where(row_ids(8) == 6, cc, right_ref[...]))
    down = jnp.concatenate(downs, axis=0)
    up = jnp.concatenate(ups, axis=0)
    size = up.shape[0]
    put(0, down[0:size], up)
    put(size, down[size:DOWN_ROWS], down[size:DOWN_ROWS])
    across_ref[DOWN_ROWS : DOWN_ROWS + 8, :] = jnp.zeros((8, LANES), jnp.float32)


def inner_error(state_ref, first, size, columns):
    part = slice(2 * first, 2 * (first + size))
    for comp in range(3):
        left, right = state_ref[comp, part, 0:LANES], state_ref[comp, part, LANES : 2 * LANES]
        for parity in range(2):
            columns[comp, parity] = every_other(left, right, parity)
    phases = [
        [[columns[c, y, pl.ds(x, size, stride=2), :] for c in range(3)] for y in range(2)]
        for x in range(2)
    ]
    return coarse_error(phases)


def upper_error(state_ref, error_ref, columns):
    rows = error_ref.shape[0]
    error_ref[...] = inner_error(state_ref, 0, rows + 8, columns)[0:rows]


def lower_error(pos_ref, ext_ref, state_ref, rim_ref, error_ref, numbers_ref, columns, pos, ext, sems):
    copies = [pltpu.make_async_copy(src, dst, sems.at[k]) for k, (src, dst) in enumerate(((pos_ref, pos), (ext_ref, ext)))]
    for copy in copies:
        copy.start()
    rows = error_ref.shape[0]
    error_ref[...] = inner_error(state_ref, state_ref.shape[1] // 2 - rows - 8, rows + 8, columns)[8 : rows + 8]
    for copy in copies:
        copy.wait()
    pair = [v[0].astype(jnp.float32) for v in (pos, ext)]
    numbers = jnp.broadcast_to(pair[1][:, 1:2], (8, LANES))
    for k, number in enumerate((pair[0][:, 0:1], pair[0][:, 1:2], pair[1][:, 0:1])):
        numbers = jnp.where(row_ids(8) == k, number, numbers)
    numbers_ref[...] = numbers


def edge_phases(state_ref, slab_ref, above_rim, below, edge_ref, near_rows, columns, corners_ref):
    rows, cols = state_ref.shape[1], state_ref.shape[2]
    right = slice(cols, cols + LANES)
    lanes = lane_ids(8)
    packed_up, packed_down = None, None
    for comp in range(3):
        near_rows[comp][0:2, :] = slab_ref[comp, SLAB - 2 : SLAB, :]
        near_rows[comp][2:6, :] = state_ref[comp, 0:4, :]
        near_rows[comp][6:10, :] = state_ref[comp, rows - 4 : rows, :]
        near_rows[comp][10:12, :] = below[comp][0:2, 0:cols]
        near_rows[comp][12:16, :] = state_ref[comp, 0:4, :]
        first, second = near_rows[comp][:, 0:LANES], near_rows[comp][:, LANES : 2 * LANES]
        for parity in range(2):
            columns[comp][parity] = every_other(first, second, parity)

        def around_corner(body, rim):
            start = jnp.where(lanes < LANES // 2, body[:, 0:LANES], rim)
            end = jnp.where(lanes < LANES // 2, rim, body[:, cols - LANES : cols])
            first_six = (lanes >= 12 * comp) & (lanes < 12 * comp + 6)
            return jnp.where(first_six, roll(start, 12 * comp + 2, 1), roll(end, 12 * comp + 10, 1))

        up = around_corner(slab_ref[comp, SLAB - 8 : SLAB, :], above_rim[comp][SLAB - 8 : SLAB, :])
        down = around_corner(below[comp][:, 0:cols], below[comp][:, right])
        packed_up = up if comp == 0 else jnp.where(lanes >= 12 * comp, up, packed_up)
        packed_down = down if comp == 0 else jnp.where(lanes >= 12 * comp, down, packed_down)
    corners = jnp.concatenate([packed_down, jnp.ones((LANES - 16, LANES), jnp.float32), packed_up], axis=0).T
    for comp in range(3):
        corners_ref[comp][0:12, :] = corners[12 * comp : 12 * comp + 12, :]
        corners_ref[comp][12:16, :] = edge_ref[comp, 12:16, :]
    phases = []
    for x in range(2):
        phases.append([])
        for y in range(2):
            cells = []
            for comp, turned in ((0, 0), (1, 2), (2, 1)):
                by_row = columns[comp][y, pl.ds(x, 8, stride=2), :]
                own = edge_ref[turned, pl.ds(x, 8, stride=2), :]
                outer = corners_ref[turned][pl.ds(x, 8, stride=2), :]
                cells.append(jnp.concatenate([by_row, every_other(own, outer, y)], axis=0))
            phases[-1].append(cells)
    return phases


def put_edges(error, edges):
    half_rows = error.shape[0]
    turned = jnp.concatenate([edges, jnp.zeros((LANES - 16, LANES), jnp.float32)], axis=0).T[0:half_rows]
    lanes, ids = lane_ids(half_rows), row_ids(half_rows)
    error = jnp.where(ids == 0, edges[1:2], jnp.where(ids == half_rows - 1, edges[4:5], error))
    return jnp.where(
        lanes == 0, roll(turned, -9, 1), jnp.where(lanes == LANES - 1, roll(turned, LANES - 13, 1), error)
    )


def minmod(lower_diff, upper_diff):
    smaller, larger = jnp.minimum(lower_diff, upper_diff), jnp.maximum(lower_diff, upper_diff)
    return jnp.maximum(smaller, jnp.minimum(larger, 0.0))


def axis_terms(cells, axis):
    depth, normal, tangent = cells[0], cells[1 + axis], cells[2 - axis]
    inverse_root = lax.rsqrt(depth)
    velocity = normal * (inverse_root * inverse_root)
    along = normal * velocity + 0.5 * depth * depth
    beside = tangent * velocity
    speed = jnp.abs(velocity) + depth * inverse_root
    return (normal, along, beside, speed) if axis == 0 else (normal, beside, along, speed)


def paired_change(near, far, axis):
    down = lambda v: roll(v, 1, axis)
    up = lambda v: roll(v, -1, axis)
    inner = [f - n for n, f in zip(near, far)]
    outer = [n - down(f) for n, f in zip(near, far)]
    near_half = [0.5 * minmod(o, i) for o, i in zip(outer, inner)]
    far_half = [0.5 * minmod(i, up(o)) for o, i in zip(outer, inner)]
    near_hi = [n + s for n, s in zip(near, near_half)]
    near_lo = [n - s for n, s in zip(near, near_half)]
    far_hi = [down(f + s) for f, s in zip(far, far_half)]
    far_lo = [f - s for f, s in zip(far, far_half)]
    terms = lambda cells: axis_terms(cells, axis)
    inner_flux = doubled_flux(near_hi, far_lo, terms(near_hi), terms(far_lo))
    outer_flux = doubled_flux(far_hi, near_lo, terms(far_hi), terms(near_lo))
    near_change = [i - o for i, o in zip(inner_flux, outer_flux)]
    far_change = [up(o) - i for i, o in zip(inner_flux, outer_flux)]
    return near_change, far_change


def doubled_first_step(cells):
    all_terms = cell_terms(*cells)
    changes = []
    for axis in (0, 1):
        terms = all_terms[axis]
        lower = [roll(f, 1, axis) for f in cells]
        lower_terms = [lower[1 + axis] if c == 0 else roll(terms[c], 1, axis) for c in range(4)]
        flux = doubled_flux(lower, cells, lower_terms, terms)
        own = [2.0 * terms[c] for c in range(3)]
        changes.append(
            (
                [o - f for o, f in zip(own, flux)],
                [roll(f, -1, axis) - o for o, f in zip(own, flux)],
            )
        )
    rows, cols = changes
    return [
        [
            [cells[c] - (0.5 * RATIO) * (rows[a][c] + cols[b][c]) for c in range(3)]
            for b in range(2)
        ]
        for a in range(2)
    ]


def patch_rows(cells):
    half = doubled_first_step(cells)
    by_row = [paired_change(half[0][b], half[1][b], 0) for b in range(2)]
    by_col = [paired_change(half[a][0], half[a][1], 1) for a in range(2)]
    size = cells[0].shape[0] - 8
    lanes = lane_ids(size)
    result = []
    for a in range(2):
        fine = [
            [half[a][b][c] - (0.5 * RATIO) * (by_row[b][a][c] + by_col[a][b][c]) for c in range(3)]
            for b in range(2)
        ]
        parts = []
        for c in range(3):
            pick = lanes // 2 + 2
            even = jnp.take_along_axis(fine[0][c][4 : 4 + size], pick, axis=1)
            odd = jnp.take_along_axis(fine[1][c][4 : 4 + size], pick, axis=1)
            parts.append(jnp.where(lanes % 2 == 0, even, odd))
        result.append(parts)
    return result


def sliding(load, start, size):
    group, shift = start // 8, start % 8
    turn = (8 - shift) % 8
    parts = [pltpu.roll(load(group + k), turn, 0) for k in range(size // 8 + 1)]
    keep = row_ids(8, parts[0].shape[1]) < 8 - shift
    return [jnp.where(keep, parts[k], parts[k + 1]) for k in range(size // 8)]


def scalar(values, row, lane):
    return values[row, lane].astype(jnp.int32)


def slab_rows(ref, first, count, size):
    last = SLAB // 8 - 1
    load = lambda k: ref[pl.ds(pl.multiple_of(first + 8 * jnp.minimum(k, last), 8), 8), :]
    return sliding(load, SLAB - count, size)


def column_move(first_cols, last_cols, side, here, right_count):
    lanes = lane_ids(8)
    head = jnp.where(lanes < here, pltpu.roll(side, here, 1), first_cols)
    outer = jnp.where(lanes < right_count, pltpu.roll(last_cols, right_count, 1), side)
    return head, jnp.where(lanes >= LANES // 2, side, outer)


def move_rows(state_ref, rim_ref, slab_ref, wide_ref):
    rows, cols = state_ref.shape[1], state_ref.shape[2]
    counts = rim_ref[0, 0:8, :]
    rc, cc, cc_right = [scalar(counts, 0, k) for k in (OWN_ROWS, OWN_COLS, RIGHT_COLS)]
    for comp in range(3):
        bodies = slab_rows(slab_ref.at[comp], 0, rc, SLAB)
        for k in range(rows // 8):
            part, at = slice(8 * k, 8 * k + 8), slice(8 * k + 8, 8 * k + 16)
            body = state_ref[comp, part, :]
            if 8 * k < SLAB:
                body = jnp.where(row_ids(8, cols) + 8 * k < rc, bodies[k], body)
                wide_ref[comp, at, LANES : LANES + cols] = body
                continue
            head, outer = column_move(
                body[:, 0:LANES], body[:, cols - LANES : cols], rim_ref[comp, part, :], cc, cc_right
            )
            wide_ref[comp, at, 0:LANES] = outer
            wide_ref[comp, at, LANES : 2 * LANES] = head
            wide_ref[comp, at, 2 * LANES : LANES + cols] = body[:, LANES:cols]
            wide_ref[comp, at, LANES + cols : 2 * LANES + cols] = outer


def finish(
    state_ref, rim_ref, slab_ref, rows_ref, within_ref, across_ref, upper_ref, lower_ref, edge_ref, numbers_ref,
    error_out, moved_out, patch_out,
    wide, window, near_rows, columns, corners, above_rim, below, patch, error, sems,
):
    rows, cols = state_ref.shape[1], state_ref.shape[2]
    right = slice(cols, cols + LANES)
    inside_wide = slice(LANES, LANES + cols)
    on_left = lane_ids(8) >= LANES // 2
    copies = [
        pltpu.make_async_copy(rows_ref.at[:, SLAB + 8 : rows + 8, inside_wide], moved_out.at[:, SLAB:rows, :], sems.at[0])
    ]
    copies[-1].start()

    odd = is_odd()
    packed_half = SLAB // 2
    beside = jnp.where(odd, within_ref[DOWN_ROWS - 8 : DOWN_ROWS, :], across_ref[DOWN_ROWS - 8 : DOWN_ROWS, :])
    turned = jnp.concatenate([beside, jnp.zeros((LANES - 8, LANES), jnp.float32)], axis=0).T[rows - SLAB : rows]
    lanes = lane_ids(packed_half)
    tiles = cols // LANES + 1
    for comp in range(3):
        at = slice(comp * packed_half, (comp + 1) * packed_half)
        packed = jnp.where(odd, within_ref[at, :], across_ref[at, :])
        inner = turned if comp == 0 else roll(turned, -2 * comp, 1)
        upper = jnp.where(lanes >= LANES // 2, roll(packed, LANES // 2, 1), inner[0:packed_half])
        lower = jnp.where(lanes >= LANES // 2, packed, inner[packed_half:SLAB])
        above_rim[comp][0:packed_half, :] = upper
        above_rim[comp][packed_half:SLAB, :] = lower
        for t in range(tiles):
            at = slice(8 * (comp * tiles + t), 8 * (comp * tiles + t) + 8)
            below[comp][:, LANES * t : LANES * (t + 1)] = jnp.where(odd, across_ref[at, :], within_ref[at, :])

    edges = coarse_error(
        edge_phases(state_ref, slab_ref, above_rim, below, edge_ref, near_rows, columns, corners)
    )
    error[...] = put_edges(jnp.concatenate([upper_ref[...], lower_ref[...]], axis=0), edges)

    own_counts, below_counts, numbers = rim_ref[0, 0:8, :], below[0][:, right], numbers_ref[...]
    cc, rc_left, rc_right, cc_right = [
        scalar(own_counts, 0, k) for k in (OWN_COLS, LEFT_ROWS, RIGHT_ROWS, RIGHT_COLS)
    ]
    cc_above, cc_above_right = [scalar(beside, k, 0) for k in (6, 7)]
    rc_below, cc_below, rc_below_left, rc_below_right, cc_below_right = [
        scalar(below_counts, 0, k) for k in (OWN_ROWS, OWN_COLS, LEFT_ROWS, RIGHT_ROWS, RIGHT_COLS)
    ]
    pos_row, pos_col, ext_row, ext_col = [scalar(numbers, k, 0) for k in range(4)]

    def put(comp, at, body, side, here, right_count):
        tail = body[:, LANES:cols]
        head, outer = column_move(body[:, 0:LANES], tail[:, cols - 2 * LANES :], side, here, right_count)
        wide[comp][at : at + 8, 0:LANES] = outer
        wide[comp][at : at + 8, LANES : 2 * LANES] = head
        wide[comp][at : at + 8, 2 * LANES : LANES + cols] = tail
        wide[comp][at : at + 8, LANES + cols : 2 * LANES + cols] = outer

    def moved_rim(ref, first, left, right_count, size):
        from_left = slab_rows(ref, first, left, size)
        from_right = slab_rows(ref, first, right_count, size)
        return [jnp.where(on_left, a, b) for a, b in zip(from_left, from_right)]

    for comp in range(3):
        sides = moved_rim(above_rim[comp], 0, rc_left, rc_right, SLAB)
        for k in range(SLAB // 8):
            side = rim_ref[comp, 8 * k : 8 * k + 8, :]
            side = jnp.where(row_ids(8) + 8 * k < jnp.where(on_left, rc_left, rc_right), sides[k], side)
            put(comp, 8 * k + 8, rows_ref[comp, 8 * k + 8 : 8 * k + 16, inside_wide], side, cc, cc_right)
        wide[comp][SLAB + 8 : rows + 8, :] = rows_ref[comp, SLAB + 8 : rows + 8, :]
        put(comp, 0, slab_ref[comp, SLAB - 8 : SLAB, :], above_rim[comp][SLAB - 8 : SLAB, :], cc_above, cc_above_right)
        (body,) = slab_rows(state_ref.at[comp], rows - SLAB, rc_below, 8)
        (side,) = moved_rim(rim_ref.at[comp], rows - SLAB, rc_below_left, rc_below_right, 8)
        body = jnp.where(row_ids(8, cols) < rc_below, body, below[comp][:, 0:cols])
        side = jnp.where(
            row_ids(8) < jnp.where(on_left, rc_below_left, rc_below_right), side, below[comp][:, right]
        )
        put(comp, rows + 8, body, side, cc_below, cc_below_right)
    copies.append(pltpu.make_async_copy(error, error_out, sems.at[1]))
    copies += [
        pltpu.make_async_copy(wide[c].at[8 : SLAB + 8, inside_wide], moved_out.at[c, 0:SLAB, :], sems.at[2 + c])
        for c in range(3)
    ]

    first_lane = pos_col + LANES - 2
    tile, shift = first_lane // LANES, first_lane % LANES
    turn = (LANES - shift) % LANES
    keep = lane_ids(8) < LANES - shift
    for comp in range(3):

        def load(k):
            group = pl.ds(pl.multiple_of(8 * k, 8), 8)
            near = wide[comp][group, pl.ds(pl.multiple_of(LANES * tile, LANES), LANES)]
            far = wide[comp][group, pl.ds(pl.multiple_of(LANES * tile + LANES, LANES), LANES)]
            return jnp.where(keep, pltpu.roll(near, turn, 1), pltpu.roll(far, turn, 1))

        for k, part in enumerate(sliding(load, pos_row + 4, 72)):
            window[comp][8 * k : 8 * k + 8, :] = part

    fine_rows, fine_cols = 2 * ext_row, 2 * ext_col
    size = PATCH_ROWS
    for start in range(0, PATCH, size):
        cells = [window[c][start : start + size + 8, :] for c in range(3)]
        fine = patch_rows(cells)
        lanes, ids = lane_ids(size), row_ids(size)
        for a in range(2):
            inside = (2 * (ids + start) + a < fine_rows) & (lanes < fine_cols)
            for c in range(3):
                patch[c][pl.ds(2 * start + a, size, stride=2), :] = jnp.where(inside, fine[a][c], 0.0)
        part = pl.ds(2 * start, 2 * size)
        for c in range(3):
            copies.append(pltpu.make_async_copy(patch[c].at[part, :], patch_out.at[c, part, :], sems.at[5 + c]))
            copies[-1].start()
    for copy in copies[1:5]:
        copy.start()
    for copy in copies:
        copy.wait()


def around(axis, by):
    devices = lax.axis_size(axis)
    return [(i, (i + by) % devices) for i in range(devices)]


def in_vmem(value):
    return pltpu.with_memory_space_constraint(value, pltpu.VMEM)


def in_hbm(value):
    return pltpu.with_memory_space_constraint(value, pltpu.HBM)


def vmem(*shape):
    return pltpu.VMEM(shape, jnp.float32)


def per_device(state, row_count, col_count, patch_pos, patch_ext):
    rows, cols = state.shape[1], state.shape[2]
    width = cols + LANES
    half = rows // 2
    here = in_vmem(state)
    ahead = pl.pallas_call(
        blank,
        out_shape=vmem(8, LANES),
        out_specs=VMEM,
        cost_estimate=pl.CostEstimate(flops=10_000_000_000, bytes_accessed=10_000_000, transcendentals=0),
        name="ahead",
    )()
    to_right, strip, slab = pl.pallas_call(
        pack_cols,
        out_shape=(vmem(3 * half + 8, LANES), vmem(32, LANES), vmem(3, SLAB, cols)),
        in_specs=[SMEM, VMEM, VMEM],
        out_specs=(VMEM,) * 3,
        name="pack_cols",
    )(row_count, in_vmem(ahead), here)
    strip = in_vmem(strip)
    to_left, counts = pl.pallas_call(
        pack_right, out_shape=(vmem(8, LANES), vmem(8, LANES)), in_specs=[SMEM, VMEM], out_specs=(VMEM,) * 2, name="pack_right"
    )(col_count, strip)
    from_left = in_vmem(lax.ppermute(to_right, "col", around("col", 1)))
    from_right = in_vmem(lax.ppermute(to_left, "col", around("col", -1)))
    slab_above = in_vmem(lax.ppermute(slab, "row", around("row", 1)))
    upper = in_vmem(pl.pallas_call(
        upper_error,
        out_shape=vmem(UPPER, cols // 2),
        in_specs=[VMEM],
        out_specs=VMEM,
        scratch_shapes=[vmem(3, 2, 2 * UPPER + 16, LANES)],
        cost_estimate=pl.CostEstimate(flops=15_000_000, bytes_accessed=300_000, transcendentals=0),
        name="upper_error",
    )(here))
    rim, within, across, edge = pl.pallas_call(
        pack_rows,
        out_shape=(vmem(3, rows, LANES), vmem(DOWN_ROWS, LANES), vmem(DOWN_ROWS + 8, LANES), vmem(3, 16, LANES)),
        in_specs=[VMEM] * 6,
        out_specs=(VMEM,) * 4,
        cost_estimate=pl.CostEstimate(flops=3_000_000_000, bytes_accessed=600_000, transcendentals=0),
        name="pack_rows",
    )(in_vmem(counts), strip, from_left, from_right, here, upper)
    rim = in_vmem(rim)
    lower, numbers = pl.pallas_call(
        lower_error,
        out_shape=(vmem(half - UPPER, cols // 2), vmem(8, LANES)),
        in_specs=[ANY, ANY, VMEM, VMEM],
        out_specs=(VMEM,) * 2,
        scratch_shapes=[
            vmem(3, 2, 2 * (half - UPPER) + 16, LANES),
            pltpu.VMEM(patch_pos.shape, jnp.int32),
            pltpu.VMEM(patch_ext.shape, jnp.int32),
            pltpu.SemaphoreType.DMA((2,)),
        ],
        cost_estimate=pl.CostEstimate(flops=15_000_000, bytes_accessed=300_000, transcendentals=0),
        name="lower_error",
    )(in_hbm(patch_pos), in_hbm(patch_ext), here, rim)
    devices = lax.axis_size("row")
    from_within = in_vmem(lax.ppermute(within, "row", [(i, i ^ 1) for i in range(devices)]))
    from_across = in_vmem(
        lax.ppermute(across, "row", [(i, (i + (1 if i % 2 else -1)) % devices) for i in range(devices)])
    )
    moved_rows = in_vmem(pl.pallas_call(
        move_rows,
        out_shape=vmem(3, rows + 16, width + LANES),
        in_specs=[VMEM] * 3,
        out_specs=VMEM,
        cost_estimate=pl.CostEstimate(flops=3_000_000, bytes_accessed=1_000_000, transcendentals=0),
        name="move_rows",
    )(here, rim, slab_above))
    return pl.pallas_call(
        finish,
        out_shape=(f32(half, cols // 2), f32(3, rows, cols), f32(3, 2 * PATCH, 2 * PATCH)),
        in_specs=[VMEM] * 10,
        out_specs=(ANY,) * 3,
        scratch_shapes=[
            [vmem(rows + 16, width + LANES)] * 3,
            [vmem(72, LANES)] * 3,
            [vmem(16, cols)] * 3,
            [vmem(2, 16, LANES)] * 3,
            [vmem(16, LANES)] * 3,
            [vmem(SLAB, LANES)] * 3,
            [vmem(8, width)] * 3,
            [vmem(2 * PATCH, 2 * PATCH)] * 3,
            vmem(half, cols // 2),
            pltpu.SemaphoreType.DMA((8,)),
        ],
        compiler_params=PARAMS,
        name="finish",
    )(here, rim, slab_above, moved_rows, from_within, from_across, upper, lower, edge, numbers)


def solution(mesh):
    placed = (
        P(None, "row", "col"),
        P("row", "col"),
        P("row", "col"),
        P("row", "col", None),
        P("row", "col", None),
    )
    return jax.shard_map(
        per_device,
        mesh=mesh,
        in_specs=placed,
        out_specs=(P("row", "col"), P(None, "row", "col"), P(None, "row", "col")),
        check_vma=False,
    )
```

```python
import jax
import jax.numpy as jnp
from jax import lax
from jax.experimental import pallas as pl
from jax.experimental.pallas import tpu as pltpu
from jax.sharding import PartitionSpec as P

SLAB = 64
PATCH = 64
LANES = 128
UPPER = 32

RATIO = 0.1
ERR_SCALE = 10.0

RIGHT_ROWS, RIGHT_COLS, LEFT_ROWS, OWN_ROWS, OWN_COLS = 6, 7, 8, 10, 11
DOWN_ROWS = 3 * SLAB // 2 + 8

VMEM = pl.BlockSpec(memory_space=pltpu.VMEM)
SMEM = pl.BlockSpec(memory_space=pltpu.SMEM)
ANY = pl.BlockSpec(memory_space=pl.ANY)
PARAMS = pltpu.CompilerParams(vmem_limit_bytes=32 * 1024 * 1024)


def f32(*shape):
    return jax.ShapeDtypeStruct(shape, jnp.float32)


def lane_ids(rows, width=LANES):
    return lax.broadcasted_iota(jnp.int32, (rows, width), 1)


def row_ids(rows, width=LANES):
    return lax.broadcasted_iota(jnp.int32, (rows, width), 0)


def roll(value, by, axis):
    return pltpu.roll(value, by % value.shape[axis], axis)


def cell_terms(depth, first, second):
    inverse_root = lax.rsqrt(depth)
    wave = depth * inverse_root
    inverse = inverse_root * inverse_root
    first_vel = first * inverse
    second_vel = second * inverse
    pressure = 0.5 * depth * depth
    cross = first * second_vel
    row_terms = (first, first * first_vel + pressure, cross, jnp.abs(first_vel) + wave)
    col_terms = (second, cross, second * second_vel + pressure, jnp.abs(second_vel) + wave)
    return row_terms, col_terms


def doubled_flux(left, right, left_terms, right_terms):
    speed = jnp.maximum(left_terms[3], right_terms[3])
    return [(left_terms[c] + right_terms[c]) - speed * (right[c] - left[c]) for c in range(3)]


def spread_step(fields, row_by, col_by):
    row_terms, col_terms = cell_terms(*fields)
    total = None
    for terms, by, axis in ((row_terms, row_by, 0), (col_terms, col_by, 1)):
        lower = [roll(f, by, axis) for f in fields]
        momentum = lower[1 + axis]
        lower_terms = [momentum if c == 0 else roll(terms[c], by, axis) for c in range(4)]
        flux = doubled_flux(lower, fields, lower_terms, terms)
        change = [roll(f, -by, axis) - f for f in flux]
        total = change if total is None else [t + c for t, c in zip(total, change)]
    return [f - (0.5 * RATIO) * t for f, t in zip(fields, total)]


def pair_change(near, far, near_terms, far_terms, axis):
    inner = doubled_flux(near, far, near_terms, far_terms)
    before = [roll(f, 1, axis) for f in far]
    before_terms = [before[1 + axis] if c == 0 else roll(far_terms[c], 1, axis) for c in range(4)]
    outer = doubled_flux(before, near, before_terms, near_terms)
    near_change = [i - o for i, o in zip(inner, outer)]
    far_change = [roll(o, -1, axis) - i for i, o in zip(inner, outer)]
    return near_change, far_change


def paired_step(phases):
    terms = [[cell_terms(*phases[x][y]) for y in range(2)] for x in range(2)]
    along_first = [
        pair_change(phases[0][y], phases[1][y], terms[0][y][0], terms[1][y][0], 0) for y in range(2)
    ]
    along_second = [
        pair_change(phases[x][0], phases[x][1], terms[x][0][1], terms[x][1][1], 1) for x in range(2)
    ]
    return [
        [
            [
                phases[x][y][c] - (0.5 * RATIO) * (along_first[y][x][c] + along_second[x][y][c])
                for c in range(3)
            ]
            for y in range(2)
        ]
        for x in range(2)
    ]


def block_mean(phases):
    return [
        0.25 * ((phases[0][0][c] + phases[1][0][c]) + (phases[0][1][c] + phases[1][1][c])) for c in range(3)
    ]


def coarse_error(phases):
    fine = block_mean(paired_step(paired_step(phases)))
    coarse = spread_step(block_mean(phases), 1, 1)
    parts = [jnp.abs(f - c) for f, c in zip(fine, coarse)]
    return ERR_SCALE * ((parts[0] + parts[1]) + parts[2])


def every_other(first, second, parity):
    lanes = lane_ids(first.shape[0])
    pick = (2 * lanes + parity) % LANES
    low = jnp.take_along_axis(first, pick, axis=1)
    high = jnp.take_along_axis(second, pick, axis=1)
    return jnp.where(lanes < LANES // 2, low, high)


def blank(out_ref):
    out_ref[...] = jnp.zeros(out_ref.shape, jnp.float32)


def pack_cols(row_count, blank_ref, state_ref, left_ref, strip_ref, slab_ref):
    rows, cols = state_ref.shape[1], state_ref.shape[2]
    half = rows // 2
    rc = row_count[0, 0].astype(jnp.float32)
    lanes = lane_ids(half)
    for comp in range(3):
        upper = state_ref[comp, 0:half, cols - LANES : cols]
        lower = roll(state_ref[comp, half:rows, cols - LANES : cols], LANES // 2, 1)
        left_ref[comp * half : (comp + 1) * half, :] = jnp.where(lanes >= LANES // 2, upper, lower)
    lanes = lane_ids(rows)
    packed = None
    for comp in range(3):
        ends = jnp.where(lanes < LANES // 2, state_ref[comp, :, 0:LANES], state_ref[comp, :, cols - LANES : cols])
        ends = roll(ends, 8 * comp + 4, 1)
        packed = ends if packed is None else jnp.where(lanes >= 8 * comp, ends, packed)
    strip_ref[0:24, :] = packed.T[0:24]
    strip_ref[24:32, :] = jnp.full((8, LANES), rc)
    left_ref[3 * half : 3 * half + 8, :] = jnp.full((8, LANES), rc)
    for comp in range(3):
        left_ref[3 * half + 2 * comp : 3 * half + 2 * comp + 2, :] = strip_ref[8 * comp + 2 : 8 * comp + 4, :]
    slab_ref[...] = state_ref[:, rows - SLAB : rows, :]


def pack_right(col_count, strip_ref, right_ref, counts_ref):
    cc = col_count[0, 0].astype(jnp.float32)
    counts = jnp.where(row_ids(8) == 6, strip_ref[24:32, :], cc)
    counts_ref[...] = counts
    right_ref[...] = counts
    for comp in range(3):
        right_ref[2 * comp : 2 * comp + 2, :] = strip_ref[8 * comp + 4 : 8 * comp + 6, :]


def is_odd():
    return lax.axis_index("row") % 2 == 1


def pack_rows(counts_ref, strip_ref, left_ref, right_ref, state_ref, upper_ref, rim_ref, within_ref, across_ref, edge_ref):
    rows, cols = state_ref.shape[1], state_ref.shape[2]
    half = rows // 2
    rc, cc = counts_ref[6:7, :], counts_ref[7:8, :]
    right = jnp.concatenate([right_ref[...], jnp.zeros((LANES - 8, LANES), jnp.float32)], axis=0).T
    lanes = lane_ids(rows)
    left_rc = left_ref[3 * half + 6 : 3 * half + 7, :]
    counts = jnp.where(lanes == LEFT_ROWS, left_rc, jnp.where(lanes == OWN_ROWS, rc, cc))
    odd = is_odd()
    packed_half = SLAB // 2
    low = lane_ids(packed_half) < LANES // 2

    def put(at, down, up):
        size = down.shape[0]
        within_ref[at : at + size, :] = jnp.where(odd, up, down)
        across_ref[at : at + size, :] = jnp.where(odd, down, up)

    ups, downs = [], []
    for comp in range(3):
        packed = left_ref[comp * half : (comp + 1) * half, :]
        left = jnp.concatenate([packed, roll(packed, LANES // 2, 1)], axis=0)
        inner = right if comp == 0 else roll(right, -2 * comp, 1)
        inner = jnp.where(lanes < LEFT_ROWS, inner, counts)
        rim = jnp.where(lanes >= LANES // 2, left, inner)
        rim_ref[comp] = rim
        last = packed[half - SLAB : half]
        downs.append(jnp.where(low, last[0:packed_half], roll(last[packed_half:SLAB], LANES // 2, 1)))
        ups += [state_ref[comp, 0:8, LANES * t : LANES * (t + 1)] for t in range(cols // LANES)] + [rim[0:8]]
        edge_ref[comp, 0:2, :] = left_ref[3 * half + 2 * comp : 3 * half + 2 * comp + 2, :]
        edge_ref[comp, 2:6, :] = strip_ref[8 * comp + 4 : 8 * comp + 8, :]
        edge_ref[comp, 6:10, :] = strip_ref[8 * comp : 8 * comp + 4, :]
        edge_ref[comp, 10:12, :] = right_ref[2 * comp : 2 * comp + 2, :]
        edge_ref[comp, 12:16, :] = strip_ref[8 * comp + 4 : 8 * comp + 8, :]
    downs.append(jnp.where(row_ids(8) == 6, cc, right_ref[...]))
    down = jnp.concatenate(downs, axis=0)
    up = jnp.concatenate(ups, axis=0)
    size = up.shape[0]
    put(0, down[0:size], up)
    put(size, down[size:DOWN_ROWS], down[size:DOWN_ROWS])
    across_ref[DOWN_ROWS : DOWN_ROWS + 8, :] = jnp.zeros((8, LANES), jnp.float32)


def inner_error(state_ref, first, size, columns):
    part = slice(2 * first, 2 * (first + size))
    for comp in range(3):
        left, right = state_ref[comp, part, 0:LANES], state_ref[comp, part, LANES : 2 * LANES]
        for parity in range(2):
            columns[comp, parity] = every_other(left, right, parity)
    phases = [
        [[columns[c, y, pl.ds(x, size, stride=2), :] for c in range(3)] for y in range(2)]
        for x in range(2)
    ]
    return coarse_error(phases)


def upper_error(state_ref, error_ref, columns):
    rows = error_ref.shape[0]
    error_ref[...] = inner_error(state_ref, 0, rows + 8, columns)[0:rows]


def lower_error(pos_ref, ext_ref, state_ref, rim_ref, error_ref, numbers_ref, columns, pos, ext, sems):
    copies = [pltpu.make_async_copy(src, dst, sems.at[k]) for k, (src, dst) in enumerate(((pos_ref, pos), (ext_ref, ext)))]
    for copy in copies:
        copy.start()
    rows = error_ref.shape[0]
    error_ref[...] = inner_error(state_ref, state_ref.shape[1] // 2 - rows - 8, rows + 8, columns)[8 : rows + 8]
    for copy in copies:
        copy.wait()
    pair = [v[0].astype(jnp.float32) for v in (pos, ext)]
    numbers = jnp.broadcast_to(pair[1][:, 1:2], (8, LANES))
    for k, number in enumerate((pair[0][:, 0:1], pair[0][:, 1:2], pair[1][:, 0:1])):
        numbers = jnp.where(row_ids(8) == k, number, numbers)
    numbers_ref[...] = numbers


def edge_phases(state_ref, slab_ref, above_rim, below, edge_ref, near_rows, columns, corners_ref):
    rows, cols = state_ref.shape[1], state_ref.shape[2]
    right = slice(cols, cols + LANES)
    lanes = lane_ids(8)
    packed_up, packed_down = None, None
    for comp in range(3):
        near_rows[comp][0:2, :] = slab_ref[comp, SLAB - 2 : SLAB, :]
        near_rows[comp][2:6, :] = state_ref[comp, 0:4, :]
        near_rows[comp][6:10, :] = state_ref[comp, rows - 4 : rows, :]
        near_rows[comp][10:12, :] = below[comp][0:2, 0:cols]
        near_rows[comp][12:16, :] = state_ref[comp, 0:4, :]
        first, second = near_rows[comp][:, 0:LANES], near_rows[comp][:, LANES : 2 * LANES]
        for parity in range(2):
            columns[comp][parity] = every_other(first, second, parity)

        def around_corner(body, rim):
            start = jnp.where(lanes < LANES // 2, body[:, 0:LANES], rim)
            end = jnp.where(lanes < LANES // 2, rim, body[:, cols - LANES : cols])
            first_six = (lanes >= 12 * comp) & (lanes < 12 * comp + 6)
            return jnp.where(first_six, roll(start, 12 * comp + 2, 1), roll(end, 12 * comp + 10, 1))

        up = around_corner(slab_ref[comp, SLAB - 8 : SLAB, :], above_rim[comp][SLAB - 8 : SLAB, :])
        down = around_corner(below[comp][:, 0:cols], below[comp][:, right])
        packed_up = up if comp == 0 else jnp.where(lanes >= 12 * comp, up, packed_up)
        packed_down = down if comp == 0 else jnp.where(lanes >= 12 * comp, down, packed_down)
    corners = jnp.concatenate([packed_down, jnp.ones((LANES - 16, LANES), jnp.float32), packed_up], axis=0).T
    for comp in range(3):
        corners_ref[comp][0:12, :] = corners[12 * comp : 12 * comp + 12, :]
        corners_ref[comp][12:16, :] = edge_ref[comp, 12:16, :]
    phases = []
    for x in range(2):
        phases.append([])
        for y in range(2):
            cells = []
            for comp, turned in ((0, 0), (1, 2), (2, 1)):
                by_row = columns[comp][y, pl.ds(x, 8, stride=2), :]
                own = edge_ref[turned, pl.ds(x, 8, stride=2), :]
                outer = corners_ref[turned][pl.ds(x, 8, stride=2), :]
                cells.append(jnp.concatenate([by_row, every_other(own, outer, y)], axis=0))
            phases[-1].append(cells)
    return phases


def put_edges(error, edges):
    half_rows = error.shape[0]
    turned = jnp.concatenate([edges, jnp.zeros((LANES - 16, LANES), jnp.float32)], axis=0).T[0:half_rows]
    lanes, ids = lane_ids(half_rows), row_ids(half_rows)
    error = jnp.where(ids == 0, edges[1:2], jnp.where(ids == half_rows - 1, edges[4:5], error))
    return jnp.where(
        lanes == 0, roll(turned, -9, 1), jnp.where(lanes == LANES - 1, roll(turned, LANES - 13, 1), error)
    )


def minmod(lower_diff, upper_diff):
    smaller, larger = jnp.minimum(lower_diff, upper_diff), jnp.maximum(lower_diff, upper_diff)
    return jnp.maximum(smaller, jnp.minimum(larger, 0.0))


def axis_terms(cells, axis):
    depth, normal, tangent = cells[0], cells[1 + axis], cells[2 - axis]
    inverse_root = lax.rsqrt(depth)
    velocity = normal * (inverse_root * inverse_root)
    along = normal * velocity + 0.5 * depth * depth
    beside = tangent * velocity
    speed = jnp.abs(velocity) + depth * inverse_root
    return (normal, along, beside, speed) if axis == 0 else (normal, beside, along, speed)


def paired_change(near, far, axis):
    down = lambda v: roll(v, 1, axis)
    up = lambda v: roll(v, -1, axis)
    inner = [f - n for n, f in zip(near, far)]
    outer = [n - down(f) for n, f in zip(near, far)]
    near_half = [0.5 * minmod(o, i) for o, i in zip(outer, inner)]
    far_half = [0.5 * minmod(i, up(o)) for o, i in zip(outer, inner)]
    near_hi = [n + s for n, s in zip(near, near_half)]
    near_lo = [n - s for n, s in zip(near, near_half)]
    far_hi = [down(f + s) for f, s in zip(far, far_half)]
    far_lo = [f - s for f, s in zip(far, far_half)]
    terms = lambda cells: axis_terms(cells, axis)
    inner_flux = doubled_flux(near_hi, far_lo, terms(near_hi), terms(far_lo))
    outer_flux = doubled_flux(far_hi, near_lo, terms(far_hi), terms(near_lo))
    near_change = [i - o for i, o in zip(inner_flux, outer_flux)]
    far_change = [up(o) - i for i, o in zip(inner_flux, outer_flux)]
    return near_change, far_change


def doubled_first_step(cells):
    all_terms = cell_terms(*cells)
    changes = []
    for axis in (0, 1):
        terms = all_terms[axis]
        lower = [roll(f, 1, axis) for f in cells]
        lower_terms = [lower[1 + axis] if c == 0 else roll(terms[c], 1, axis) for c in range(4)]
        flux = doubled_flux(lower, cells, lower_terms, terms)
        own = [2.0 * terms[c] for c in range(3)]
        changes.append(
            (
                [o - f for o, f in zip(own, flux)],
                [roll(f, -1, axis) - o for o, f in zip(own, flux)],
            )
        )
    rows, cols = changes
    return [
        [
            [cells[c] - (0.5 * RATIO) * (rows[a][c] + cols[b][c]) for c in range(3)]
            for b in range(2)
        ]
        for a in range(2)
    ]


def patch_rows(cells, size):
    half = doubled_first_step(cells)
    by_row = [paired_change(half[0][b], half[1][b], 0) for b in range(2)]
    by_col = [paired_change(half[a][0], half[a][1], 1) for a in range(2)]
    lanes = lane_ids(size)
    result = []
    for a in range(2):
        fine = [
            [half[a][b][c] - (0.5 * RATIO) * (by_row[b][a][c] + by_col[a][b][c]) for c in range(3)]
            for b in range(2)
        ]
        parts = []
        for c in range(3):
            pick = lanes // 2 + 2
            even = jnp.take_along_axis(fine[0][c][0:size], pick, axis=1)
            odd = jnp.take_along_axis(fine[1][c][0:size], pick, axis=1)
            parts.append(jnp.where(lanes % 2 == 0, even, odd))
        result.append(parts)
    return result


def sliding(load, start, size):
    group, shift = start // 8, start % 8
    turn = (8 - shift) % 8
    parts = [pltpu.roll(load(group + k), turn, 0) for k in range(size // 8 + 1)]
    keep = row_ids(8, parts[0].shape[1]) < 8 - shift
    return [jnp.where(keep, parts[k], parts[k + 1]) for k in range(size // 8)]


def scalar(values, row, lane):
    return values[row, lane].astype(jnp.int32)


def slab_rows(ref, first, count, size):
    last = SLAB // 8 - 1
    load = lambda k: ref[pl.ds(pl.multiple_of(first + 8 * jnp.minimum(k, last), 8), 8), :]
    return sliding(load, SLAB - count, size)


def column_move(first_cols, last_cols, side, here, right_count):
    lanes = lane_ids(8)
    head = jnp.where(lanes < here, pltpu.roll(side, here, 1), first_cols)
    outer = jnp.where(lanes < right_count, pltpu.roll(last_cols, right_count, 1), side)
    return head, jnp.where(lanes >= LANES // 2, side, outer)


def move_rows(state_ref, rim_ref, slab_ref, wide_ref):
    rows, cols = state_ref.shape[1], state_ref.shape[2]
    counts = rim_ref[0, 0:8, :]
    rc, cc, cc_right = [scalar(counts, 0, k) for k in (OWN_ROWS, OWN_COLS, RIGHT_COLS)]
    for comp in range(3):
        bodies = slab_rows(slab_ref.at[comp], 0, rc, SLAB)
        for k in range(rows // 8):
            part, at = slice(8 * k, 8 * k + 8), slice(8 * k + 8, 8 * k + 16)
            body = state_ref[comp, part, :]
            if 8 * k < SLAB:
                body = jnp.where(row_ids(8, cols) + 8 * k < rc, bodies[k], body)
                wide_ref[comp, at, LANES : LANES + cols] = body
                continue
            head, outer = column_move(
                body[:, 0:LANES], body[:, cols - LANES : cols], rim_ref[comp, part, :], cc, cc_right
            )
            wide_ref[comp, at, 0:LANES] = outer
            wide_ref[comp, at, LANES : 2 * LANES] = head
            wide_ref[comp, at, 2 * LANES : LANES + cols] = body[:, LANES:cols]
            wide_ref[comp, at, LANES + cols : 2 * LANES + cols] = outer


def finish(
    state_ref, rim_ref, slab_ref, rows_ref, within_ref, across_ref, upper_ref, lower_ref, edge_ref, numbers_ref,
    error_out, moved_out, patch_out,
    wide, window, near_rows, columns, corners, above_rim, below, patch, error, sems,
):
    rows, cols = state_ref.shape[1], state_ref.shape[2]
    right = slice(cols, cols + LANES)
    inside_wide = slice(LANES, LANES + cols)
    on_left = lane_ids(8) >= LANES // 2
    copies = [
        pltpu.make_async_copy(rows_ref.at[:, SLAB + 8 : rows + 8, inside_wide], moved_out.at[:, SLAB:rows, :], sems.at[0])
    ]
    copies[-1].start()

    odd = is_odd()
    packed_half = SLAB // 2
    beside = jnp.where(odd, within_ref[DOWN_ROWS - 8 : DOWN_ROWS, :], across_ref[DOWN_ROWS - 8 : DOWN_ROWS, :])
    turned = jnp.concatenate([beside, jnp.zeros((LANES - 8, LANES), jnp.float32)], axis=0).T[rows - SLAB : rows]
    lanes = lane_ids(packed_half)
    tiles = cols // LANES + 1
    for comp in range(3):
        at = slice(comp * packed_half, (comp + 1) * packed_half)
        packed = jnp.where(odd, within_ref[at, :], across_ref[at, :])
        inner = turned if comp == 0 else roll(turned, -2 * comp, 1)
        upper = jnp.where(lanes >= LANES // 2, roll(packed, LANES // 2, 1), inner[0:packed_half])
        lower = jnp.where(lanes >= LANES // 2, packed, inner[packed_half:SLAB])
        above_rim[comp][0:packed_half, :] = upper
        above_rim[comp][packed_half:SLAB, :] = lower
        for t in range(tiles):
            at = slice(8 * (comp * tiles + t), 8 * (comp * tiles + t) + 8)
            below[comp][:, LANES * t : LANES * (t + 1)] = jnp.where(odd, across_ref[at, :], within_ref[at, :])

    edges = coarse_error(
        edge_phases(state_ref, slab_ref, above_rim, below, edge_ref, near_rows, columns, corners)
    )
    error[...] = put_edges(jnp.concatenate([upper_ref[...], lower_ref[...]], axis=0), edges)

    own_counts, below_counts, numbers = rim_ref[0, 0:8, :], below[0][:, right], numbers_ref[...]
    cc, rc_left, rc_right, cc_right = [
        scalar(own_counts, 0, k) for k in (OWN_COLS, LEFT_ROWS, RIGHT_ROWS, RIGHT_COLS)
    ]
    cc_above, cc_above_right = [scalar(beside, k, 0) for k in (6, 7)]
    rc_below, cc_below, rc_below_left, rc_below_right, cc_below_right = [
        scalar(below_counts, 0, k) for k in (OWN_ROWS, OWN_COLS, LEFT_ROWS, RIGHT_ROWS, RIGHT_COLS)
    ]
    pos_row, pos_col, ext_row, ext_col = [scalar(numbers, k, 0) for k in range(4)]

    def put(comp, at, body, side, here, right_count):
        tail = body[:, LANES:cols]
        head, outer = column_move(body[:, 0:LANES], tail[:, cols - 2 * LANES :], side, here, right_count)
        wide[comp][at : at + 8, 0:LANES] = outer
        wide[comp][at : at + 8, LANES : 2 * LANES] = head
        wide[comp][at : at + 8, 2 * LANES : LANES + cols] = tail
        wide[comp][at : at + 8, LANES + cols : 2 * LANES + cols] = outer

    def moved_rim(ref, first, left, right_count, size):
        from_left = slab_rows(ref, first, left, size)
        from_right = slab_rows(ref, first, right_count, size)
        return [jnp.where(on_left, a, b) for a, b in zip(from_left, from_right)]

    for comp in range(3):
        sides = moved_rim(above_rim[comp], 0, rc_left, rc_right, SLAB)
        for k in range(SLAB // 8):
            side = rim_ref[comp, 8 * k : 8 * k + 8, :]
            side = jnp.where(row_ids(8) + 8 * k < jnp.where(on_left, rc_left, rc_right), sides[k], side)
            put(comp, 8 * k + 8, rows_ref[comp, 8 * k + 8 : 8 * k + 16, inside_wide], side, cc, cc_right)
        wide[comp][SLAB + 8 : rows + 8, :] = rows_ref[comp, SLAB + 8 : rows + 8, :]
        put(comp, 0, slab_ref[comp, SLAB - 8 : SLAB, :], above_rim[comp][SLAB - 8 : SLAB, :], cc_above, cc_above_right)
        (body,) = slab_rows(state_ref.at[comp], rows - SLAB, rc_below, 8)
        (side,) = moved_rim(rim_ref.at[comp], rows - SLAB, rc_below_left, rc_below_right, 8)
        body = jnp.where(row_ids(8, cols) < rc_below, body, below[comp][:, 0:cols])
        side = jnp.where(
            row_ids(8) < jnp.where(on_left, rc_below_left, rc_below_right), side, below[comp][:, right]
        )
        put(comp, rows + 8, body, side, cc_below, cc_below_right)
    copies.append(pltpu.make_async_copy(error, error_out, sems.at[1]))
    copies += [
        pltpu.make_async_copy(wide[c].at[8 : SLAB + 8, inside_wide], moved_out.at[c, 0:SLAB, :], sems.at[2 + c])
        for c in range(3)
    ]

    first_lane = pos_col + LANES - 2
    tile, shift = first_lane // LANES, first_lane % LANES
    turn = (LANES - shift) % LANES
    keep = lane_ids(8) < LANES - shift
    for comp in range(3):

        def load(k):
            group = pl.ds(pl.multiple_of(8 * jnp.minimum(k, rows // 8 + 1), 8), 8)
            near = wide[comp][group, pl.ds(pl.multiple_of(LANES * tile, LANES), LANES)]
            far = wide[comp][group, pl.ds(pl.multiple_of(LANES * tile + LANES, LANES), LANES)]
            return jnp.where(keep, pltpu.roll(near, turn, 1), pltpu.roll(far, turn, 1))

        parts = sliding(load, pos_row + 8, PATCH + 8)
        (above,) = sliding(load, pos_row, 8)
        parts[-1] = jnp.where(row_ids(8) < 4, parts[-1], above)
        for k, part in enumerate(parts):
            window[comp][8 * k : 8 * k + 8, :] = part

    fine_rows, fine_cols = 2 * ext_row, 2 * ext_col
    fine = patch_rows([window[c][...] for c in range(3)], PATCH)
    lanes, ids = lane_ids(PATCH), row_ids(PATCH)
    for a in range(2):
        inside = (2 * ids + a < fine_rows) & (lanes < fine_cols)
        for c in range(3):
            patch[c][pl.ds(a, PATCH, stride=2), :] = jnp.where(inside, fine[a][c], 0.0)
    for c in range(3):
        copies.append(pltpu.make_async_copy(patch[c], patch_out.at[c], sems.at[5 + c]))
        copies[-1].start()
    for copy in copies[1:5]:
        copy.start()
    for copy in copies:
        copy.wait()


def around(axis, by):
    devices = lax.axis_size(axis)
    return [(i, (i + by) % devices) for i in range(devices)]


def in_vmem(value):
    return pltpu.with_memory_space_constraint(value, pltpu.VMEM)


def in_hbm(value):
    return pltpu.with_memory_space_constraint(value, pltpu.HBM)


def vmem(*shape):
    return pltpu.VMEM(shape, jnp.float32)


def per_device(state, row_count, col_count, patch_pos, patch_ext):
    rows, cols = state.shape[1], state.shape[2]
    width = cols + LANES
    half = rows // 2
    here = in_vmem(state)
    ahead = pl.pallas_call(
        blank,
        out_shape=vmem(8, LANES),
        out_specs=VMEM,
        cost_estimate=pl.CostEstimate(flops=10_000_000_000, bytes_accessed=10_000_000, transcendentals=0),
        name="ahead",
    )()
    to_right, strip, slab = pl.pallas_call(
        pack_cols,
        out_shape=(vmem(3 * half + 8, LANES), vmem(32, LANES), vmem(3, SLAB, cols)),
        in_specs=[SMEM, VMEM, VMEM],
        out_specs=(VMEM,) * 3,
        name="pack_cols",
    )(row_count, in_vmem(ahead), here)
    strip = in_vmem(strip)
    to_left, counts = pl.pallas_call(
        pack_right, out_shape=(vmem(8, LANES), vmem(8, LANES)), in_specs=[SMEM, VMEM], out_specs=(VMEM,) * 2, name="pack_right"
    )(col_count, strip)
    from_left = in_vmem(lax.ppermute(to_right, "col", around("col", 1)))
    from_right = in_vmem(lax.ppermute(to_left, "col", around("col", -1)))
    slab_above = in_vmem(lax.ppermute(slab, "row", around("row", 1)))
    upper = in_vmem(pl.pallas_call(
        upper_error,
        out_shape=vmem(UPPER, cols // 2),
        in_specs=[VMEM],
        out_specs=VMEM,
        scratch_shapes=[vmem(3, 2, 2 * UPPER + 16, LANES)],
        cost_estimate=pl.CostEstimate(flops=15_000_000, bytes_accessed=300_000, transcendentals=0),
        name="upper_error",
    )(here))
    rim, within, across, edge = pl.pallas_call(
        pack_rows,
        out_shape=(vmem(3, rows, LANES), vmem(DOWN_ROWS, LANES), vmem(DOWN_ROWS + 8, LANES), vmem(3, 16, LANES)),
        in_specs=[VMEM] * 6,
        out_specs=(VMEM,) * 4,
        cost_estimate=pl.CostEstimate(flops=3_000_000_000, bytes_accessed=600_000, transcendentals=0),
        name="pack_rows",
    )(in_vmem(counts), strip, from_left, from_right, here, upper)
    rim = in_vmem(rim)
    lower, numbers = pl.pallas_call(
        lower_error,
        out_shape=(vmem(half - UPPER, cols // 2), vmem(8, LANES)),
        in_specs=[ANY, ANY, VMEM, VMEM],
        out_specs=(VMEM,) * 2,
        scratch_shapes=[
            vmem(3, 2, 2 * (half - UPPER) + 16, LANES),
            pltpu.VMEM(patch_pos.shape, jnp.int32),
            pltpu.VMEM(patch_ext.shape, jnp.int32),
            pltpu.SemaphoreType.DMA((2,)),
        ],
        cost_estimate=pl.CostEstimate(flops=15_000_000, bytes_accessed=300_000, transcendentals=0),
        name="lower_error",
    )(in_hbm(patch_pos), in_hbm(patch_ext), here, rim)
    devices = lax.axis_size("row")
    from_within = in_vmem(lax.ppermute(within, "row", [(i, i ^ 1) for i in range(devices)]))
    from_across = in_vmem(
        lax.ppermute(across, "row", [(i, (i + (1 if i % 2 else -1)) % devices) for i in range(devices)])
    )
    moved_rows = in_vmem(pl.pallas_call(
        move_rows,
        out_shape=vmem(3, rows + 16, width + LANES),
        in_specs=[VMEM] * 3,
        out_specs=VMEM,
        cost_estimate=pl.CostEstimate(flops=3_000_000, bytes_accessed=1_000_000, transcendentals=0),
        name="move_rows",
    )(here, rim, slab_above))
    return pl.pallas_call(
        finish,
        out_shape=(f32(half, cols // 2), f32(3, rows, cols), f32(3, 2 * PATCH, 2 * PATCH)),
        in_specs=[VMEM] * 10,
        out_specs=(ANY,) * 3,
        scratch_shapes=[
            [vmem(rows + 16, width + LANES)] * 3,
            [vmem(PATCH + 8, LANES)] * 3,
            [vmem(16, cols)] * 3,
            [vmem(2, 16, LANES)] * 3,
            [vmem(16, LANES)] * 3,
            [vmem(SLAB, LANES)] * 3,
            [vmem(8, width)] * 3,
            [vmem(2 * PATCH, 2 * PATCH)] * 3,
            vmem(half, cols // 2),
            pltpu.SemaphoreType.DMA((8,)),
        ],
        compiler_params=PARAMS,
        name="finish",
    )(here, rim, slab_above, moved_rows, from_within, from_across, upper, lower, edge, numbers)


def solution(mesh):
    placed = (
        P(None, "row", "col"),
        P("row", "col"),
        P("row", "col"),
        P("row", "col", None),
        P("row", "col", None),
    )
    return jax.shard_map(
        per_device,
        mesh=mesh,
        in_specs=placed,
        out_specs=(P("row", "col"), P(None, "row", "col"), P(None, "row", "col")),
        check_vma=False,
    )
```

```python
import jax
import jax.numpy as jnp
from jax import lax
from jax.experimental import pallas as pl
from jax.experimental.pallas import tpu as pltpu
from jax.sharding import PartitionSpec as P

SLAB = 64
PATCH = 64
LANES = 128
UPPER = 32

RATIO = 0.1
ERR_SCALE = 10.0

RIGHT_ROWS, RIGHT_COLS, LEFT_ROWS, OWN_ROWS, OWN_COLS = 6, 7, 8, 10, 11
DOWN_ROWS = 3 * SLAB // 2 + 8

VMEM = pl.BlockSpec(memory_space=pltpu.VMEM)
SMEM = pl.BlockSpec(memory_space=pltpu.SMEM)
ANY = pl.BlockSpec(memory_space=pl.ANY)
PARAMS = pltpu.CompilerParams(vmem_limit_bytes=32 * 1024 * 1024)


def f32(*shape):
    return jax.ShapeDtypeStruct(shape, jnp.float32)


def lane_ids(rows, width=LANES):
    return lax.broadcasted_iota(jnp.int32, (rows, width), 1)


def row_ids(rows, width=LANES):
    return lax.broadcasted_iota(jnp.int32, (rows, width), 0)


def roll(value, by, axis):
    return pltpu.roll(value, by % value.shape[axis], axis)


def cell_terms(depth, first, second):
    inverse_root = lax.rsqrt(depth)
    wave = depth * inverse_root
    inverse = inverse_root * inverse_root
    first_vel = first * inverse
    second_vel = second * inverse
    pressure = 0.5 * depth * depth
    cross = first * second_vel
    row_terms = (first, first * first_vel + pressure, cross, jnp.abs(first_vel) + wave)
    col_terms = (second, cross, second * second_vel + pressure, jnp.abs(second_vel) + wave)
    return row_terms, col_terms


def doubled_flux(left, right, left_terms, right_terms):
    speed = jnp.maximum(left_terms[3], right_terms[3])
    return [(left_terms[c] + right_terms[c]) - speed * (right[c] - left[c]) for c in range(3)]


def spread_step(fields, row_by, col_by):
    row_terms, col_terms = cell_terms(*fields)
    total = None
    for terms, by, axis in ((row_terms, row_by, 0), (col_terms, col_by, 1)):
        lower = [roll(f, by, axis) for f in fields]
        momentum = lower[1 + axis]
        lower_terms = [momentum if c == 0 else roll(terms[c], by, axis) for c in range(4)]
        flux = doubled_flux(lower, fields, lower_terms, terms)
        change = [roll(f, -by, axis) - f for f in flux]
        total = change if total is None else [t + c for t, c in zip(total, change)]
    return [f - (0.5 * RATIO) * t for f, t in zip(fields, total)]


def pair_change(near, far, near_terms, far_terms, axis):
    inner = doubled_flux(near, far, near_terms, far_terms)
    before = [roll(f, 1, axis) for f in far]
    before_terms = [before[1 + axis] if c == 0 else roll(far_terms[c], 1, axis) for c in range(4)]
    outer = doubled_flux(before, near, before_terms, near_terms)
    near_change = [i - o for i, o in zip(inner, outer)]
    far_change = [roll(o, -1, axis) - i for i, o in zip(inner, outer)]
    return near_change, far_change


def paired_step(phases):
    terms = [[cell_terms(*phases[x][y]) for y in range(2)] for x in range(2)]
    along_first = [
        pair_change(phases[0][y], phases[1][y], terms[0][y][0], terms[1][y][0], 0) for y in range(2)
    ]
    along_second = [
        pair_change(phases[x][0], phases[x][1], terms[x][0][1], terms[x][1][1], 1) for x in range(2)
    ]
    return [
        [
            [
                phases[x][y][c] - (0.5 * RATIO) * (along_first[y][x][c] + along_second[x][y][c])
                for c in range(3)
            ]
            for y in range(2)
        ]
        for x in range(2)
    ]


def block_mean(phases):
    return [
        0.25 * ((phases[0][0][c] + phases[1][0][c]) + (phases[0][1][c] + phases[1][1][c])) for c in range(3)
    ]


def coarse_error(phases):
    fine = block_mean(paired_step(paired_step(phases)))
    coarse = spread_step(block_mean(phases), 1, 1)
    parts = [jnp.abs(f - c) for f, c in zip(fine, coarse)]
    return ERR_SCALE * ((parts[0] + parts[1]) + parts[2])


def every_other(first, second, parity):
    lanes = lane_ids(first.shape[0])
    pick = (2 * lanes + parity) % LANES
    low = jnp.take_along_axis(first, pick, axis=1)
    high = jnp.take_along_axis(second, pick, axis=1)
    return jnp.where(lanes < LANES // 2, low, high)


def blank(out_ref):
    out_ref[...] = jnp.zeros(out_ref.shape, jnp.float32)


def pack_cols(row_count, blank_ref, state_ref, left_ref, strip_ref, slab_ref):
    rows, cols = state_ref.shape[1], state_ref.shape[2]
    half = rows // 2
    rc = row_count[0, 0].astype(jnp.float32)
    lanes = lane_ids(half)
    for comp in range(3):
        upper = state_ref[comp, 0:half, cols - LANES : cols]
        lower = roll(state_ref[comp, half:rows, cols - LANES : cols], LANES // 2, 1)
        left_ref[comp * half : (comp + 1) * half, :] = jnp.where(lanes >= LANES // 2, upper, lower)
    lanes = lane_ids(rows)
    packed = None
    for comp in range(3):
        ends = jnp.where(lanes < LANES // 2, state_ref[comp, :, 0:LANES], state_ref[comp, :, cols - LANES : cols])
        ends = roll(ends, 8 * comp + 4, 1)
        packed = ends if packed is None else jnp.where(lanes >= 8 * comp, ends, packed)
    strip_ref[0:24, :] = packed.T[0:24]
    strip_ref[24:32, :] = jnp.full((8, LANES), rc)
    left_ref[3 * half : 3 * half + 8, :] = jnp.full((8, LANES), rc)
    for comp in range(3):
        left_ref[3 * half + 2 * comp : 3 * half + 2 * comp + 2, :] = strip_ref[8 * comp + 2 : 8 * comp + 4, :]
    slab_ref[...] = state_ref[:, rows - SLAB : rows, :]


def pack_right(col_count, strip_ref, right_ref, counts_ref):
    cc = col_count[0, 0].astype(jnp.float32)
    counts = jnp.where(row_ids(8) == 6, strip_ref[24:32, :], cc)
    counts_ref[...] = counts
    right_ref[...] = counts
    for comp in range(3):
        right_ref[2 * comp : 2 * comp + 2, :] = strip_ref[8 * comp + 4 : 8 * comp + 6, :]


def is_odd():
    return lax.axis_index("row") % 2 == 1


def pack_rows(counts_ref, strip_ref, left_ref, right_ref, state_ref, upper_ref, rim_ref, within_ref, across_ref, edge_ref):
    rows, cols = state_ref.shape[1], state_ref.shape[2]
    half = rows // 2
    rc, cc = counts_ref[6:7, :], counts_ref[7:8, :]
    right = jnp.concatenate([right_ref[...], jnp.zeros((LANES - 8, LANES), jnp.float32)], axis=0).T
    lanes = lane_ids(rows)
    left_rc = left_ref[3 * half + 6 : 3 * half + 7, :]
    counts = jnp.where(lanes == LEFT_ROWS, left_rc, jnp.where(lanes == OWN_ROWS, rc, cc))
    odd = is_odd()
    packed_half = SLAB // 2
    low = lane_ids(packed_half) < LANES // 2

    def put(at, down, up):
        size = down.shape[0]
        within_ref[at : at + size, :] = jnp.where(odd, up, down)
        across_ref[at : at + size, :] = jnp.where(odd, down, up)

    ups, downs = [], []
    for comp in range(3):
        packed = left_ref[comp * half : (comp + 1) * half, :]
        left = jnp.concatenate([packed, roll(packed, LANES // 2, 1)], axis=0)
        inner = right if comp == 0 else roll(right, -2 * comp, 1)
        inner = jnp.where(lanes < LEFT_ROWS, inner, counts)
        rim = jnp.where(lanes >= LANES // 2, left, inner)
        rim_ref[comp] = rim
        last = packed[half - SLAB : half]
        downs.append(jnp.where(low, last[0:packed_half], roll(last[packed_half:SLAB], LANES // 2, 1)))
        ups += [state_ref[comp, 0:8, LANES * t : LANES * (t + 1)] for t in range(cols // LANES)] + [rim[0:8]]
        edge_ref[comp, 0:2, :] = left_ref[3 * half + 2 * comp : 3 * half + 2 * comp + 2, :]
        edge_ref[comp, 2:6, :] = strip_ref[8 * comp + 4 : 8 * comp + 8, :]
        edge_ref[comp, 6:10, :] = strip_ref[8 * comp : 8 * comp + 4, :]
        edge_ref[comp, 10:12, :] = right_ref[2 * comp : 2 * comp + 2, :]
        edge_ref[comp, 12:16, :] = strip_ref[8 * comp + 4 : 8 * comp + 8, :]
    last_row = jnp.where(lane_ids(8) < LANES // 2, cc, right_ref[7:8, :])
    downs.append(jnp.where(row_ids(8) >= 6, last_row, right_ref[...]))
    down = jnp.concatenate(downs, axis=0)
    up = jnp.concatenate(ups, axis=0)
    size = up.shape[0]
    put(0, down[0:size], up)
    across_ref[size:DOWN_ROWS, :] = down[size:DOWN_ROWS]
    within_ref[size : DOWN_ROWS - 1, :] = down[size : DOWN_ROWS - 1]


def inner_error(state_ref, first, size, columns):
    part = slice(2 * first, 2 * (first + size))
    for comp in range(3):
        left, right = state_ref[comp, part, 0:LANES], state_ref[comp, part, LANES : 2 * LANES]
        for parity in range(2):
            columns[comp, parity] = every_other(left, right, parity)
    phases = [
        [[columns[c, y, pl.ds(x, size, stride=2), :] for c in range(3)] for y in range(2)]
        for x in range(2)
    ]
    return coarse_error(phases)


def upper_error(state_ref, error_ref, columns):
    rows = error_ref.shape[0]
    error_ref[...] = inner_error(state_ref, 0, rows + 8, columns)[0:rows]


def lower_error(pos_ref, ext_ref, state_ref, rim_ref, error_ref, numbers_ref, columns, pos, ext, sems):
    copies = [pltpu.make_async_copy(src, dst, sems.at[k]) for k, (src, dst) in enumerate(((pos_ref, pos), (ext_ref, ext)))]
    for copy in copies:
        copy.start()
    rows = error_ref.shape[0]
    error_ref[...] = inner_error(state_ref, state_ref.shape[1] // 2 - rows - 8, rows + 8, columns)[8 : rows + 8]
    for copy in copies:
        copy.wait()
    pair = [v[0].astype(jnp.float32) for v in (pos, ext)]
    numbers = jnp.broadcast_to(pair[1][:, 1:2], (8, LANES))
    for k, number in enumerate((pair[0][:, 0:1], pair[0][:, 1:2], pair[1][:, 0:1])):
        numbers = jnp.where(row_ids(8) == k, number, numbers)
    numbers_ref[...] = numbers


def edge_phases(state_ref, slab_ref, above_rim, below, edge_ref, near_rows, columns, corners_ref):
    rows, cols = state_ref.shape[1], state_ref.shape[2]
    right = slice(cols, cols + LANES)
    lanes = lane_ids(8)
    packed_up, packed_down = None, None
    for comp in range(3):
        near_rows[comp][0:2, :] = slab_ref[comp, SLAB - 2 : SLAB, :]
        near_rows[comp][2:6, :] = state_ref[comp, 0:4, :]
        near_rows[comp][6:10, :] = state_ref[comp, rows - 4 : rows, :]
        near_rows[comp][10:12, :] = below[comp][0:2, 0:cols]
        near_rows[comp][12:16, :] = state_ref[comp, 0:4, :]
        first, second = near_rows[comp][:, 0:LANES], near_rows[comp][:, LANES : 2 * LANES]
        for parity in range(2):
            columns[comp][parity] = every_other(first, second, parity)

        def around_corner(body, rim):
            start = jnp.where(lanes < LANES // 2, body[:, 0:LANES], rim)
            end = jnp.where(lanes < LANES // 2, rim, body[:, cols - LANES : cols])
            first_six = (lanes >= 12 * comp) & (lanes < 12 * comp + 6)
            return jnp.where(first_six, roll(start, 12 * comp + 2, 1), roll(end, 12 * comp + 10, 1))

        up = around_corner(slab_ref[comp, SLAB - 8 : SLAB, :], above_rim[comp][SLAB - 8 : SLAB, :])
        down = around_corner(below[comp][:, 0:cols], below[comp][:, right])
        packed_up = up if comp == 0 else jnp.where(lanes >= 12 * comp, up, packed_up)
        packed_down = down if comp == 0 else jnp.where(lanes >= 12 * comp, down, packed_down)
    corners = jnp.concatenate([packed_down, jnp.ones((LANES - 16, LANES), jnp.float32), packed_up], axis=0).T
    for comp in range(3):
        corners_ref[comp][0:12, :] = corners[12 * comp : 12 * comp + 12, :]
        corners_ref[comp][12:16, :] = edge_ref[comp, 12:16, :]
    phases = []
    for x in range(2):
        phases.append([])
        for y in range(2):
            cells = []
            for comp, turned in ((0, 0), (1, 2), (2, 1)):
                by_row = columns[comp][y, pl.ds(x, 8, stride=2), :]
                own = edge_ref[turned, pl.ds(x, 8, stride=2), :]
                outer = corners_ref[turned][pl.ds(x, 8, stride=2), :]
                cells.append(jnp.concatenate([by_row, every_other(own, outer, y)], axis=0))
            phases[-1].append(cells)
    return phases


def put_edges(error, edges):
    half_rows = error.shape[0]
    turned = jnp.concatenate([edges, jnp.zeros((LANES - 16, LANES), jnp.float32)], axis=0).T[0:half_rows]
    lanes, ids = lane_ids(half_rows), row_ids(half_rows)
    error = jnp.where(ids == 0, edges[1:2], jnp.where(ids == half_rows - 1, edges[4:5], error))
    return jnp.where(
        lanes == 0, roll(turned, -9, 1), jnp.where(lanes == LANES - 1, roll(turned, LANES - 13, 1), error)
    )


def minmod(lower_diff, upper_diff):
    smaller, larger = jnp.minimum(lower_diff, upper_diff), jnp.maximum(lower_diff, upper_diff)
    return jnp.maximum(smaller, jnp.minimum(larger, 0.0))


def axis_terms(cells, axis):
    depth, normal, tangent = cells[0], cells[1 + axis], cells[2 - axis]
    inverse_root = lax.rsqrt(depth)
    velocity = normal * (inverse_root * inverse_root)
    along = normal * velocity + 0.5 * depth * depth
    beside = tangent * velocity
    speed = jnp.abs(velocity) + depth * inverse_root
    return (normal, along, beside, speed) if axis == 0 else (normal, beside, along, speed)


def paired_change(near, far, axis):
    down = lambda v: roll(v, 1, axis)
    up = lambda v: roll(v, -1, axis)
    inner = [f - n for n, f in zip(near, far)]
    outer = [n - down(f) for n, f in zip(near, far)]
    near_half = [0.5 * minmod(o, i) for o, i in zip(outer, inner)]
    far_half = [0.5 * minmod(i, up(o)) for o, i in zip(outer, inner)]
    near_hi = [n + s for n, s in zip(near, near_half)]
    near_lo = [n - s for n, s in zip(near, near_half)]
    far_hi = [down(f + s) for f, s in zip(far, far_half)]
    far_lo = [f - s for f, s in zip(far, far_half)]
    terms = lambda cells: axis_terms(cells, axis)
    inner_flux = doubled_flux(near_hi, far_lo, terms(near_hi), terms(far_lo))
    outer_flux = doubled_flux(far_hi, near_lo, terms(far_hi), terms(near_lo))
    near_change = [i - o for i, o in zip(inner_flux, outer_flux)]
    far_change = [up(o) - i for i, o in zip(inner_flux, outer_flux)]
    return near_change, far_change


def doubled_first_step(cells):
    all_terms = cell_terms(*cells)
    changes = []
    for axis in (0, 1):
        terms = all_terms[axis]
        lower = [roll(f, 1, axis) for f in cells]
        lower_terms = [lower[1 + axis] if c == 0 else roll(terms[c], 1, axis) for c in range(4)]
        flux = doubled_flux(lower, cells, lower_terms, terms)
        own = [2.0 * terms[c] for c in range(3)]
        changes.append(
            (
                [o - f for o, f in zip(own, flux)],
                [roll(f, -1, axis) - o for o, f in zip(own, flux)],
            )
        )
    rows, cols = changes
    return [
        [
            [cells[c] - (0.5 * RATIO) * (rows[a][c] + cols[b][c]) for c in range(3)]
            for b in range(2)
        ]
        for a in range(2)
    ]


def patch_rows(cells, size):
    half = doubled_first_step(cells)
    by_row = [paired_change(half[0][b], half[1][b], 0) for b in range(2)]
    by_col = [paired_change(half[a][0], half[a][1], 1) for a in range(2)]
    lanes = lane_ids(size)
    result = []
    for a in range(2):
        fine = [
            [half[a][b][c] - (0.5 * RATIO) * (by_row[b][a][c] + by_col[a][b][c]) for c in range(3)]
            for b in range(2)
        ]
        parts = []
        for c in range(3):
            pick = lanes // 2 + 2
            even = jnp.take_along_axis(fine[0][c][0:size], pick, axis=1)
            odd = jnp.take_along_axis(fine[1][c][0:size], pick, axis=1)
            parts.append(jnp.where(lanes % 2 == 0, even, odd))
        result.append(parts)
    return result


def sliding(load, start, size):
    group, shift = start // 8, start % 8
    turn = (8 - shift) % 8
    parts = [pltpu.roll(load(group + k), turn, 0) for k in range(size // 8 + 1)]
    keep = row_ids(8, parts[0].shape[1]) < 8 - shift
    return [jnp.where(keep, parts[k], parts[k + 1]) for k in range(size // 8)]


def scalar(values, row, lane):
    return values[row, lane].astype(jnp.int32)


def slab_rows(ref, first, count, size):
    last = SLAB // 8 - 1
    load = lambda k: ref[pl.ds(pl.multiple_of(first + 8 * jnp.minimum(k, last), 8), 8), :]
    return sliding(load, SLAB - count, size)


def column_move(first_cols, last_cols, side, here, right_count):
    lanes = lane_ids(8)
    head = jnp.where(lanes < here, pltpu.roll(side, here, 1), first_cols)
    outer = jnp.where(lanes < right_count, pltpu.roll(last_cols, right_count, 1), side)
    return head, jnp.where(lanes >= LANES // 2, side, outer)


def move_rows(state_ref, rim_ref, slab_ref, wide_ref):
    rows, cols = state_ref.shape[1], state_ref.shape[2]
    counts = rim_ref[0, 0:8, :]
    rc, cc, cc_right = [scalar(counts, 0, k) for k in (OWN_ROWS, OWN_COLS, RIGHT_COLS)]
    for comp in range(3):
        bodies = slab_rows(slab_ref.at[comp], 0, rc, SLAB)
        for k in range(rows // 8):
            part, at = slice(8 * k, 8 * k + 8), slice(8 * k + 8, 8 * k + 16)
            body = state_ref[comp, part, :]
            if 8 * k < SLAB:
                body = jnp.where(row_ids(8, cols) + 8 * k < rc, bodies[k], body)
                wide_ref[comp, at, LANES : LANES + cols] = body
                continue
            head, outer = column_move(
                body[:, 0:LANES], body[:, cols - LANES : cols], rim_ref[comp, part, :], cc, cc_right
            )
            wide_ref[comp, at, 0:LANES] = outer
            wide_ref[comp, at, LANES : 2 * LANES] = head
            wide_ref[comp, at, 2 * LANES : LANES + cols] = body[:, LANES:cols]
            wide_ref[comp, at, LANES + cols : 2 * LANES + cols] = outer


def finish(
    state_ref, rim_ref, slab_ref, rows_ref, within_ref, across_ref, upper_ref, lower_ref, edge_ref, numbers_ref,
    error_out, moved_out, patch_out,
    wide, window, near_rows, columns, corners, above_rim, below, patch, error, sems,
):
    rows, cols = state_ref.shape[1], state_ref.shape[2]
    right = slice(cols, cols + LANES)
    inside_wide = slice(LANES, LANES + cols)
    on_left = lane_ids(8) >= LANES // 2
    copies = [
        pltpu.make_async_copy(rows_ref.at[:, SLAB + 8 : rows + 8, inside_wide], moved_out.at[:, SLAB:rows, :], sems.at[0])
    ]
    copies[-1].start()

    odd = is_odd()
    packed_half = SLAB // 2
    beside = jnp.where(odd, within_ref[DOWN_ROWS - 8 : DOWN_ROWS - 1, :], across_ref[DOWN_ROWS - 8 : DOWN_ROWS - 1, :])
    turned = jnp.concatenate([beside, jnp.zeros((LANES - 7, LANES), jnp.float32)], axis=0).T[rows - SLAB : rows]
    lanes = lane_ids(packed_half)
    tiles = cols // LANES + 1
    for comp in range(3):
        at = slice(comp * packed_half, (comp + 1) * packed_half)
        packed = jnp.where(odd, within_ref[at, :], across_ref[at, :])
        inner = turned if comp == 0 else roll(turned, -2 * comp, 1)
        upper = jnp.where(lanes >= LANES // 2, roll(packed, LANES // 2, 1), inner[0:packed_half])
        lower = jnp.where(lanes >= LANES // 2, packed, inner[packed_half:SLAB])
        above_rim[comp][0:packed_half, :] = upper
        above_rim[comp][packed_half:SLAB, :] = lower
        for t in range(tiles):
            at = slice(8 * (comp * tiles + t), 8 * (comp * tiles + t) + 8)
            below[comp][:, LANES * t : LANES * (t + 1)] = jnp.where(odd, across_ref[at, :], within_ref[at, :])

    edges = coarse_error(
        edge_phases(state_ref, slab_ref, above_rim, below, edge_ref, near_rows, columns, corners)
    )
    error[...] = put_edges(jnp.concatenate([upper_ref[...], lower_ref[...]], axis=0), edges)

    own_counts, below_counts, numbers = rim_ref[0, 0:8, :], below[0][:, right], numbers_ref[...]
    cc, rc_left, rc_right, cc_right = [
        scalar(own_counts, 0, k) for k in (OWN_COLS, LEFT_ROWS, RIGHT_ROWS, RIGHT_COLS)
    ]
    cc_above, cc_above_right = [scalar(beside, 6, k) for k in (0, LANES - 1)]
    rc_below, cc_below, rc_below_left, rc_below_right, cc_below_right = [
        scalar(below_counts, 0, k) for k in (OWN_ROWS, OWN_COLS, LEFT_ROWS, RIGHT_ROWS, RIGHT_COLS)
    ]
    pos_row, pos_col, ext_row, ext_col = [scalar(numbers, k, 0) for k in range(4)]

    def put(comp, at, body, side, here, right_count):
        tail = body[:, LANES:cols]
        head, outer = column_move(body[:, 0:LANES], tail[:, cols - 2 * LANES :], side, here, right_count)
        wide[comp][at : at + 8, 0:LANES] = outer
        wide[comp][at : at + 8, LANES : 2 * LANES] = head
        wide[comp][at : at + 8, 2 * LANES : LANES + cols] = tail
        wide[comp][at : at + 8, LANES + cols : 2 * LANES + cols] = outer

    def moved_rim(ref, first, left, right_count, size):
        from_left = slab_rows(ref, first, left, size)
        from_right = slab_rows(ref, first, right_count, size)
        return [jnp.where(on_left, a, b) for a, b in zip(from_left, from_right)]

    for comp in range(3):
        sides = moved_rim(above_rim[comp], 0, rc_left, rc_right, SLAB)
        for k in range(SLAB // 8):
            side = rim_ref[comp, 8 * k : 8 * k + 8, :]
            side = jnp.where(row_ids(8) + 8 * k < jnp.where(on_left, rc_left, rc_right), sides[k], side)
            put(comp, 8 * k + 8, rows_ref[comp, 8 * k + 8 : 8 * k + 16, inside_wide], side, cc, cc_right)
        wide[comp][SLAB + 8 : rows + 8, :] = rows_ref[comp, SLAB + 8 : rows + 8, :]
        put(comp, 0, slab_ref[comp, SLAB - 8 : SLAB, :], above_rim[comp][SLAB - 8 : SLAB, :], cc_above, cc_above_right)
        (body,) = slab_rows(state_ref.at[comp], rows - SLAB, rc_below, 8)
        (side,) = moved_rim(rim_ref.at[comp], rows - SLAB, rc_below_left, rc_below_right, 8)
        body = jnp.where(row_ids(8, cols) < rc_below, body, below[comp][:, 0:cols])
        side = jnp.where(
            row_ids(8) < jnp.where(on_left, rc_below_left, rc_below_right), side, below[comp][:, right]
        )
        put(comp, rows + 8, body, side, cc_below, cc_below_right)
    copies.append(pltpu.make_async_copy(error, error_out, sems.at[1]))
    copies += [
        pltpu.make_async_copy(wide[c].at[8 : SLAB + 8, inside_wide], moved_out.at[c, 0:SLAB, :], sems.at[2 + c])
        for c in range(3)
    ]

    first_lane = pos_col + LANES - 2
    tile, shift = first_lane // LANES, first_lane % LANES
    turn = (LANES - shift) % LANES
    keep = lane_ids(8) < LANES - shift
    for comp in range(3):

        def load(k):
            group = pl.ds(pl.multiple_of(8 * jnp.minimum(k, rows // 8 + 1), 8), 8)
            near = wide[comp][group, pl.ds(pl.multiple_of(LANES * tile, LANES), LANES)]
            far = wide[comp][group, pl.ds(pl.multiple_of(LANES * tile + LANES, LANES), LANES)]
            return jnp.where(keep, pltpu.roll(near, turn, 1), pltpu.roll(far, turn, 1))

        parts = sliding(load, pos_row + 8, PATCH + 8)
        (above,) = sliding(load, pos_row, 8)
        parts[-1] = jnp.where(row_ids(8) < 4, parts[-1], above)
        for k, part in enumerate(parts):
            window[comp][8 * k : 8 * k + 8, :] = part

    fine_rows, fine_cols = 2 * ext_row, 2 * ext_col
    fine = patch_rows([window[c][...] for c in range(3)], PATCH)
    lanes, ids = lane_ids(PATCH), row_ids(PATCH)
    for a in range(2):
        inside = (2 * ids + a < fine_rows) & (lanes < fine_cols)
        for c in range(3):
            patch[c][pl.ds(a, PATCH, stride=2), :] = jnp.where(inside, fine[a][c], 0.0)
    for c in range(3):
        copies.append(pltpu.make_async_copy(patch[c], patch_out.at[c], sems.at[5 + c]))
        copies[-1].start()
    for copy in copies[1:5]:
        copy.start()
    for copy in copies:
        copy.wait()


def around(axis, by):
    devices = lax.axis_size(axis)
    return [(i, (i + by) % devices) for i in range(devices)]


def in_vmem(value):
    return pltpu.with_memory_space_constraint(value, pltpu.VMEM)


def in_hbm(value):
    return pltpu.with_memory_space_constraint(value, pltpu.HBM)


def vmem(*shape):
    return pltpu.VMEM(shape, jnp.float32)


def per_device(state, row_count, col_count, patch_pos, patch_ext):
    rows, cols = state.shape[1], state.shape[2]
    width = cols + LANES
    half = rows // 2
    here = in_vmem(state)
    ahead = pl.pallas_call(
        blank,
        out_shape=vmem(8, LANES),
        out_specs=VMEM,
        cost_estimate=pl.CostEstimate(flops=10_000_000_000, bytes_accessed=10_000_000, transcendentals=0),
        name="ahead",
    )()
    to_right, strip, slab = pl.pallas_call(
        pack_cols,
        out_shape=(vmem(3 * half + 8, LANES), vmem(32, LANES), vmem(3, SLAB, cols)),
        in_specs=[SMEM, VMEM, VMEM],
        out_specs=(VMEM,) * 3,
        name="pack_cols",
    )(row_count, in_vmem(ahead), here)
    strip = in_vmem(strip)
    to_left, counts = pl.pallas_call(
        pack_right, out_shape=(vmem(8, LANES), vmem(8, LANES)), in_specs=[SMEM, VMEM], out_specs=(VMEM,) * 2, name="pack_right"
    )(col_count, strip)
    from_left = in_vmem(lax.ppermute(to_right, "col", around("col", 1)))
    from_right = in_vmem(lax.ppermute(to_left, "col", around("col", -1)))
    slab_above = in_vmem(lax.ppermute(slab, "row", around("row", 1)))
    upper = in_vmem(pl.pallas_call(
        upper_error,
        out_shape=vmem(UPPER, cols // 2),
        in_specs=[VMEM],
        out_specs=VMEM,
        scratch_shapes=[vmem(3, 2, 2 * UPPER + 16, LANES)],
        cost_estimate=pl.CostEstimate(flops=15_000_000, bytes_accessed=300_000, transcendentals=0),
        name="upper_error",
    )(here))
    rim, within, across, edge = pl.pallas_call(
        pack_rows,
        out_shape=(vmem(3, rows, LANES), vmem(DOWN_ROWS - 1, LANES), vmem(DOWN_ROWS, LANES), vmem(3, 16, LANES)),
        in_specs=[VMEM] * 6,
        out_specs=(VMEM,) * 4,
        cost_estimate=pl.CostEstimate(flops=3_000_000_000, bytes_accessed=600_000, transcendentals=0),
        name="pack_rows",
    )(in_vmem(counts), strip, from_left, from_right, here, upper)
    rim = in_vmem(rim)
    lower, numbers = pl.pallas_call(
        lower_error,
        out_shape=(vmem(half - UPPER, cols // 2), vmem(8, LANES)),
        in_specs=[ANY, ANY, VMEM, VMEM],
        out_specs=(VMEM,) * 2,
        scratch_shapes=[
            vmem(3, 2, 2 * (half - UPPER) + 16, LANES),
            pltpu.VMEM(patch_pos.shape, jnp.int32),
            pltpu.VMEM(patch_ext.shape, jnp.int32),
            pltpu.SemaphoreType.DMA((2,)),
        ],
        cost_estimate=pl.CostEstimate(flops=15_000_000, bytes_accessed=300_000, transcendentals=0),
        name="lower_error",
    )(in_hbm(patch_pos), in_hbm(patch_ext), here, rim)
    devices = lax.axis_size("row")
    from_within = in_vmem(lax.ppermute(within, "row", [(i, i ^ 1) for i in range(devices)]))
    from_across = in_vmem(
        lax.ppermute(across, "row", [(i, (i + (1 if i % 2 else -1)) % devices) for i in range(devices)])
    )
    moved_rows = in_vmem(pl.pallas_call(
        move_rows,
        out_shape=vmem(3, rows + 16, width + LANES),
        in_specs=[VMEM] * 3,
        out_specs=VMEM,
        cost_estimate=pl.CostEstimate(flops=3_000_000, bytes_accessed=1_000_000, transcendentals=0),
        name="move_rows",
    )(here, rim, slab_above))
    return pl.pallas_call(
        finish,
        out_shape=(f32(half, cols // 2), f32(3, rows, cols), f32(3, 2 * PATCH, 2 * PATCH)),
        in_specs=[VMEM] * 10,
        out_specs=(ANY,) * 3,
        scratch_shapes=[
            [vmem(rows + 16, width + LANES)] * 3,
            [vmem(PATCH + 8, LANES)] * 3,
            [vmem(16, cols)] * 3,
            [vmem(2, 16, LANES)] * 3,
            [vmem(16, LANES)] * 3,
            [vmem(SLAB, LANES)] * 3,
            [vmem(8, width)] * 3,
            [vmem(2 * PATCH, 2 * PATCH)] * 3,
            vmem(half, cols // 2),
            pltpu.SemaphoreType.DMA((8,)),
        ],
        compiler_params=PARAMS,
        name="finish",
    )(here, rim, slab_above, moved_rows, from_within, from_across, upper, lower, edge, numbers)


def solution(mesh):
    placed = (
        P(None, "row", "col"),
        P("row", "col"),
        P("row", "col"),
        P("row", "col", None),
        P("row", "col", None),
    )
    return jax.shard_map(
        per_device,
        mesh=mesh,
        in_specs=placed,
        out_specs=(P("row", "col"), P(None, "row", "col"), P(None, "row", "col")),
        check_vma=False,
    )
```

```python
import jax
import jax.numpy as jnp
from jax import lax
from jax.experimental import pallas as pl
from jax.experimental.pallas import tpu as pltpu
from jax.sharding import PartitionSpec as P

SLAB = 64
PATCH = 64
LANES = 128
UPPER = 32

RATIO = 0.1
ERR_SCALE = 10.0

RIGHT_ROWS, RIGHT_COLS, LEFT_ROWS, OWN_ROWS, OWN_COLS = 6, 7, 8, 10, 11
DOWN_ROWS = 3 * SLAB // 2 + 8

VMEM = pl.BlockSpec(memory_space=pltpu.VMEM)
SMEM = pl.BlockSpec(memory_space=pltpu.SMEM)
ANY = pl.BlockSpec(memory_space=pl.ANY)
PARAMS = pltpu.CompilerParams(vmem_limit_bytes=32 * 1024 * 1024)


def f32(*shape):
    return jax.ShapeDtypeStruct(shape, jnp.float32)


def lane_ids(rows, width=LANES):
    return lax.broadcasted_iota(jnp.int32, (rows, width), 1)


def row_ids(rows, width=LANES):
    return lax.broadcasted_iota(jnp.int32, (rows, width), 0)


def roll(value, by, axis):
    return pltpu.roll(value, by % value.shape[axis], axis)


def cell_terms(depth, first, second):
    inverse_root = lax.rsqrt(depth)
    wave = depth * inverse_root
    inverse = inverse_root * inverse_root
    first_vel = first * inverse
    second_vel = second * inverse
    pressure = 0.5 * depth * depth
    cross = first * second_vel
    row_terms = (first, first * first_vel + pressure, cross, jnp.abs(first_vel) + wave)
    col_terms = (second, cross, second * second_vel + pressure, jnp.abs(second_vel) + wave)
    return row_terms, col_terms


def doubled_flux(left, right, left_terms, right_terms):
    speed = jnp.maximum(left_terms[3], right_terms[3])
    return [(left_terms[c] + right_terms[c]) - speed * (right[c] - left[c]) for c in range(3)]


def spread_step(fields, row_by, col_by):
    row_terms, col_terms = cell_terms(*fields)
    total = None
    for terms, by, axis in ((row_terms, row_by, 0), (col_terms, col_by, 1)):
        lower = [roll(f, by, axis) for f in fields]
        momentum = lower[1 + axis]
        lower_terms = [momentum if c == 0 else roll(terms[c], by, axis) for c in range(4)]
        flux = doubled_flux(lower, fields, lower_terms, terms)
        change = [roll(f, -by, axis) - f for f in flux]
        total = change if total is None else [t + c for t, c in zip(total, change)]
    return [f - (0.5 * RATIO) * t for f, t in zip(fields, total)]


def pair_change(near, far, near_terms, far_terms, axis):
    inner = doubled_flux(near, far, near_terms, far_terms)
    before = [roll(f, 1, axis) for f in far]
    before_terms = [before[1 + axis] if c == 0 else roll(far_terms[c], 1, axis) for c in range(4)]
    outer = doubled_flux(before, near, before_terms, near_terms)
    near_change = [i - o for i, o in zip(inner, outer)]
    far_change = [roll(o, -1, axis) - i for i, o in zip(inner, outer)]
    return near_change, far_change


def paired_step(phases):
    terms = [[cell_terms(*phases[x][y]) for y in range(2)] for x in range(2)]
    along_first = [
        pair_change(phases[0][y], phases[1][y], terms[0][y][0], terms[1][y][0], 0) for y in range(2)
    ]
    along_second = [
        pair_change(phases[x][0], phases[x][1], terms[x][0][1], terms[x][1][1], 1) for x in range(2)
    ]
    return [
        [
            [
                phases[x][y][c] - (0.5 * RATIO) * (along_first[y][x][c] + along_second[x][y][c])
                for c in range(3)
            ]
            for y in range(2)
        ]
        for x in range(2)
    ]


def block_mean(phases):
    return [
        0.25 * ((phases[0][0][c] + phases[1][0][c]) + (phases[0][1][c] + phases[1][1][c])) for c in range(3)
    ]


def coarse_error(phases):
    fine = block_mean(paired_step(paired_step(phases)))
    coarse = spread_step(block_mean(phases), 1, 1)
    parts = [jnp.abs(f - c) for f, c in zip(fine, coarse)]
    return ERR_SCALE * ((parts[0] + parts[1]) + parts[2])


def every_other(first, second, parity):
    lanes = lane_ids(first.shape[0])
    pick = (2 * lanes + parity) % LANES
    low = jnp.take_along_axis(first, pick, axis=1)
    high = jnp.take_along_axis(second, pick, axis=1)
    return jnp.where(lanes < LANES // 2, low, high)


def blank(out_ref):
    out_ref[...] = jnp.zeros(out_ref.shape, jnp.float32)


def pack_cols(row_count, blank_ref, state_ref, left_ref, strip_ref, slab_ref):
    rows, cols = state_ref.shape[1], state_ref.shape[2]
    half = rows // 2
    rc = row_count[0, 0].astype(jnp.float32)
    lanes = lane_ids(half)
    for comp in range(3):
        upper = state_ref[comp, 0:half, cols - LANES : cols]
        lower = roll(state_ref[comp, half:rows, cols - LANES : cols], LANES // 2, 1)
        left_ref[comp * half : (comp + 1) * half, :] = jnp.where(lanes >= LANES // 2, upper, lower)
    lanes = lane_ids(rows)
    packed = None
    for comp in range(3):
        ends = jnp.where(lanes < LANES // 2, state_ref[comp, :, 0:LANES], state_ref[comp, :, cols - LANES : cols])
        ends = roll(ends, 8 * comp + 4, 1)
        packed = ends if packed is None else jnp.where(lanes >= 8 * comp, ends, packed)
    strip_ref[0:24, :] = packed.T[0:24]
    strip_ref[24:32, :] = jnp.full((8, LANES), rc)
    left_ref[3 * half : 3 * half + 8, :] = jnp.full((8, LANES), rc)
    for comp in range(3):
        left_ref[3 * half + 2 * comp : 3 * half + 2 * comp + 2, :] = strip_ref[8 * comp + 2 : 8 * comp + 4, :]
    slab_ref[...] = state_ref[:, rows - SLAB : rows, :]


def pack_right(col_count, strip_ref, right_ref, counts_ref):
    cc = col_count[0, 0].astype(jnp.float32)
    counts = jnp.where(row_ids(8) == 6, strip_ref[24:32, :], cc)
    counts_ref[...] = counts
    right_ref[...] = counts
    for comp in range(3):
        right_ref[2 * comp : 2 * comp + 2, :] = strip_ref[8 * comp + 4 : 8 * comp + 6, :]


def is_odd():
    return lax.axis_index("row") % 2 == 1


def pack_rows(counts_ref, strip_ref, left_ref, right_ref, state_ref, upper_ref, rim_ref, within_ref, across_ref, edge_ref):
    rows, cols = state_ref.shape[1], state_ref.shape[2]
    half = rows // 2
    rc, cc = counts_ref[6:7, :], counts_ref[7:8, :]
    right = jnp.concatenate([right_ref[...], jnp.zeros((LANES - 8, LANES), jnp.float32)], axis=0).T
    lanes = lane_ids(rows)
    left_rc = left_ref[3 * half + 6 : 3 * half + 7, :]
    counts = jnp.where(lanes == LEFT_ROWS, left_rc, jnp.where(lanes == OWN_ROWS, rc, cc))
    odd = is_odd()
    packed_half = SLAB // 2
    low = lane_ids(packed_half) < LANES // 2

    def put(at, down, up):
        size = down.shape[0]
        within_ref[at : at + size, :] = jnp.where(odd, up, down)
        across_ref[at : at + size, :] = jnp.where(odd, down, up)

    ups, downs = [], []
    for comp in range(3):
        packed = left_ref[comp * half : (comp + 1) * half, :]
        left = jnp.concatenate([packed, roll(packed, LANES // 2, 1)], axis=0)
        inner = right if comp == 0 else roll(right, -2 * comp, 1)
        inner = jnp.where(lanes < LEFT_ROWS, inner, counts)
        rim = jnp.where(lanes >= LANES // 2, left, inner)
        rim_ref[comp] = rim
        last = packed[half - SLAB : half]
        downs.append(jnp.where(low, last[0:packed_half], roll(last[packed_half:SLAB], LANES // 2, 1)))
        ups += [state_ref[comp, 0:8, LANES * t : LANES * (t + 1)] for t in range(cols // LANES)] + [rim[0:8]]
        edge_ref[comp, 0:2, :] = left_ref[3 * half + 2 * comp : 3 * half + 2 * comp + 2, :]
        edge_ref[comp, 2:6, :] = strip_ref[8 * comp + 4 : 8 * comp + 8, :]
        edge_ref[comp, 6:10, :] = strip_ref[8 * comp : 8 * comp + 4, :]
        edge_ref[comp, 10:12, :] = right_ref[2 * comp : 2 * comp + 2, :]
        edge_ref[comp, 12:16, :] = strip_ref[8 * comp + 4 : 8 * comp + 8, :]
    last_row = jnp.where(lane_ids(8) < LANES // 2, cc, right_ref[7:8, :])
    downs.append(jnp.where(row_ids(8) >= 6, last_row, right_ref[...]))
    down = jnp.concatenate(downs, axis=0)
    up = jnp.concatenate(ups, axis=0)
    size = up.shape[0]
    put(0, down[0:size], up)
    across_ref[size:DOWN_ROWS, :] = down[size:DOWN_ROWS]
    within_ref[size : DOWN_ROWS - 1, :] = down[size : DOWN_ROWS - 1]


def inner_error(state_ref, first, size, columns):
    part = slice(2 * first, 2 * (first + size))
    for comp in range(3):
        left, right = state_ref[comp, part, 0:LANES], state_ref[comp, part, LANES : 2 * LANES]
        for parity in range(2):
            columns[comp, parity] = every_other(left, right, parity)
    phases = [
        [[columns[c, y, pl.ds(x, size, stride=2), :] for c in range(3)] for y in range(2)]
        for x in range(2)
    ]
    return coarse_error(phases)


def upper_error(state_ref, error_ref, columns):
    rows = error_ref.shape[0]
    error_ref[...] = inner_error(state_ref, 0, rows + 8, columns)[0:rows]


def lower_error(pos_ref, ext_ref, state_ref, rim_ref, error_ref, numbers_ref, columns, pos, ext, sems):
    copies = [pltpu.make_async_copy(src, dst, sems.at[k]) for k, (src, dst) in enumerate(((pos_ref, pos), (ext_ref, ext)))]
    for copy in copies:
        copy.start()
    rows = error_ref.shape[0]
    error_ref[...] = inner_error(state_ref, state_ref.shape[1] // 2 - rows - 8, rows + 8, columns)[8 : rows + 8]
    for copy in copies:
        copy.wait()
    pair = [v[0].astype(jnp.float32) for v in (pos, ext)]
    numbers = jnp.broadcast_to(pair[1][:, 1:2], (8, LANES))
    for k, number in enumerate((pair[0][:, 0:1], pair[0][:, 1:2], pair[1][:, 0:1])):
        numbers = jnp.where(row_ids(8) == k, number, numbers)
    numbers_ref[...] = numbers


def edge_phases(state_ref, slab_ref, above_rim, below, edge_ref, near_rows, columns, corners_ref):
    rows, cols = state_ref.shape[1], state_ref.shape[2]
    right = slice(cols, cols + LANES)
    lanes = lane_ids(8)
    packed_up, packed_down = None, None
    for comp in range(3):
        near_rows[comp][0:2, :] = slab_ref[comp, SLAB - 2 : SLAB, :]
        near_rows[comp][2:6, :] = state_ref[comp, 0:4, :]
        near_rows[comp][6:10, :] = state_ref[comp, rows - 4 : rows, :]
        near_rows[comp][10:12, :] = below[comp][0:2, 0:cols]
        near_rows[comp][12:16, :] = state_ref[comp, 0:4, :]
        first, second = near_rows[comp][:, 0:LANES], near_rows[comp][:, LANES : 2 * LANES]
        for parity in range(2):
            columns[comp][parity] = every_other(first, second, parity)

        def around_corner(body, rim):
            start = jnp.where(lanes < LANES // 2, body[:, 0:LANES], rim)
            end = jnp.where(lanes < LANES // 2, rim, body[:, cols - LANES : cols])
            first_six = (lanes >= 12 * comp) & (lanes < 12 * comp + 6)
            return jnp.where(first_six, roll(start, 12 * comp + 2, 1), roll(end, 12 * comp + 10, 1))

        up = around_corner(slab_ref[comp, SLAB - 8 : SLAB, :], above_rim[comp][SLAB - 8 : SLAB, :])
        down = around_corner(below[comp][:, 0:cols], below[comp][:, right])
        packed_up = up if comp == 0 else jnp.where(lanes >= 12 * comp, up, packed_up)
        packed_down = down if comp == 0 else jnp.where(lanes >= 12 * comp, down, packed_down)
    corners = jnp.concatenate([packed_down, jnp.ones((LANES - 16, LANES), jnp.float32), packed_up], axis=0).T
    for comp in range(3):
        corners_ref[comp][0:12, :] = corners[12 * comp : 12 * comp + 12, :]
        corners_ref[comp][12:16, :] = edge_ref[comp, 12:16, :]
    phases = []
    for x in range(2):
        phases.append([])
        for y in range(2):
            cells = []
            for comp, turned in ((0, 0), (1, 2), (2, 1)):
                by_row = columns[comp][y, pl.ds(x, 8, stride=2), :]
                own = edge_ref[turned, pl.ds(x, 8, stride=2), :]
                outer = corners_ref[turned][pl.ds(x, 8, stride=2), :]
                cells.append(jnp.concatenate([by_row, every_other(own, outer, y)], axis=0))
            phases[-1].append(cells)
    return phases


def put_edges(error, edges):
    half_rows = error.shape[0]
    turned = jnp.concatenate([edges, jnp.zeros((LANES - 16, LANES), jnp.float32)], axis=0).T[0:half_rows]
    lanes, ids = lane_ids(half_rows), row_ids(half_rows)
    error = jnp.where(ids == 0, edges[1:2], jnp.where(ids == half_rows - 1, edges[4:5], error))
    return jnp.where(
        lanes == 0, roll(turned, -9, 1), jnp.where(lanes == LANES - 1, roll(turned, LANES - 13, 1), error)
    )


def minmod(lower_diff, upper_diff):
    smaller, larger = jnp.minimum(lower_diff, upper_diff), jnp.maximum(lower_diff, upper_diff)
    return jnp.maximum(smaller, jnp.minimum(larger, 0.0))


def axis_terms(cells, axis):
    depth, normal, tangent = cells[0], cells[1 + axis], cells[2 - axis]
    inverse_root = lax.rsqrt(depth)
    velocity = normal * (inverse_root * inverse_root)
    along = normal * velocity + 0.5 * depth * depth
    beside = tangent * velocity
    speed = jnp.abs(velocity) + depth * inverse_root
    return (normal, along, beside, speed) if axis == 0 else (normal, beside, along, speed)


def paired_change(near, far, axis):
    down = lambda v: roll(v, 1, axis)
    up = lambda v: roll(v, -1, axis)
    inner = [f - n for n, f in zip(near, far)]
    outer = [n - down(f) for n, f in zip(near, far)]
    near_half = [0.5 * minmod(o, i) for o, i in zip(outer, inner)]
    far_half = [0.5 * minmod(i, up(o)) for o, i in zip(outer, inner)]
    near_hi = [n + s for n, s in zip(near, near_half)]
    near_lo = [n - s for n, s in zip(near, near_half)]
    far_hi = [down(f + s) for f, s in zip(far, far_half)]
    far_lo = [f - s for f, s in zip(far, far_half)]
    terms = lambda cells: axis_terms(cells, axis)
    inner_flux = doubled_flux(near_hi, far_lo, terms(near_hi), terms(far_lo))
    outer_flux = doubled_flux(far_hi, near_lo, terms(far_hi), terms(near_lo))
    near_change = [i - o for i, o in zip(inner_flux, outer_flux)]
    far_change = [up(o) - i for i, o in zip(inner_flux, outer_flux)]
    return near_change, far_change


def doubled_first_step(cells):
    all_terms = cell_terms(*cells)
    changes = []
    for axis in (0, 1):
        terms = all_terms[axis]
        lower = [roll(f, 1, axis) for f in cells]
        lower_terms = [lower[1 + axis] if c == 0 else roll(terms[c], 1, axis) for c in range(4)]
        flux = doubled_flux(lower, cells, lower_terms, terms)
        own = [2.0 * terms[c] for c in range(3)]
        changes.append(
            (
                [o - f for o, f in zip(own, flux)],
                [roll(f, -1, axis) - o for o, f in zip(own, flux)],
            )
        )
    rows, cols = changes
    return [
        [
            [cells[c] - (0.5 * RATIO) * (rows[a][c] + cols[b][c]) for c in range(3)]
            for b in range(2)
        ]
        for a in range(2)
    ]


def patch_rows(cells, size):
    half = doubled_first_step(cells)
    by_row = [paired_change(half[0][b], half[1][b], 0) for b in range(2)]
    by_col = [paired_change(half[a][0], half[a][1], 1) for a in range(2)]
    lanes = lane_ids(size)
    result = []
    for a in range(2):
        fine = [
            [half[a][b][c] - (0.5 * RATIO) * (by_row[b][a][c] + by_col[a][b][c]) for c in range(3)]
            for b in range(2)
        ]
        parts = []
        for c in range(3):
            pick = lanes // 2 + 2
            even = jnp.take_along_axis(fine[0][c][0:size], pick, axis=1)
            odd = jnp.take_along_axis(fine[1][c][0:size], pick, axis=1)
            parts.append(jnp.where(lanes % 2 == 0, even, odd))
        result.append(parts)
    return result


def sliding(load, start, size):
    group, shift = start // 8, start % 8
    turn = (8 - shift) % 8
    parts = [pltpu.roll(load(group + k), turn, 0) for k in range(size // 8 + 1)]
    keep = row_ids(8, parts[0].shape[1]) < 8 - shift
    return [jnp.where(keep, parts[k], parts[k + 1]) for k in range(size // 8)]


def scalar(values, row, lane):
    return values[row, lane].astype(jnp.int32)


def slab_rows(ref, first, count, size):
    last = SLAB // 8 - 1
    load = lambda k: ref[pl.ds(pl.multiple_of(first + 8 * jnp.minimum(k, last), 8), 8), :]
    return sliding(load, SLAB - count, size)


def column_move(first_cols, last_cols, side, here, right_count):
    lanes = lane_ids(8)
    head = jnp.where(lanes < here, pltpu.roll(side, here, 1), first_cols)
    outer = jnp.where(lanes < right_count, pltpu.roll(last_cols, right_count, 1), side)
    return head, jnp.where(lanes >= LANES // 2, side, outer)


def move_rows(state_ref, rim_ref, slab_ref, wide_ref):
    rows, cols = state_ref.shape[1], state_ref.shape[2]
    counts = rim_ref[0, 0:8, :]
    rc, cc, cc_right = [scalar(counts, 0, k) for k in (OWN_ROWS, OWN_COLS, RIGHT_COLS)]
    for comp in range(3):
        bodies = slab_rows(slab_ref.at[comp], 0, rc, SLAB)
        for k in range(rows // 8):
            part, at = slice(8 * k, 8 * k + 8), slice(8 * k + 8, 8 * k + 16)
            body = state_ref[comp, part, :]
            if 8 * k < SLAB:
                body = jnp.where(row_ids(8, cols) + 8 * k < rc, bodies[k], body)
                wide_ref[comp, at, LANES : LANES + cols] = body
                continue
            head, outer = column_move(
                body[:, 0:LANES], body[:, cols - LANES : cols], rim_ref[comp, part, :], cc, cc_right
            )
            wide_ref[comp, at, 0:LANES] = outer
            wide_ref[comp, at, LANES : 2 * LANES] = head
            wide_ref[comp, at, 2 * LANES : LANES + cols] = body[:, LANES:cols]
            wide_ref[comp, at, LANES + cols : 2 * LANES + cols] = outer


def finish(
    state_ref, rim_ref, slab_ref, rows_ref, within_ref, across_ref, upper_ref, lower_ref, edge_ref, numbers_ref,
    error_out, moved_out, patch_out,
    wide, window, near_rows, columns, corners, above_rim, below, patch, error, aside, sems,
):
    rows, cols = state_ref.shape[1], state_ref.shape[2]
    right = slice(cols, cols + LANES)
    inside_wide = slice(LANES, LANES + cols)
    on_left = lane_ids(8) >= LANES // 2
    copies = [
        pltpu.make_async_copy(rows_ref.at[:, SLAB + 8 : rows + 8, inside_wide], moved_out.at[:, SLAB:rows, :], sems.at[0])
    ]
    copies[-1].start()

    odd = is_odd()
    packed_half = SLAB // 2
    last_rows = slice(DOWN_ROWS - 8, DOWN_ROWS - 1)
    aside[0:7, :] = jnp.where(odd, within_ref[last_rows, :], across_ref[last_rows, :])
    aside[7:8, :] = jnp.zeros((1, LANES), jnp.float32)
    beside = aside[...]
    turned = jnp.concatenate([beside, jnp.zeros((LANES - 8, LANES), jnp.float32)], axis=0).T[rows - SLAB : rows]
    lanes = lane_ids(packed_half)
    tiles = cols // LANES + 1
    for comp in range(3):
        at = slice(comp * packed_half, (comp + 1) * packed_half)
        packed = jnp.where(odd, within_ref[at, :], across_ref[at, :])
        inner = turned if comp == 0 else roll(turned, -2 * comp, 1)
        upper = jnp.where(lanes >= LANES // 2, roll(packed, LANES // 2, 1), inner[0:packed_half])
        lower = jnp.where(lanes >= LANES // 2, packed, inner[packed_half:SLAB])
        above_rim[comp][0:packed_half, :] = upper
        above_rim[comp][packed_half:SLAB, :] = lower
        for t in range(tiles):
            at = slice(8 * (comp * tiles + t), 8 * (comp * tiles + t) + 8)
            below[comp][:, LANES * t : LANES * (t + 1)] = jnp.where(odd, across_ref[at, :], within_ref[at, :])

    edges = coarse_error(
        edge_phases(state_ref, slab_ref, above_rim, below, edge_ref, near_rows, columns, corners)
    )
    error[...] = put_edges(jnp.concatenate([upper_ref[...], lower_ref[...]], axis=0), edges)

    own_counts, below_counts, numbers = rim_ref[0, 0:8, :], below[0][:, right], numbers_ref[...]
    cc, rc_left, rc_right, cc_right = [
        scalar(own_counts, 0, k) for k in (OWN_COLS, LEFT_ROWS, RIGHT_ROWS, RIGHT_COLS)
    ]
    cc_above, cc_above_right = [scalar(beside, 6, k) for k in (0, LANES - 1)]
    rc_below, cc_below, rc_below_left, rc_below_right, cc_below_right = [
        scalar(below_counts, 0, k) for k in (OWN_ROWS, OWN_COLS, LEFT_ROWS, RIGHT_ROWS, RIGHT_COLS)
    ]
    pos_row, pos_col, ext_row, ext_col = [scalar(numbers, k, 0) for k in range(4)]

    def put(comp, at, body, side, here, right_count):
        tail = body[:, LANES:cols]
        head, outer = column_move(body[:, 0:LANES], tail[:, cols - 2 * LANES :], side, here, right_count)
        wide[comp][at : at + 8, 0:LANES] = outer
        wide[comp][at : at + 8, LANES : 2 * LANES] = head
        wide[comp][at : at + 8, 2 * LANES : LANES + cols] = tail
        wide[comp][at : at + 8, LANES + cols : 2 * LANES + cols] = outer

    def moved_rim(ref, first, left, right_count, size):
        from_left = slab_rows(ref, first, left, size)
        from_right = slab_rows(ref, first, right_count, size)
        return [jnp.where(on_left, a, b) for a, b in zip(from_left, from_right)]

    for comp in range(3):
        sides = moved_rim(above_rim[comp], 0, rc_left, rc_right, SLAB)
        for k in range(SLAB // 8):
            side = rim_ref[comp, 8 * k : 8 * k + 8, :]
            side = jnp.where(row_ids(8) + 8 * k < jnp.where(on_left, rc_left, rc_right), sides[k], side)
            put(comp, 8 * k + 8, rows_ref[comp, 8 * k + 8 : 8 * k + 16, inside_wide], side, cc, cc_right)
        wide[comp][SLAB + 8 : rows + 8, :] = rows_ref[comp, SLAB + 8 : rows + 8, :]
        put(comp, 0, slab_ref[comp, SLAB - 8 : SLAB, :], above_rim[comp][SLAB - 8 : SLAB, :], cc_above, cc_above_right)
        (body,) = slab_rows(state_ref.at[comp], rows - SLAB, rc_below, 8)
        (side,) = moved_rim(rim_ref.at[comp], rows - SLAB, rc_below_left, rc_below_right, 8)
        body = jnp.where(row_ids(8, cols) < rc_below, body, below[comp][:, 0:cols])
        side = jnp.where(
            row_ids(8) < jnp.where(on_left, rc_below_left, rc_below_right), side, below[comp][:, right]
        )
        put(comp, rows + 8, body, side, cc_below, cc_below_right)
    copies.append(pltpu.make_async_copy(error, error_out, sems.at[1]))
    copies += [
        pltpu.make_async_copy(wide[c].at[8 : SLAB + 8, inside_wide], moved_out.at[c, 0:SLAB, :], sems.at[2 + c])
        for c in range(3)
    ]

    first_lane = pos_col + LANES - 2
    tile, shift = first_lane // LANES, first_lane % LANES
    turn = (LANES - shift) % LANES
    keep = lane_ids(8) < LANES - shift
    for comp in range(3):

        def load(k):
            group = pl.ds(pl.multiple_of(8 * jnp.minimum(k, rows // 8 + 1), 8), 8)
            near = wide[comp][group, pl.ds(pl.multiple_of(LANES * tile, LANES), LANES)]
            far = wide[comp][group, pl.ds(pl.multiple_of(LANES * tile + LANES, LANES), LANES)]
            return jnp.where(keep, pltpu.roll(near, turn, 1), pltpu.roll(far, turn, 1))

        parts = sliding(load, pos_row + 8, PATCH + 8)
        (above,) = sliding(load, pos_row, 8)
        parts[-1] = jnp.where(row_ids(8) < 4, parts[-1], above)
        for k, part in enumerate(parts):
            window[comp][8 * k : 8 * k + 8, :] = part

    fine_rows, fine_cols = 2 * ext_row, 2 * ext_col
    fine = patch_rows([window[c][...] for c in range(3)], PATCH)
    lanes, ids = lane_ids(PATCH), row_ids(PATCH)
    for a in range(2):
        inside = (2 * ids + a < fine_rows) & (lanes < fine_cols)
        for c in range(3):
            patch[c][pl.ds(a, PATCH, stride=2), :] = jnp.where(inside, fine[a][c], 0.0)
    for c in range(3):
        copies.append(pltpu.make_async_copy(patch[c], patch_out.at[c], sems.at[5 + c]))
        copies[-1].start()
    for copy in copies[1:5]:
        copy.start()
    for copy in copies:
        copy.wait()


def around(axis, by):
    devices = lax.axis_size(axis)
    return [(i, (i + by) % devices) for i in range(devices)]


def in_vmem(value):
    return pltpu.with_memory_space_constraint(value, pltpu.VMEM)


def in_hbm(value):
    return pltpu.with_memory_space_constraint(value, pltpu.HBM)


def vmem(*shape):
    return pltpu.VMEM(shape, jnp.float32)


def per_device(state, row_count, col_count, patch_pos, patch_ext):
    rows, cols = state.shape[1], state.shape[2]
    width = cols + LANES
    half = rows // 2
    here = in_vmem(state)
    ahead = pl.pallas_call(
        blank,
        out_shape=vmem(8, LANES),
        out_specs=VMEM,
        cost_estimate=pl.CostEstimate(flops=10_000_000_000, bytes_accessed=10_000_000, transcendentals=0),
        name="ahead",
    )()
    to_right, strip, slab = pl.pallas_call(
        pack_cols,
        out_shape=(vmem(3 * half + 8, LANES), vmem(32, LANES), vmem(3, SLAB, cols)),
        in_specs=[SMEM, VMEM, VMEM],
        out_specs=(VMEM,) * 3,
        name="pack_cols",
    )(row_count, in_vmem(ahead), here)
    strip = in_vmem(strip)
    to_left, counts = pl.pallas_call(
        pack_right, out_shape=(vmem(8, LANES), vmem(8, LANES)), in_specs=[SMEM, VMEM], out_specs=(VMEM,) * 2, name="pack_right"
    )(col_count, strip)
    from_left = in_vmem(lax.ppermute(to_right, "col", around("col", 1)))
    from_right = in_vmem(lax.ppermute(to_left, "col", around("col", -1)))
    slab_above = in_vmem(lax.ppermute(slab, "row", around("row", 1)))
    upper = in_vmem(pl.pallas_call(
        upper_error,
        out_shape=vmem(UPPER, cols // 2),
        in_specs=[VMEM],
        out_specs=VMEM,
        scratch_shapes=[vmem(3, 2, 2 * UPPER + 16, LANES)],
        cost_estimate=pl.CostEstimate(flops=15_000_000, bytes_accessed=300_000, transcendentals=0),
        name="upper_error",
    )(here))
    rim, within, across, edge = pl.pallas_call(
        pack_rows,
        out_shape=(vmem(3, rows, LANES), vmem(DOWN_ROWS - 1, LANES), vmem(DOWN_ROWS, LANES), vmem(3, 16, LANES)),
        in_specs=[VMEM] * 6,
        out_specs=(VMEM,) * 4,
        cost_estimate=pl.CostEstimate(flops=3_000_000_000, bytes_accessed=600_000, transcendentals=0),
        name="pack_rows",
    )(in_vmem(counts), strip, from_left, from_right, here, upper)
    rim = in_vmem(rim)
    lower, numbers = pl.pallas_call(
        lower_error,
        out_shape=(vmem(half - UPPER, cols // 2), vmem(8, LANES)),
        in_specs=[ANY, ANY, VMEM, VMEM],
        out_specs=(VMEM,) * 2,
        scratch_shapes=[
            vmem(3, 2, 2 * (half - UPPER) + 16, LANES),
            pltpu.VMEM(patch_pos.shape, jnp.int32),
            pltpu.VMEM(patch_ext.shape, jnp.int32),
            pltpu.SemaphoreType.DMA((2,)),
        ],
        cost_estimate=pl.CostEstimate(flops=15_000_000, bytes_accessed=300_000, transcendentals=0),
        name="lower_error",
    )(in_hbm(patch_pos), in_hbm(patch_ext), here, rim)
    devices = lax.axis_size("row")
    from_within = in_vmem(lax.ppermute(within, "row", [(i, i ^ 1) for i in range(devices)]))
    from_across = in_vmem(
        lax.ppermute(across, "row", [(i, (i + (1 if i % 2 else -1)) % devices) for i in range(devices)])
    )
    moved_rows = in_vmem(pl.pallas_call(
        move_rows,
        out_shape=vmem(3, rows + 16, width + LANES),
        in_specs=[VMEM] * 3,
        out_specs=VMEM,
        cost_estimate=pl.CostEstimate(flops=3_000_000, bytes_accessed=1_000_000, transcendentals=0),
        name="move_rows",
    )(here, rim, slab_above))
    return pl.pallas_call(
        finish,
        out_shape=(f32(half, cols // 2), f32(3, rows, cols), f32(3, 2 * PATCH, 2 * PATCH)),
        in_specs=[VMEM] * 10,
        out_specs=(ANY,) * 3,
        scratch_shapes=[
            [vmem(rows + 16, width + LANES)] * 3,
            [vmem(PATCH + 8, LANES)] * 3,
            [vmem(16, cols)] * 3,
            [vmem(2, 16, LANES)] * 3,
            [vmem(16, LANES)] * 3,
            [vmem(SLAB, LANES)] * 3,
            [vmem(8, width)] * 3,
            [vmem(2 * PATCH, 2 * PATCH)] * 3,
            vmem(half, cols // 2),
            vmem(8, LANES),
            pltpu.SemaphoreType.DMA((8,)),
        ],
        compiler_params=PARAMS,
        name="finish",
    )(here, rim, slab_above, moved_rows, from_within, from_across, upper, lower, edge, numbers)


def solution(mesh):
    placed = (
        P(None, "row", "col"),
        P("row", "col"),
        P("row", "col"),
        P("row", "col", None),
        P("row", "col", None),
    )
    return jax.shard_map(
        per_device,
        mesh=mesh,
        in_specs=placed,
        out_specs=(P("row", "col"), P(None, "row", "col"), P(None, "row", "col")),
        check_vma=False,
    )
```

```python
import jax
import jax.numpy as jnp
from jax import lax
from jax.experimental import pallas as pl
from jax.experimental.pallas import tpu as pltpu
from jax.sharding import PartitionSpec as P

SLAB = 64
PATCH = 64
LANES = 128
UPPER = 32

RATIO = 0.1
ERR_SCALE = 10.0

RIGHT_ROWS, RIGHT_COLS, LEFT_ROWS, OWN_ROWS, OWN_COLS = 6, 7, 8, 10, 11
DOWN_ROWS = 3 * SLAB // 2 + 8

VMEM = pl.BlockSpec(memory_space=pltpu.VMEM)
SMEM = pl.BlockSpec(memory_space=pltpu.SMEM)
ANY = pl.BlockSpec(memory_space=pl.ANY)
PARAMS = pltpu.CompilerParams(vmem_limit_bytes=32 * 1024 * 1024)


def f32(*shape):
    return jax.ShapeDtypeStruct(shape, jnp.float32)


def lane_ids(rows, width=LANES):
    return lax.broadcasted_iota(jnp.int32, (rows, width), 1)


def row_ids(rows, width=LANES):
    return lax.broadcasted_iota(jnp.int32, (rows, width), 0)


def roll(value, by, axis):
    return pltpu.roll(value, by % value.shape[axis], axis)


def cell_terms(depth, first, second):
    inverse_root = lax.rsqrt(depth)
    wave = depth * inverse_root
    inverse = inverse_root * inverse_root
    first_vel = first * inverse
    second_vel = second * inverse
    pressure = 0.5 * depth * depth
    cross = first * second_vel
    row_terms = (first, first * first_vel + pressure, cross, jnp.abs(first_vel) + wave)
    col_terms = (second, cross, second * second_vel + pressure, jnp.abs(second_vel) + wave)
    return row_terms, col_terms


def doubled_flux(left, right, left_terms, right_terms):
    speed = jnp.maximum(left_terms[3], right_terms[3])
    return [(left_terms[c] + right_terms[c]) - speed * (right[c] - left[c]) for c in range(3)]


def spread_step(fields, row_by, col_by):
    row_terms, col_terms = cell_terms(*fields)
    total = None
    for terms, by, axis in ((row_terms, row_by, 0), (col_terms, col_by, 1)):
        lower = [roll(f, by, axis) for f in fields]
        momentum = lower[1 + axis]
        lower_terms = [momentum if c == 0 else roll(terms[c], by, axis) for c in range(4)]
        flux = doubled_flux(lower, fields, lower_terms, terms)
        change = [roll(f, -by, axis) - f for f in flux]
        total = change if total is None else [t + c for t, c in zip(total, change)]
    return [f - (0.5 * RATIO) * t for f, t in zip(fields, total)]


def pair_change(near, far, near_terms, far_terms, axis):
    inner = doubled_flux(near, far, near_terms, far_terms)
    before = [roll(f, 1, axis) for f in far]
    before_terms = [before[1 + axis] if c == 0 else roll(far_terms[c], 1, axis) for c in range(4)]
    outer = doubled_flux(before, near, before_terms, near_terms)
    near_change = [i - o for i, o in zip(inner, outer)]
    far_change = [roll(o, -1, axis) - i for i, o in zip(inner, outer)]
    return near_change, far_change


def paired_step(phases):
    terms = [[cell_terms(*phases[x][y]) for y in range(2)] for x in range(2)]
    along_first = [
        pair_change(phases[0][y], phases[1][y], terms[0][y][0], terms[1][y][0], 0) for y in range(2)
    ]
    along_second = [
        pair_change(phases[x][0], phases[x][1], terms[x][0][1], terms[x][1][1], 1) for x in range(2)
    ]
    return [
        [
            [
                phases[x][y][c] - (0.5 * RATIO) * (along_first[y][x][c] + along_second[x][y][c])
                for c in range(3)
            ]
            for y in range(2)
        ]
        for x in range(2)
    ]


def block_mean(phases):
    return [
        0.25 * ((phases[0][0][c] + phases[1][0][c]) + (phases[0][1][c] + phases[1][1][c])) for c in range(3)
    ]


def coarse_error(phases):
    fine = block_mean(paired_step(paired_step(phases)))
    coarse = spread_step(block_mean(phases), 1, 1)
    parts = [jnp.abs(f - c) for f, c in zip(fine, coarse)]
    return ERR_SCALE * ((parts[0] + parts[1]) + parts[2])


def every_other(first, second, parity):
    lanes = lane_ids(first.shape[0])
    pick = (2 * lanes + parity) % LANES
    low = jnp.take_along_axis(first, pick, axis=1)
    high = jnp.take_along_axis(second, pick, axis=1)
    return jnp.where(lanes < LANES // 2, low, high)


def blank(out_ref):
    out_ref[...] = jnp.zeros(out_ref.shape, jnp.float32)


def pack_cols(row_count, blank_ref, state_ref, left_ref, strip_ref):
    rows, cols = state_ref.shape[1], state_ref.shape[2]
    half = rows // 2
    rc = row_count[0, 0].astype(jnp.float32)
    lanes = lane_ids(half)
    for comp in range(3):
        upper = state_ref[comp, 0:half, cols - LANES : cols]
        lower = roll(state_ref[comp, half:rows, cols - LANES : cols], LANES // 2, 1)
        left_ref[comp * half : (comp + 1) * half, :] = jnp.where(lanes >= LANES // 2, upper, lower)
    lanes = lane_ids(rows)
    packed = None
    for comp in range(3):
        ends = jnp.where(lanes < LANES // 2, state_ref[comp, :, 0:LANES], state_ref[comp, :, cols - LANES : cols])
        ends = roll(ends, 8 * comp + 4, 1)
        packed = ends if packed is None else jnp.where(lanes >= 8 * comp, ends, packed)
    strip_ref[0:24, :] = packed.T[0:24]
    strip_ref[24:32, :] = jnp.full((8, LANES), rc)
    left_ref[3 * half : 3 * half + 8, :] = jnp.full((8, LANES), rc)
    for comp in range(3):
        left_ref[3 * half + 2 * comp : 3 * half + 2 * comp + 2, :] = strip_ref[8 * comp + 2 : 8 * comp + 4, :]


def pack_right(col_count, strip_ref, state_ref, right_ref, counts_ref, slab_ref):
    slab_ref[...] = state_ref[:, state_ref.shape[1] - SLAB :, :]
    cc = col_count[0, 0].astype(jnp.float32)
    counts = jnp.where(row_ids(8) == 6, strip_ref[24:32, :], cc)
    counts_ref[...] = counts
    right_ref[...] = counts
    for comp in range(3):
        right_ref[2 * comp : 2 * comp + 2, :] = strip_ref[8 * comp + 4 : 8 * comp + 6, :]


def is_odd():
    return lax.axis_index("row") % 2 == 1


def pack_rows(counts_ref, strip_ref, left_ref, right_ref, state_ref, upper_ref, rim_ref, within_ref, across_ref, edge_ref):
    rows, cols = state_ref.shape[1], state_ref.shape[2]
    half = rows // 2
    rc, cc = counts_ref[6:7, :], counts_ref[7:8, :]
    right = jnp.concatenate([right_ref[...], jnp.zeros((LANES - 8, LANES), jnp.float32)], axis=0).T
    lanes = lane_ids(rows)
    left_rc = left_ref[3 * half + 6 : 3 * half + 7, :]
    counts = jnp.where(lanes == LEFT_ROWS, left_rc, jnp.where(lanes == OWN_ROWS, rc, cc))
    odd = is_odd()
    packed_half = SLAB // 2
    low = lane_ids(packed_half) < LANES // 2

    def put(at, down, up):
        size = down.shape[0]
        within_ref[at : at + size, :] = jnp.where(odd, up, down)
        across_ref[at : at + size, :] = jnp.where(odd, down, up)

    ups, downs = [], []
    for comp in range(3):
        packed = left_ref[comp * half : (comp + 1) * half, :]
        left = jnp.concatenate([packed, roll(packed, LANES // 2, 1)], axis=0)
        inner = right if comp == 0 else roll(right, -2 * comp, 1)
        inner = jnp.where(lanes < LEFT_ROWS, inner, counts)
        rim = jnp.where(lanes >= LANES // 2, left, inner)
        rim_ref[comp] = rim
        last = packed[half - SLAB : half]
        downs.append(jnp.where(low, last[0:packed_half], roll(last[packed_half:SLAB], LANES // 2, 1)))
        ups += [state_ref[comp, 0:8, LANES * t : LANES * (t + 1)] for t in range(cols // LANES)] + [rim[0:8]]
        edge_ref[comp, 0:2, :] = left_ref[3 * half + 2 * comp : 3 * half + 2 * comp + 2, :]
        edge_ref[comp, 2:6, :] = strip_ref[8 * comp + 4 : 8 * comp + 8, :]
        edge_ref[comp, 6:10, :] = strip_ref[8 * comp : 8 * comp + 4, :]
        edge_ref[comp, 10:12, :] = right_ref[2 * comp : 2 * comp + 2, :]
        edge_ref[comp, 12:16, :] = strip_ref[8 * comp + 4 : 8 * comp + 8, :]
    last_row = jnp.where(lane_ids(8) < LANES // 2, cc, right_ref[7:8, :])
    downs.append(jnp.where(row_ids(8) >= 6, last_row, right_ref[...]))
    down = jnp.concatenate(downs, axis=0)
    up = jnp.concatenate(ups, axis=0)
    size = up.shape[0]
    put(0, down[0:size], up)
    across_ref[size:DOWN_ROWS, :] = down[size:DOWN_ROWS]
    within_ref[size : DOWN_ROWS - 1, :] = down[size : DOWN_ROWS - 1]


def inner_error(state_ref, first, size, columns):
    part = slice(2 * first, 2 * (first + size))
    for comp in range(3):
        left, right = state_ref[comp, part, 0:LANES], state_ref[comp, part, LANES : 2 * LANES]
        for parity in range(2):
            columns[comp, parity] = every_other(left, right, parity)
    phases = [
        [[columns[c, y, pl.ds(x, size, stride=2), :] for c in range(3)] for y in range(2)]
        for x in range(2)
    ]
    return coarse_error(phases)


def upper_error(state_ref, error_ref, columns):
    rows = error_ref.shape[0]
    error_ref[...] = inner_error(state_ref, 0, rows + 8, columns)[0:rows]


def lower_error(pos_ref, ext_ref, state_ref, rim_ref, error_ref, numbers_ref, columns, pos, ext, sems):
    copies = [pltpu.make_async_copy(src, dst, sems.at[k]) for k, (src, dst) in enumerate(((pos_ref, pos), (ext_ref, ext)))]
    for copy in copies:
        copy.start()
    rows = error_ref.shape[0]
    error_ref[...] = inner_error(state_ref, state_ref.shape[1] // 2 - rows - 8, rows + 8, columns)[8 : rows + 8]
    for copy in copies:
        copy.wait()
    pair = [v[0].astype(jnp.float32) for v in (pos, ext)]
    numbers = jnp.broadcast_to(pair[1][:, 1:2], (8, LANES))
    for k, number in enumerate((pair[0][:, 0:1], pair[0][:, 1:2], pair[1][:, 0:1])):
        numbers = jnp.where(row_ids(8) == k, number, numbers)
    numbers_ref[...] = numbers


def edge_phases(state_ref, slab_ref, above_rim, below, edge_ref, near_rows, columns, corners_ref):
    rows, cols = state_ref.shape[1], state_ref.shape[2]
    right = slice(cols, cols + LANES)
    lanes = lane_ids(8)
    packed_up, packed_down = None, None
    for comp in range(3):
        near_rows[comp][0:2, :] = slab_ref[comp, SLAB - 2 : SLAB, :]
        near_rows[comp][2:6, :] = state_ref[comp, 0:4, :]
        near_rows[comp][6:10, :] = state_ref[comp, rows - 4 : rows, :]
        near_rows[comp][10:12, :] = below[comp][0:2, 0:cols]
        near_rows[comp][12:16, :] = state_ref[comp, 0:4, :]
        first, second = near_rows[comp][:, 0:LANES], near_rows[comp][:, LANES : 2 * LANES]
        for parity in range(2):
            columns[comp][parity] = every_other(first, second, parity)

        def around_corner(body, rim):
            start = jnp.where(lanes < LANES // 2, body[:, 0:LANES], rim)
            end = jnp.where(lanes < LANES // 2, rim, body[:, cols - LANES : cols])
            first_six = (lanes >= 12 * comp) & (lanes < 12 * comp + 6)
            return jnp.where(first_six, roll(start, 12 * comp + 2, 1), roll(end, 12 * comp + 10, 1))

        up = around_corner(slab_ref[comp, SLAB - 8 : SLAB, :], above_rim[comp][SLAB - 8 : SLAB, :])
        down = around_corner(below[comp][:, 0:cols], below[comp][:, right])
        packed_up = up if comp == 0 else jnp.where(lanes >= 12 * comp, up, packed_up)
        packed_down = down if comp == 0 else jnp.where(lanes >= 12 * comp, down, packed_down)
    corners = jnp.concatenate([packed_down, jnp.ones((LANES - 16, LANES), jnp.float32), packed_up], axis=0).T
    for comp in range(3):
        corners_ref[comp][0:12, :] = corners[12 * comp : 12 * comp + 12, :]
        corners_ref[comp][12:16, :] = edge_ref[comp, 12:16, :]
    phases = []
    for x in range(2):
        phases.append([])
        for y in range(2):
            cells = []
            for comp, turned in ((0, 0), (1, 2), (2, 1)):
                by_row = columns[comp][y, pl.ds(x, 8, stride=2), :]
                own = edge_ref[turned, pl.ds(x, 8, stride=2), :]
                outer = corners_ref[turned][pl.ds(x, 8, stride=2), :]
                cells.append(jnp.concatenate([by_row, every_other(own, outer, y)], axis=0))
            phases[-1].append(cells)
    return phases


def put_edges(error, edges):
    half_rows = error.shape[0]
    turned = jnp.concatenate([edges, jnp.zeros((LANES - 16, LANES), jnp.float32)], axis=0).T[0:half_rows]
    lanes, ids = lane_ids(half_rows), row_ids(half_rows)
    error = jnp.where(ids == 0, edges[1:2], jnp.where(ids == half_rows - 1, edges[4:5], error))
    return jnp.where(
        lanes == 0, roll(turned, -9, 1), jnp.where(lanes == LANES - 1, roll(turned, LANES - 13, 1), error)
    )


def minmod(lower_diff, upper_diff):
    smaller, larger = jnp.minimum(lower_diff, upper_diff), jnp.maximum(lower_diff, upper_diff)
    return jnp.maximum(smaller, jnp.minimum(larger, 0.0))


def axis_terms(cells, axis):
    depth, normal, tangent = cells[0], cells[1 + axis], cells[2 - axis]
    inverse_root = lax.rsqrt(depth)
    velocity = normal * (inverse_root * inverse_root)
    along = normal * velocity + 0.5 * depth * depth
    beside = tangent * velocity
    speed = jnp.abs(velocity) + depth * inverse_root
    return (normal, along, beside, speed) if axis == 0 else (normal, beside, along, speed)


def paired_change(near, far, axis):
    down = lambda v: roll(v, 1, axis)
    up = lambda v: roll(v, -1, axis)
    inner = [f - n for n, f in zip(near, far)]
    outer = [n - down(f) for n, f in zip(near, far)]
    near_half = [0.5 * minmod(o, i) for o, i in zip(outer, inner)]
    far_half = [0.5 * minmod(i, up(o)) for o, i in zip(outer, inner)]
    near_hi = [n + s for n, s in zip(near, near_half)]
    near_lo = [n - s for n, s in zip(near, near_half)]
    far_hi = [down(f + s) for f, s in zip(far, far_half)]
    far_lo = [f - s for f, s in zip(far, far_half)]
    terms = lambda cells: axis_terms(cells, axis)
    inner_flux = doubled_flux(near_hi, far_lo, terms(near_hi), terms(far_lo))
    outer_flux = doubled_flux(far_hi, near_lo, terms(far_hi), terms(near_lo))
    near_change = [i - o for i, o in zip(inner_flux, outer_flux)]
    far_change = [up(o) - i for i, o in zip(inner_flux, outer_flux)]
    return near_change, far_change


def doubled_first_step(cells):
    all_terms = cell_terms(*cells)
    changes = []
    for axis in (0, 1):
        terms = all_terms[axis]
        lower = [roll(f, 1, axis) for f in cells]
        lower_terms = [lower[1 + axis] if c == 0 else roll(terms[c], 1, axis) for c in range(4)]
        flux = doubled_flux(lower, cells, lower_terms, terms)
        own = [2.0 * terms[c] for c in range(3)]
        changes.append(
            (
                [o - f for o, f in zip(own, flux)],
                [roll(f, -1, axis) - o for o, f in zip(own, flux)],
            )
        )
    rows, cols = changes
    return [
        [
            [cells[c] - (0.5 * RATIO) * (rows[a][c] + cols[b][c]) for c in range(3)]
            for b in range(2)
        ]
        for a in range(2)
    ]


def patch_rows(cells, size):
    half = doubled_first_step(cells)
    by_row = [paired_change(half[0][b], half[1][b], 0) for b in range(2)]
    by_col = [paired_change(half[a][0], half[a][1], 1) for a in range(2)]
    lanes = lane_ids(size)
    result = []
    for a in range(2):
        fine = [
            [half[a][b][c] - (0.5 * RATIO) * (by_row[b][a][c] + by_col[a][b][c]) for c in range(3)]
            for b in range(2)
        ]
        parts = []
        for c in range(3):
            pick = lanes // 2 + 2
            even = jnp.take_along_axis(fine[0][c][0:size], pick, axis=1)
            odd = jnp.take_along_axis(fine[1][c][0:size], pick, axis=1)
            parts.append(jnp.where(lanes % 2 == 0, even, odd))
        result.append(parts)
    return result


def sliding(load, start, size):
    group, shift = start // 8, start % 8
    turn = (8 - shift) % 8
    parts = [pltpu.roll(load(group + k), turn, 0) for k in range(size // 8 + 1)]
    keep = row_ids(8, parts[0].shape[1]) < 8 - shift
    return [jnp.where(keep, parts[k], parts[k + 1]) for k in range(size // 8)]


def scalar(values, row, lane):
    return values[row, lane].astype(jnp.int32)


def slab_rows(ref, first, count, size):
    last = SLAB // 8 - 1
    load = lambda k: ref[pl.ds(pl.multiple_of(first + 8 * jnp.minimum(k, last), 8), 8), :]
    return sliding(load, SLAB - count, size)


def column_move(first_cols, last_cols, side, here, right_count):
    lanes = lane_ids(8)
    head = jnp.where(lanes < here, pltpu.roll(side, here, 1), first_cols)
    outer = jnp.where(lanes < right_count, pltpu.roll(last_cols, right_count, 1), side)
    return head, jnp.where(lanes >= LANES // 2, side, outer)


def move_rows(state_ref, rim_ref, slab_ref, wide_ref):
    rows, cols = state_ref.shape[1], state_ref.shape[2]
    counts = rim_ref[0, 0:8, :]
    rc, cc, cc_right = [scalar(counts, 0, k) for k in (OWN_ROWS, OWN_COLS, RIGHT_COLS)]
    for comp in range(3):
        bodies = slab_rows(slab_ref.at[comp], 0, rc, SLAB)
        for k in range(rows // 8):
            part, at = slice(8 * k, 8 * k + 8), slice(8 * k + 8, 8 * k + 16)
            body = state_ref[comp, part, :]
            if 8 * k < SLAB:
                body = jnp.where(row_ids(8, cols) + 8 * k < rc, bodies[k], body)
                wide_ref[comp, at, LANES : LANES + cols] = body
                continue
            head, outer = column_move(
                body[:, 0:LANES], body[:, cols - LANES : cols], rim_ref[comp, part, :], cc, cc_right
            )
            wide_ref[comp, at, 0:LANES] = outer
            wide_ref[comp, at, LANES : 2 * LANES] = head
            wide_ref[comp, at, 2 * LANES : LANES + cols] = body[:, LANES:cols]
            wide_ref[comp, at, LANES + cols : 2 * LANES + cols] = outer


def finish(
    state_ref, rim_ref, slab_ref, rows_ref, within_ref, across_ref, upper_ref, lower_ref, edge_ref, numbers_ref,
    error_out, moved_out, patch_out,
    wide, window, near_rows, columns, corners, above_rim, below, patch, error, aside, sems,
):
    rows, cols = state_ref.shape[1], state_ref.shape[2]
    right = slice(cols, cols + LANES)
    inside_wide = slice(LANES, LANES + cols)
    on_left = lane_ids(8) >= LANES // 2
    copies = [
        pltpu.make_async_copy(rows_ref.at[:, SLAB + 8 : rows + 8, inside_wide], moved_out.at[:, SLAB:rows, :], sems.at[0])
    ]
    copies[-1].start()

    odd = is_odd()
    packed_half = SLAB // 2
    last_rows = slice(DOWN_ROWS - 8, DOWN_ROWS - 1)
    aside[0:7, :] = jnp.where(odd, within_ref[last_rows, :], across_ref[last_rows, :])
    aside[7:8, :] = jnp.zeros((1, LANES), jnp.float32)
    beside = aside[...]
    turned = jnp.concatenate([beside, jnp.zeros((LANES - 8, LANES), jnp.float32)], axis=0).T[rows - SLAB : rows]
    lanes = lane_ids(packed_half)
    tiles = cols // LANES + 1
    for comp in range(3):
        at = slice(comp * packed_half, (comp + 1) * packed_half)
        packed = jnp.where(odd, within_ref[at, :], across_ref[at, :])
        inner = turned if comp == 0 else roll(turned, -2 * comp, 1)
        upper = jnp.where(lanes >= LANES // 2, roll(packed, LANES // 2, 1), inner[0:packed_half])
        lower = jnp.where(lanes >= LANES // 2, packed, inner[packed_half:SLAB])
        above_rim[comp][0:packed_half, :] = upper
        above_rim[comp][packed_half:SLAB, :] = lower
        for t in range(tiles):
            at = slice(8 * (comp * tiles + t), 8 * (comp * tiles + t) + 8)
            below[comp][:, LANES * t : LANES * (t + 1)] = jnp.where(odd, across_ref[at, :], within_ref[at, :])

    edges = coarse_error(
        edge_phases(state_ref, slab_ref, above_rim, below, edge_ref, near_rows, columns, corners)
    )
    error[...] = put_edges(jnp.concatenate([upper_ref[...], lower_ref[...]], axis=0), edges)

    own_counts, below_counts, numbers = rim_ref[0, 0:8, :], below[0][:, right], numbers_ref[...]
    cc, rc_left, rc_right, cc_right = [
        scalar(own_counts, 0, k) for k in (OWN_COLS, LEFT_ROWS, RIGHT_ROWS, RIGHT_COLS)
    ]
    cc_above, cc_above_right = [scalar(beside, 6, k) for k in (0, LANES - 1)]
    rc_below, cc_below, rc_below_left, rc_below_right, cc_below_right = [
        scalar(below_counts, 0, k) for k in (OWN_ROWS, OWN_COLS, LEFT_ROWS, RIGHT_ROWS, RIGHT_COLS)
    ]
    pos_row, pos_col, ext_row, ext_col = [scalar(numbers, k, 0) for k in range(4)]

    def put(comp, at, body, side, here, right_count):
        tail = body[:, LANES:cols]
        head, outer = column_move(body[:, 0:LANES], tail[:, cols - 2 * LANES :], side, here, right_count)
        wide[comp][at : at + 8, 0:LANES] = outer
        wide[comp][at : at + 8, LANES : 2 * LANES] = head
        wide[comp][at : at + 8, 2 * LANES : LANES + cols] = tail
        wide[comp][at : at + 8, LANES + cols : 2 * LANES + cols] = outer

    def moved_rim(ref, first, left, right_count, size):
        from_left = slab_rows(ref, first, left, size)
        from_right = slab_rows(ref, first, right_count, size)
        return [jnp.where(on_left, a, b) for a, b in zip(from_left, from_right)]

    for comp in range(3):
        sides = moved_rim(above_rim[comp], 0, rc_left, rc_right, SLAB)
        for k in range(SLAB // 8):
            side = rim_ref[comp, 8 * k : 8 * k + 8, :]
            side = jnp.where(row_ids(8) + 8 * k < jnp.where(on_left, rc_left, rc_right), sides[k], side)
            put(comp, 8 * k + 8, rows_ref[comp, 8 * k + 8 : 8 * k + 16, inside_wide], side, cc, cc_right)
        wide[comp][SLAB + 8 : rows + 8, :] = rows_ref[comp, SLAB + 8 : rows + 8, :]
        put(comp, 0, slab_ref[comp, SLAB - 8 : SLAB, :], above_rim[comp][SLAB - 8 : SLAB, :], cc_above, cc_above_right)
        (body,) = slab_rows(state_ref.at[comp], rows - SLAB, rc_below, 8)
        (side,) = moved_rim(rim_ref.at[comp], rows - SLAB, rc_below_left, rc_below_right, 8)
        body = jnp.where(row_ids(8, cols) < rc_below, body, below[comp][:, 0:cols])
        side = jnp.where(
            row_ids(8) < jnp.where(on_left, rc_below_left, rc_below_right), side, below[comp][:, right]
        )
        put(comp, rows + 8, body, side, cc_below, cc_below_right)
    copies.append(pltpu.make_async_copy(error, error_out, sems.at[1]))
    copies += [
        pltpu.make_async_copy(wide[c].at[8 : SLAB + 8, inside_wide], moved_out.at[c, 0:SLAB, :], sems.at[2 + c])
        for c in range(3)
    ]

    first_lane = pos_col + LANES - 2
    tile, shift = first_lane // LANES, first_lane % LANES
    turn = (LANES - shift) % LANES
    keep = lane_ids(8) < LANES - shift
    for comp in range(3):

        def load(k):
            group = pl.ds(pl.multiple_of(8 * jnp.minimum(k, rows // 8 + 1), 8), 8)
            near = wide[comp][group, pl.ds(pl.multiple_of(LANES * tile, LANES), LANES)]
            far = wide[comp][group, pl.ds(pl.multiple_of(LANES * tile + LANES, LANES), LANES)]
            return jnp.where(keep, pltpu.roll(near, turn, 1), pltpu.roll(far, turn, 1))

        parts = sliding(load, pos_row + 8, PATCH + 8)
        (above,) = sliding(load, pos_row, 8)
        parts[-1] = jnp.where(row_ids(8) < 4, parts[-1], above)
        for k, part in enumerate(parts):
            window[comp][8 * k : 8 * k + 8, :] = part

    fine_rows, fine_cols = 2 * ext_row, 2 * ext_col
    fine = patch_rows([window[c][...] for c in range(3)], PATCH)
    lanes, ids = lane_ids(PATCH), row_ids(PATCH)
    for a in range(2):
        inside = (2 * ids + a < fine_rows) & (lanes < fine_cols)
        for c in range(3):
            patch[c][pl.ds(a, PATCH, stride=2), :] = jnp.where(inside, fine[a][c], 0.0)
    for c in range(3):
        copies.append(pltpu.make_async_copy(patch[c], patch_out.at[c], sems.at[5 + c]))
        copies[-1].start()
    for copy in copies[1:5]:
        copy.start()
    for copy in copies:
        copy.wait()


def around(axis, by):
    devices = lax.axis_size(axis)
    return [(i, (i + by) % devices) for i in range(devices)]


def in_vmem(value):
    return pltpu.with_memory_space_constraint(value, pltpu.VMEM)


def in_hbm(value):
    return pltpu.with_memory_space_constraint(value, pltpu.HBM)


def vmem(*shape):
    return pltpu.VMEM(shape, jnp.float32)


def per_device(state, row_count, col_count, patch_pos, patch_ext):
    rows, cols = state.shape[1], state.shape[2]
    width = cols + LANES
    half = rows // 2
    here = in_vmem(state)
    ahead = pl.pallas_call(
        blank,
        out_shape=vmem(8, LANES),
        out_specs=VMEM,
        cost_estimate=pl.CostEstimate(flops=10_000_000_000, bytes_accessed=10_000_000, transcendentals=0),
        name="ahead",
    )()
    to_right, strip = pl.pallas_call(
        pack_cols,
        out_shape=(vmem(3 * half + 8, LANES), vmem(32, LANES)),
        in_specs=[SMEM, VMEM, VMEM],
        out_specs=(VMEM,) * 2,
        name="pack_cols",
    )(row_count, in_vmem(ahead), here)
    strip = in_vmem(strip)
    to_left, counts, slab = pl.pallas_call(
        pack_right,
        out_shape=(vmem(8, LANES), vmem(8, LANES), vmem(3, SLAB, cols)),
        in_specs=[SMEM, VMEM, VMEM],
        out_specs=(VMEM,) * 3,
        name="pack_right",
    )(col_count, strip, here)
    from_left = in_vmem(lax.ppermute(to_right, "col", around("col", 1)))
    from_right = in_vmem(lax.ppermute(to_left, "col", around("col", -1)))
    slab_above = in_vmem(lax.ppermute(slab, "row", around("row", 1)))
    upper = in_vmem(pl.pallas_call(
        upper_error,
        out_shape=vmem(UPPER, cols // 2),
        in_specs=[VMEM],
        out_specs=VMEM,
        scratch_shapes=[vmem(3, 2, 2 * UPPER + 16, LANES)],
        cost_estimate=pl.CostEstimate(flops=15_000_000, bytes_accessed=300_000, transcendentals=0),
        name="upper_error",
    )(here))
    rim, within, across, edge = pl.pallas_call(
        pack_rows,
        out_shape=(vmem(3, rows, LANES), vmem(DOWN_ROWS - 1, LANES), vmem(DOWN_ROWS, LANES), vmem(3, 16, LANES)),
        in_specs=[VMEM] * 6,
        out_specs=(VMEM,) * 4,
        cost_estimate=pl.CostEstimate(flops=3_000_000_000, bytes_accessed=600_000, transcendentals=0),
        name="pack_rows",
    )(in_vmem(counts), strip, from_left, from_right, here, upper)
    rim = in_vmem(rim)
    lower, numbers = pl.pallas_call(
        lower_error,
        out_shape=(vmem(half - UPPER, cols // 2), vmem(8, LANES)),
        in_specs=[ANY, ANY, VMEM, VMEM],
        out_specs=(VMEM,) * 2,
        scratch_shapes=[
            vmem(3, 2, 2 * (half - UPPER) + 16, LANES),
            pltpu.VMEM(patch_pos.shape, jnp.int32),
            pltpu.VMEM(patch_ext.shape, jnp.int32),
            pltpu.SemaphoreType.DMA((2,)),
        ],
        cost_estimate=pl.CostEstimate(flops=15_000_000, bytes_accessed=300_000, transcendentals=0),
        name="lower_error",
    )(in_hbm(patch_pos), in_hbm(patch_ext), here, rim)
    devices = lax.axis_size("row")
    from_within = in_vmem(lax.ppermute(within, "row", [(i, i ^ 1) for i in range(devices)]))
    from_across = in_vmem(
        lax.ppermute(across, "row", [(i, (i + (1 if i % 2 else -1)) % devices) for i in range(devices)])
    )
    moved_rows = in_vmem(pl.pallas_call(
        move_rows,
        out_shape=vmem(3, rows + 16, width + LANES),
        in_specs=[VMEM] * 3,
        out_specs=VMEM,
        cost_estimate=pl.CostEstimate(flops=3_000_000, bytes_accessed=1_000_000, transcendentals=0),
        name="move_rows",
    )(here, rim, slab_above))
    return pl.pallas_call(
        finish,
        out_shape=(f32(half, cols // 2), f32(3, rows, cols), f32(3, 2 * PATCH, 2 * PATCH)),
        in_specs=[VMEM] * 10,
        out_specs=(ANY,) * 3,
        scratch_shapes=[
            [vmem(rows + 16, width + LANES)] * 3,
            [vmem(PATCH + 8, LANES)] * 3,
            [vmem(16, cols)] * 3,
            [vmem(2, 16, LANES)] * 3,
            [vmem(16, LANES)] * 3,
            [vmem(SLAB, LANES)] * 3,
            [vmem(8, width)] * 3,
            [vmem(2 * PATCH, 2 * PATCH)] * 3,
            vmem(half, cols // 2),
            vmem(8, LANES),
            pltpu.SemaphoreType.DMA((8,)),
        ],
        compiler_params=PARAMS,
        name="finish",
    )(here, rim, slab_above, moved_rows, from_within, from_across, upper, lower, edge, numbers)


def solution(mesh):
    placed = (
        P(None, "row", "col"),
        P("row", "col"),
        P("row", "col"),
        P("row", "col", None),
        P("row", "col", None),
    )
    return jax.shard_map(
        per_device,
        mesh=mesh,
        in_specs=placed,
        out_specs=(P("row", "col"), P(None, "row", "col"), P(None, "row", "col")),
        check_vma=False,
    )
```
